32 devices in a mesh: heads: 4 (over z), blk: 8 (over y, x, core).
Axes of the slice: x: 2, y: 2, z: 4, core: 2. Of those that a mesh axis runs over, the one named last changes fastest.
Arguments:
- versions: bfloat16 [4, 4096, 2048], P(None, ('blk', 'heads')), may hold values from -6 to 6
- layer_input: bfloat16 [4096, 256], P(('blk', 'heads')), may hold values from -6 to 6
- positions: int32 [4096], P(('blk', 'heads')), may hold values from 0 to 8191, as said below
- documents: int32 [4096], replicated, may hold values from 0 to 2, as said below
- cotangent: bfloat16 [4, 4096, 2048], P(None, ('blk', 'heads')), may hold values from -6 to 6
- norm_gains: bfloat16 [8, 2048], replicated, may hold values from 0.5 to 1.5
- router_weight: bfloat16 [4, 2048], replicated, may hold values from -0.125 to 0.125
- coefficients: bfloat16 [4, 20], replicated, may hold values from -2.5 to 2.5
- query_key_gains: bfloat16 [2, 256], replicated, may hold values from 0.25 to 0.44921875
- query_weight: bfloat16 [2048, 2048], P('blk'), may hold values from -0.125 to 0.125
- key_matrix: bfloat16 [2048, 512], P('blk'), may hold values from -0.125 to 0.125
- value_matrix: bfloat16 [2048, 512], P('blk'), may hold values from -0.125 to 0.125
- out_weight: bfloat16 [2048, 2048], P('blk'), may hold values from -0.125 to 0.125
- laurel_weight: bfloat16 [2048, 128], P('blk'), may hold values from -0.125 to 0.125
- input_gate: bfloat16 [2048, 256], P('blk'), may hold values from -0.125 to 0.125
- input_projection: bfloat16 [2048, 256], P('blk'), may hold values from -0.375 to 0.375
- gate_weight: bfloat16 [2048, 8192], P('blk', 'heads'), may hold values from -0.125 to 0.125
- up_weight: bfloat16 [2048, 8192], P('blk', 'heads'), may hold values from -0.125 to 0.125
- down_weight: bfloat16 [2048, 8192], P('blk', 'heads'), may hold values from -0.0625 to 0.0625
Outputs:
- out_versions: bfloat16 [4, 4096, 2048], P(None, ('blk', 'heads'))
- versions_grad: bfloat16 [4, 4096, 2048], P(None, ('blk', 'heads'))
- layer_input_grad: bfloat16 [4096, 256], P(('blk', 'heads'))
- norm_gains_grad: float32 [8, 2048], replicated
- router_weight_grad: float32 [4, 2048], replicated
- coefficients_grad: float32 [4, 20], replicated
- head_gains_grad: float32 [2, 256], replicated
- query_weight_grad: float32 [2048, 2048], P('blk')
- key_weight_grad: float32 [2048, 512], P('blk')
- value_weight_grad: float32 [2048, 512], P('blk')
- out_weight_grad: float32 [2048, 2048], P('blk')
- laurel_weight_grad: float32 [2048, 128], P('blk')
- input_gate_grad: float32 [2048, 256], P('blk')
- input_projection_grad: float32 [2048, 256], P('blk')
- gate_weight_grad: float32 [2048, 8192], P('blk', 'heads')
- up_weight_grad: float32 [2048, 8192], P('blk', 'heads')
- down_weight_grad: float32 [2048, 8192], P('blk', 'heads')
The draws below stay inside these ranges and needn't reach their ends.
Inputs may be any that keep to these rules, and one draw needn't show every extreme that they name: Never falls along the row; documents 0 and 2 hold 1 to half of 512 tokens each, document 1 all others. `positions`: A token's position is its document's start position plus its place in the document; document 1 starts at 0, and the last token of the row is at position 4096 + 4095.
All inputs are finite; a program needn't handle non-finite values.
Results may differ from the reference program's by a relative error of at most 0.039.
Values may be sent and summed in bfloat16 or wider, within the bound.
No kernel may reach another device: no remote copies, remote signals or barrier semaphores. Data moves between devices by JAX's collectives and lax.ppermute only.
A program may use at most 320 MiB of HBM per device.

```python
import jax
import jax.numpy as jnp
from jax import lax

MODEL_WIDTH = 2048
QUERY_HEAD_COUNT = 8
KEY_VALUE_HEADS = 2
HEAD_WIDTH = 256
FF = 8192
LAUREL_RANK = 64
LAYER_INPUT_SIZE = 256
PIECE = 512
ROW = 4096


def layout(key):
    head_length = jax.random.randint(jax.random.fold_in(key, 11), (), 1, PIECE // 2 + 1).astype(jnp.int32)
    tail_length = jax.random.randint(jax.random.fold_in(key, 12), (), 1, PIECE // 2 + 1).astype(jnp.int32)
    head_start = jax.random.randint(jax.random.fold_in(key, 13), (), 0, 4096).astype(jnp.int32)
    tail_start = (ROW + 4096 - tail_length).astype(jnp.int32)
    starts = jnp.stack([head_start, jnp.zeros((), jnp.int32), tail_start])
    places = jnp.arange(ROW, dtype=jnp.int32)
    numbers = (places >= head_length).astype(jnp.int32) + (places >= ROW - tail_length).astype(jnp.int32)
    begins = jnp.stack([jnp.zeros((), jnp.int32), head_length, (ROW - tail_length).astype(jnp.int32)])
    return (numbers, places - begins[numbers] + starts[numbers])


def draw_documents(key, part):
    numbers, places = layout(key)
    return numbers


def draw_positions(key, part):
    numbers, places = layout(key)
    return places


def levels(key, extent, pieces, smallest, largest):
    loudness, own = 1.0, jax.random.fold_in(key, 6)
    for dim, blocks in pieces:
        heights = jnp.exp(jax.random.uniform(jax.random.fold_in(own, dim), (blocks,), jnp.float32, smallest / len(pieces), largest / len(pieces)))
        loudness = loudness * jnp.repeat(heights, extent[dim] // blocks).reshape([-1 if axis == dim else 1 for axis in range(len(extent))])
    return loudness


def noise(stream_key, dims, width, bound, pieces=(), kind=jnp.bfloat16):
    level = levels(stream_key, dims, pieces, -0.22, 0.18) if pieces else 1.0
    values = jax.random.normal(stream_key, dims, jnp.float32) * width * level
    return jnp.minimum(jnp.maximum(values, -bound), bound).astype(kind)


def setup_inputs(seed: int = 0) -> dict:
    streams_of = jax.random.split(jax.random.key(seed), 20)
    versions = noise(streams_of[0], (4, ROW, MODEL_WIDTH), 1.0, 6.0, ((1, 32),))
    layer_input = noise(streams_of[1], (ROW, LAYER_INPUT_SIZE), 1.0, 6.0, ((0, 32),))
    positions = draw_positions(jax.random.fold_in(streams_of[19], 71), 0)
    documents = draw_documents(jax.random.fold_in(streams_of[19], 71), 0)
    cotangent = noise(streams_of[4], (4, ROW, MODEL_WIDTH), 1.0, 6.0, ((1, 32),))
    norm_gains = jnp.clip(1.0 + 0.1 * jax.random.normal(streams_of[5], (8, MODEL_WIDTH), jnp.float32), 0.5, 1.5).astype(jnp.bfloat16)
    router_weight = noise(streams_of[6], (4, MODEL_WIDTH), MODEL_WIDTH ** -0.5, 0.125)
    coefficients = noise(streams_of[7], (4, 20), 0.3, 2.5)
    query_key_gains = jnp.clip(jax.random.uniform(streams_of[8], (2, HEAD_WIDTH), jnp.float32, 0.25, 0.44921875), 0.25, 0.44921875).astype(jnp.bfloat16)
    query_weight = noise(streams_of[9], (MODEL_WIDTH, QUERY_HEAD_COUNT * HEAD_WIDTH), MODEL_WIDTH ** -0.5, 0.125, ((0, 8),))
    key_matrix = noise(streams_of[10], (MODEL_WIDTH, KEY_VALUE_HEADS * HEAD_WIDTH), MODEL_WIDTH ** -0.5, 0.125, ((0, 8),))
    value_matrix = noise(streams_of[11], (MODEL_WIDTH, KEY_VALUE_HEADS * HEAD_WIDTH), MODEL_WIDTH ** -0.5, 0.125, ((0, 8),))
    out_weight = noise(streams_of[12], (MODEL_WIDTH, QUERY_HEAD_COUNT * HEAD_WIDTH), (QUERY_HEAD_COUNT * HEAD_WIDTH) ** -0.5, 0.125, ((0, 8),))
    laurel_weight = noise(streams_of[13], (MODEL_WIDTH, 2 * LAUREL_RANK), MODEL_WIDTH ** -0.5, 0.125, ((0, 8),))
    input_gate = noise(streams_of[14], (MODEL_WIDTH, LAYER_INPUT_SIZE), MODEL_WIDTH ** -0.5, 0.125, ((0, 8),))
    input_projection = noise(streams_of[15], (MODEL_WIDTH, LAYER_INPUT_SIZE), LAYER_INPUT_SIZE ** -0.5, 0.375, ((0, 8),))
    gate_weight = noise(streams_of[16], (MODEL_WIDTH, FF), MODEL_WIDTH ** -0.5, 0.125, ((0, 8), (1, 4)))
    up_weight = noise(streams_of[17], (MODEL_WIDTH, FF), MODEL_WIDTH ** -0.5, 0.125, ((0, 8), (1, 4)))
    down_weight = noise(streams_of[18], (MODEL_WIDTH, FF), FF ** -0.5, 0.0625, ((0, 8), (1, 4)))
    return {"versions": versions, "layer_input": layer_input, "positions": positions, "documents": documents, "cotangent": cotangent, "norm_gains": norm_gains, "router_weight": router_weight, "coefficients": coefficients, "query_key_gains": query_key_gains, "query_weight": query_weight, "key_matrix": key_matrix, "value_matrix": value_matrix, "out_weight": out_weight, "laurel_weight": laurel_weight, "input_gate": input_gate, "input_projection": input_projection, "gate_weight": gate_weight, "up_weight": up_weight, "down_weight": down_weight}


epsilon = 1e-06
rotary_base = 1000000.0
highest = lax.Precision.HIGHEST
root_half = 0.5 ** 0.5

@jax.custom_vjp
def low(v):
    return lax.optimization_barrier(v.astype(jnp.bfloat16)).astype(jnp.float32)

@jax.custom_vjp
def low_back(v):
    return v

def low_keep(v):
    return (low(v), None)

def low_pass(kept, grad):
    return (grad,)

def back_keep(v):
    return (v, None)

def back_low(kept, grad):
    return (low(grad),)
low.defvjp(low_keep, low_pass)
low_back.defvjp(back_keep, back_low)

def rms_norm_apply(value_states, gain):
    return value_states * lax.rsqrt(lax.optimization_barrier(jnp.mean(value_states * value_states, axis=-1, keepdims=True)) + epsilon) * gain

def rotary_apply(value_states, cosine_table, sine_table):
    half = value_states.shape[-1] // 2
    turned = jnp.concatenate([-value_states[..., half:], value_states[..., :half]], axis=-1)
    return value_states * cosine_table + turned * sine_table

def angles(positions):
    frequency = rotary_base ** (-2.0 * jnp.arange(HEAD_WIDTH // 2, dtype=jnp.float32) / HEAD_WIDTH)
    phase = positions.astype(jnp.float32)[:, None] * frequency[None, :]
    phase = jnp.concatenate([phase, phase], axis=-1)[:, None, :]
    return (jnp.cos(phase), jnp.sin(phase))

def modes(value_states, gain, router):
    return jnp.tanh(jnp.dot(rms_norm_apply(value_states, gain), router.T, precision=highest))

def predict(versions, gain_rows, router, coefficients):
    token_count = versions.shape[1]
    table = jnp.dot(modes(versions[0], gain_rows[0], router), coefficients[:, :16], precision=highest).reshape(token_count, 4, 4)
    predicted = versions + jnp.einsum('tij,jtd->itd', table, versions, precision=highest)
    return (predicted, rms_norm_apply(predicted[0], gain_rows[1]))

def prepare(query_states, key, value_states, query_key_gains, cosine_table, sine_table):
    token_count = query_states.shape[0]
    query_states = rotary_apply(rms_norm_apply(query_states.reshape(token_count, QUERY_HEAD_COUNT, HEAD_WIDTH), query_key_gains[0]), cosine_table, sine_table)
    key = rotary_apply(rms_norm_apply(key.reshape(token_count, KEY_VALUE_HEADS, HEAD_WIDTH), query_key_gains[1]), cosine_table, sine_table)
    value_states = value_states.reshape(token_count, KEY_VALUE_HEADS, HEAD_WIDTH)
    value_states = value_states * lax.rsqrt(lax.optimization_barrier(jnp.mean(value_states * value_states, axis=-1, keepdims=True)) + epsilon)
    return (query_states, jnp.repeat(key, QUERY_HEAD_COUNT // KEY_VALUE_HEADS, axis=1), jnp.repeat(value_states, QUERY_HEAD_COUNT // KEY_VALUE_HEADS, axis=1))

def combine(active, attention_out, normed, lifted, gain_rows):
    merged = (active + rms_norm_apply(attention_out, gain_rows[2]) + normed + rms_norm_apply(lifted, gain_rows[3])) * root_half
    return (merged, rms_norm_apply(merged, gain_rows[4]))

def activate(gate, up):
    return jax.nn.gelu(gate, approximate=True) * up

def correct(merged, fed, predicted, gain_rows, router, coefficients):
    activated = merged + rms_norm_apply(fed, gain_rows[5])
    scale = jnp.dot(modes(activated, gain_rows[0], router), coefficients[:, 16:], precision=highest) + 1.0
    corrected = predicted + scale.T[:, :, None] * (activated - predicted[0])[None]
    return (corrected, corrected[0] * gain_rows[6])

def finish(corrected, projected, gain_rows):
    extra = rms_norm_apply(projected, gain_rows[7])
    return corrected + jnp.stack([jnp.zeros_like(extra), extra, extra, extra])

def layer(versions, layer_input, norm_gains, router_weight, coefficients, query_key_gains, query_weight, key_matrix, value_matrix, out_weight, laurel_weight, input_gate, input_projection, gate_weight, up_weight, down_weight, documents, cosine_table, sine_table):
    predicted, normed = predict(versions, norm_gains, router_weight, coefficients)
    normed = low(normed)
    query_states = low_back(jnp.dot(normed, query_weight, precision=highest))
    key = low_back(jnp.dot(normed, key_matrix, precision=highest))
    value_states = low_back(jnp.dot(normed, value_matrix, precision=highest))
    rotated, keys_rep, values_rep = prepare(query_states, key, value_states, query_key_gains, cosine_table, sine_table)
    rotated = low_back(low(rotated))
    keys_rep = low_back(low(keys_rep))
    values_rep = low_back(low(values_rep))
    row_block = min(512, ROW)

    def attend_block(pair):
        block, offset = pair
        scores = low_back(jnp.einsum('qhd,khd->hqk', block, keys_rep, precision=highest))
        query_rows = offset + jnp.arange(row_block, dtype=jnp.int32)
        key_rows = jnp.arange(ROW, dtype=jnp.int32)
        query_docs = lax.dynamic_slice_in_dim(documents, offset, row_block)
        allowed = (key_rows[None, :] <= query_rows[:, None]) & (documents[None, :] == query_docs[:, None])
        scores = jnp.where(allowed[None], scores, -1e+30)
        top = lax.optimization_barrier(jnp.max(scores, axis=-1, keepdims=True))
        weights = jnp.exp(scores - top)
        shares = low(weights / lax.optimization_barrier(jnp.sum(weights, axis=-1, keepdims=True)))
        return jnp.einsum('hqk,khd->qhd', shares, values_rep, precision=highest)
    blocks = rotated.reshape(ROW // row_block, row_block, QUERY_HEAD_COUNT, HEAD_WIDTH)
    offsets = jnp.arange(ROW // row_block, dtype=jnp.int32) * row_block
    mixed = lax.map(jax.checkpoint(attend_block), (blocks, offsets)).reshape(ROW, QUERY_HEAD_COUNT * HEAD_WIDTH)
    mixed = low_back(low(mixed))
    attention_out = low_back(jnp.dot(mixed, out_weight.T, precision=highest))
    down = low(low_back(jnp.dot(normed, laurel_weight[:, :LAUREL_RANK], precision=highest)))
    lifted = low_back(jnp.dot(down, laurel_weight[:, LAUREL_RANK:].T, precision=highest))
    merged, feed_in = combine(predicted[0], attention_out, normed, lifted, norm_gains)
    feed_low = low(feed_in)
    feed_rows = min(2048, ROW)

    def feed_block(block):
        gate = low_back(jnp.dot(block, gate_weight, precision=highest))
        up = low_back(jnp.dot(block, up_weight, precision=highest))
        hidden = low(activate(gate, up))
        return low_back(jnp.dot(hidden, down_weight.T, precision=highest))
    fed = lax.map(jax.checkpoint(feed_block), feed_low.reshape(ROW // feed_rows, feed_rows, MODEL_WIDTH)).reshape(ROW, MODEL_WIDTH)
    corrected, first = correct(merged, fed, predicted, norm_gains, router_weight, coefficients)
    first = low(first)
    gate_pre = low_back(jnp.dot(first, input_gate, precision=highest))
    gated = low(activate(gate_pre, layer_input))
    projected = low_back(jnp.dot(gated, input_projection.T, precision=highest))
    return finish(corrected, projected, norm_gains)

def reference(versions, layer_input, positions, documents, cotangent, norm_gains, router_weight, coefficients, query_key_gains, query_weight, key_matrix, value_matrix, out_weight, laurel_weight, input_gate, input_projection, gate_weight, up_weight, down_weight):
    cosine_table, sine_table = angles(positions)
    floats = tuple((item.astype(jnp.float32) for item in (versions, layer_input, norm_gains, router_weight, coefficients, query_key_gains, query_weight, key_matrix, value_matrix, out_weight, laurel_weight, input_gate, input_projection, gate_weight, up_weight, down_weight)))

    def forward(*values):
        return layer(*values, documents, cosine_table, sine_table)
    result, pull = jax.vjp(forward, *floats)
    grads = pull(cotangent.astype(jnp.float32))
    return (result.astype(jnp.bfloat16), grads[0].astype(jnp.bfloat16), grads[1].astype(jnp.bfloat16), grads[2], grads[3], grads[4], grads[5], grads[6], grads[7], grads[8], grads[9], grads[10], grads[11], grads[12], grads[13], grads[14], grads[15])
```

```python
import jax
import jax.numpy as jnp
from jax import lax
from jax.experimental import pallas as pl
from jax.experimental.pallas import tpu as pltpu
from jax.sharding import PartitionSpec as P

QUERY_HEAD_COUNT = 8
KEY_VALUE_HEADS = 2
HEAD_WIDTH = 256
LAUREL_RANK = 64
LAYER_INPUT_SIZE = 256
KEYB = 2048


epsilon = 1e-06
rotary_base = 1000000.0
highest = lax.Precision.HIGHEST
root_half = 0.5**0.5


def rms_norm_apply(value_states, gain):
    return (
        value_states
        * lax.rsqrt(jnp.mean(value_states * value_states, axis=-1, keepdims=True) + epsilon)
        * gain
    )


def rotary_apply(value_states, cosine_table, sine_table):
    half = value_states.shape[-1] // 2
    turned = jnp.concatenate([-value_states[..., half:], value_states[..., :half]], axis=-1)
    return value_states * cosine_table + turned * sine_table


def angles(positions):
    frequency = rotary_base ** (-2.0 * jnp.arange(HEAD_WIDTH // 2, dtype=jnp.float32) / HEAD_WIDTH)
    phase = positions.astype(jnp.float32)[:, None] * frequency[None, :]
    phase = jnp.concatenate([phase, phase], axis=-1)[:, None, :]
    return (jnp.cos(phase), jnp.sin(phase))


def modes(value_states, gain, router):
    return jnp.tanh(jnp.dot(rms_norm_apply(value_states, gain), router.T, precision=highest))


def predict(versions, gain_rows, router, coefficients):
    token_count = versions.shape[1]
    table = jnp.dot(
        modes(versions[0], gain_rows[0], router), coefficients[:, :16], precision=highest
    ).reshape(token_count, 4, 4)
    predicted = versions + jnp.einsum("tij,jtd->itd", table, versions, precision=highest)
    return (predicted, rms_norm_apply(predicted[0], gain_rows[1]))


def prepare(query_states, key, value_states, query_key_gains, cosine_table, sine_table):
    token_count = query_states.shape[0]
    query_states = rotary_apply(
        rms_norm_apply(
            query_states.reshape(token_count, QUERY_HEAD_COUNT, HEAD_WIDTH), query_key_gains[0]
        ),
        cosine_table,
        sine_table,
    )
    key = rotary_apply(
        rms_norm_apply(key.reshape(token_count, KEY_VALUE_HEADS, HEAD_WIDTH), query_key_gains[1]),
        cosine_table,
        sine_table,
    )
    value_states = value_states.reshape(token_count, KEY_VALUE_HEADS, HEAD_WIDTH)
    value_states = value_states * lax.rsqrt(
        jnp.mean(value_states * value_states, axis=-1, keepdims=True) + epsilon
    )
    return (
        query_states,
        jnp.repeat(key, QUERY_HEAD_COUNT // KEY_VALUE_HEADS, axis=1),
        jnp.repeat(value_states, QUERY_HEAD_COUNT // KEY_VALUE_HEADS, axis=1),
    )


def combine(active, attention_out, normed, lifted, gain_rows):
    merged = (
        active
        + rms_norm_apply(attention_out, gain_rows[2])
        + normed
        + rms_norm_apply(lifted, gain_rows[3])
    ) * root_half
    return (merged, rms_norm_apply(merged, gain_rows[4]))


def activate(gate, up):
    return jax.nn.gelu(gate, approximate=True) * up


def correct(merged, fed, predicted, gain_rows, router, coefficients):
    activated = merged + rms_norm_apply(fed, gain_rows[5])
    scale = (
        jnp.dot(modes(activated, gain_rows[0], router), coefficients[:, 16:], precision=highest)
        + 1.0
    )
    corrected = predicted + scale.T[:, :, None] * (activated - predicted[0])[None]
    return (corrected, corrected[0] * gain_rows[6])


def finish(corrected, projected, gain_rows):
    extra = rms_norm_apply(projected, gain_rows[7])
    return corrected + jnp.stack([jnp.zeros_like(extra), extra, extra, extra])


def forward_product(left, right):
    return jnp.dot(left, right, preferred_element_type=jnp.float32)


def transposed_product(left, right):
    return lax.dot_general(
        left, right, (((1,), (1,)), ((), ())), preferred_element_type=jnp.float32
    )


def weight_product(left, right):
    return lax.dot_general(
        left, right, (((0,), (0,)), ((), ())), preferred_element_type=jnp.float32
    )


def general_device(
    versions,
    layer_input,
    positions,
    documents,
    cotangent,
    norm_gains,
    router_weight,
    coefficients,
    query_key_gains,
    query_weight,
    key_matrix,
    value_matrix,
    out_weight,
    laurel_weight,
    input_gate,
    input_projection,
    gate_weight,
    up_weight,
    down_weight,
):
    narrow = jnp.bfloat16
    wide = jnp.float32
    (
        query_full,
        key_full,
        value_full,
        out_full,
        laurel_full,
        gate_full,
        projection_full,
        unit_gate,
        unit_up,
        unit_down,
    ) = (
        lax.all_gather(query_weight, "blk", axis=0, tiled=True),
        lax.all_gather(key_matrix, "blk", axis=0, tiled=True),
        lax.all_gather(value_matrix, "blk", axis=0, tiled=True),
        lax.all_gather(out_weight, "blk", axis=0, tiled=True),
        lax.all_gather(laurel_weight, "blk", axis=0, tiled=True),
        lax.all_gather(input_gate, "blk", axis=0, tiled=True),
        lax.all_gather(input_projection, "blk", axis=0, tiled=True),
        lax.all_gather(gate_weight, "blk", axis=0, tiled=True),
        lax.all_gather(up_weight, "blk", axis=0, tiled=True),
        lax.all_gather(down_weight, "blk", axis=0, tiled=True),
    )
    gain_rows = norm_gains.astype(wide)
    router_wide = router_weight.astype(wide)
    coef_wide = coefficients.astype(wide)
    head_wide = query_key_gains.astype(wide)
    (predicted, normed), pull_predict = jax.vjp(
        predict, versions.astype(wide), gain_rows, router_wide, coef_wide
    )
    normed_low = normed.astype(narrow)
    cosine_table, sine_table = angles(positions)

    def prepare_here(query_states, key, value_states, gains_here):
        return prepare(query_states, key, value_states, gains_here, cosine_table, sine_table)

    (rotated, keys_rep, values_rep), pull_prepare = jax.vjp(
        prepare_here,
        forward_product(normed_low, query_full),
        forward_product(normed_low, key_full),
        forward_product(normed_low, value_full),
        head_wide,
    )
    query_heads, key_heads, value_heads = (
        lax.all_to_all(rotated.astype(narrow), "heads", split_axis=1, concat_axis=0, tiled=True),
        lax.all_to_all(keys_rep.astype(narrow), "heads", split_axis=1, concat_axis=0, tiled=True),
        lax.all_to_all(values_rep.astype(narrow), "heads", split_axis=1, concat_axis=0, tiled=True),
    )
    keys_all, values_all = (
        lax.all_gather(key_heads, "blk", axis=0, tiled=True),
        lax.all_gather(value_heads, "blk", axis=0, tiled=True),
    )
    piece, local_heads, head_size = query_heads.shape
    first_row = lax.axis_index("blk") * piece
    last_row = first_row + piece - 1
    query_rows = first_row + jnp.arange(piece, dtype=jnp.int32)
    query_docs = lax.dynamic_slice_in_dim(documents, first_row, piece)
    block_starts = jnp.arange(keys_all.shape[0] // KEYB, dtype=jnp.int32) * KEYB

    def block_scores(offset):
        key_block = lax.dynamic_slice_in_dim(keys_all, offset, KEYB)
        value_block = lax.dynamic_slice_in_dim(values_all, offset, KEYB)
        key_rows = offset + jnp.arange(KEYB, dtype=jnp.int32)
        key_docs = lax.dynamic_slice_in_dim(documents, offset, KEYB)
        allowed = (key_rows[None, :] <= query_rows[:, None]) & (
            key_docs[None, :] == query_docs[:, None]
        )
        scores = jnp.einsum("qhd,khd->hqk", query_heads, key_block, preferred_element_type=wide)
        return (key_block, value_block, allowed[None], jnp.where(allowed[None], scores, -1e30))

    def attend(state, offset):

        def visit(carry):
            top, total, summed = carry
            key_block, value_block, allowed, scores = block_scores(offset)
            new_top = jnp.maximum(top, jnp.max(scores, axis=-1))
            weights = jnp.where(allowed, jnp.exp(scores - new_top[:, :, None]), 0.0)
            decay = jnp.exp(top - new_top)
            summed = summed * decay.T[:, :, None] + jnp.einsum(
                "hqk,khd->qhd", weights.astype(narrow), value_block, preferred_element_type=wide
            )
            return (new_top, total * decay + jnp.sum(weights, axis=-1), summed)

        def keep(carry):
            return carry

        return (lax.cond(offset <= last_row, visit, keep, state), None)

    start_state = (
        jnp.full((local_heads, piece), -1e30, wide),
        jnp.zeros((local_heads, piece), wide),
        jnp.zeros((piece, local_heads, head_size), wide),
    )
    (top, total, summed), unused = lax.scan(attend, start_state, block_starts)
    log_total = top + jnp.log(total)
    attended = summed / total.T[:, :, None]
    mixed = lax.all_to_all(
        attended.astype(narrow), "heads", split_axis=0, concat_axis=1, tiled=True
    )
    mixed_low = mixed.reshape(mixed.shape[0], -1)
    attention_out = transposed_product(mixed_low, out_full)
    down_low = forward_product(normed_low, laurel_full[:, :LAUREL_RANK]).astype(narrow)
    lifted = transposed_product(down_low, laurel_full[:, LAUREL_RANK:])
    (merged, feed_in), pull_combine = jax.vjp(
        combine, predicted[0], attention_out, normed_low.astype(wide), lifted, gain_rows
    )
    feed_low = feed_in.astype(narrow)
    unit_rows = lax.all_gather(feed_low, "heads", axis=0, tiled=True)
    hidden, pull_activate = jax.vjp(
        activate, forward_product(unit_rows, unit_gate), forward_product(unit_rows, unit_up)
    )
    hidden_low = hidden.astype(narrow)
    fed = transposed_product(hidden_low, unit_down)
    fed = lax.psum_scatter(
        fed.astype(jnp.bfloat16), "heads", scatter_dimension=0, tiled=True
    ).astype(jnp.float32)
    (corrected, first), pull_correct = jax.vjp(
        correct, merged, fed, predicted, gain_rows, router_wide, coef_wide
    )
    first_low = first.astype(narrow)
    gated, pull_gate = jax.vjp(
        activate, forward_product(first_low, gate_full), layer_input.astype(wide)
    )
    gated_low = gated.astype(narrow)
    projected = transposed_product(gated_low, projection_full)
    result, pull_finish = jax.vjp(finish, corrected, projected, gain_rows)
    corrected_grad, projected_grad, gains_finish = pull_finish(cotangent.astype(wide))
    projected_low = projected_grad.astype(narrow)
    gate_pre_grad, layer_grad = pull_gate(forward_product(projected_low, projection_full))
    gate_pre_low = gate_pre_grad.astype(narrow)
    merged_grad, fed_grad, predicted_grad, gains_correct, router_correct, coef_correct = (
        pull_correct((corrected_grad, transposed_product(gate_pre_low, gate_full)))
    )
    fed_low = fed_grad.astype(narrow)
    fed_rows = lax.all_gather(fed_low, "heads", axis=0, tiled=True)
    gate_grad, up_grad = pull_activate(forward_product(fed_rows, unit_down))
    gate_low = gate_grad.astype(narrow)
    up_low = up_grad.astype(narrow)
    feed_grad = transposed_product(gate_low, unit_gate) + transposed_product(up_low, unit_up)
    feed_grad = lax.psum_scatter(
        feed_grad.astype(jnp.bfloat16), "heads", scatter_dimension=0, tiled=True
    ).astype(jnp.float32)
    active_grad, attention_grad, normed_combine, lifted_grad, gains_combine = pull_combine(
        (merged_grad, feed_grad)
    )
    lifted_low = lifted_grad.astype(narrow)
    down_grad_low = forward_product(lifted_low, laurel_full[:, LAUREL_RANK:]).astype(narrow)
    attention_low = attention_grad.astype(narrow)
    mixed_grad = forward_product(attention_low, out_full).astype(narrow).reshape(mixed.shape)
    attended_grad = lax.all_to_all(mixed_grad, "heads", split_axis=1, concat_axis=0, tiled=True)
    delta = jnp.sum(attended_grad.astype(wide) * attended, axis=-1).T

    def attend_back(query_grad, offset):

        def visit(query_grad):
            key_block, value_block, allowed, scores = block_scores(offset)
            shares = jnp.where(allowed, jnp.exp(scores - log_total[:, :, None]), 0.0)
            share_grad = jnp.einsum(
                "qhd,khd->hqk", attended_grad, value_block, preferred_element_type=wide
            )
            score_low = (shares * (share_grad - delta[:, :, None])).astype(narrow)
            query_grad = query_grad + jnp.einsum(
                "hqk,khd->qhd", score_low, key_block, preferred_element_type=wide
            )
            key_grad = jnp.einsum(
                "hqk,qhd->khd", score_low, query_heads, preferred_element_type=wide
            )
            value_grad = jnp.einsum(
                "hqk,qhd->khd", shares.astype(narrow), attended_grad, preferred_element_type=wide
            )
            return (query_grad, (key_grad, value_grad))

        def skip(query_grad):
            empty = jnp.zeros((KEYB, local_heads, head_size), wide)
            return (query_grad, (empty, empty))

        return lax.cond(offset <= last_row, visit, skip, query_grad)

    query_grad, (key_grads, value_grads) = lax.scan(
        attend_back, jnp.zeros((piece, local_heads, head_size), wide), block_starts
    )
    key_own, value_own = (
        lax.psum_scatter(
            key_grads.reshape(keys_all.shape).astype(jnp.bfloat16),
            "blk",
            scatter_dimension=0,
            tiled=True,
        ).astype(jnp.float32),
        lax.psum_scatter(
            value_grads.reshape(keys_all.shape).astype(jnp.bfloat16),
            "blk",
            scatter_dimension=0,
            tiled=True,
        ).astype(jnp.float32),
    )
    query_back, key_back, value_back = (
        lax.all_to_all(query_grad.astype(narrow), "heads", split_axis=0, concat_axis=1, tiled=True),
        lax.all_to_all(key_own.astype(narrow), "heads", split_axis=0, concat_axis=1, tiled=True),
        lax.all_to_all(value_own.astype(narrow), "heads", split_axis=0, concat_axis=1, tiled=True),
    )
    query_pre, key_pre, value_pre, head_grad = pull_prepare(
        (query_back.astype(wide), key_back.astype(wide), value_back.astype(wide))
    )
    query_low = query_pre.astype(narrow)
    key_low = key_pre.astype(narrow)
    value_low = value_pre.astype(narrow)
    normed_grad = (
        normed_combine
        + transposed_product(query_low, query_full)
        + transposed_product(key_low, key_full)
        + transposed_product(value_low, value_full)
        + transposed_product(down_grad_low, laurel_full[:, :LAUREL_RANK])
    )
    predicted_grad = predicted_grad.at[0].add(active_grad)
    version_grad, gains_predict, router_predict, coef_predict = pull_predict(
        (predicted_grad, normed_grad)
    )
    small = lax.psum(
        (
            gains_finish + gains_correct + gains_combine + gains_predict,
            router_correct + router_predict,
            coef_correct + coef_predict,
            head_grad,
        ),
        ("heads", "blk"),
    )
    normed_targets = jnp.concatenate([query_low, key_low, value_low, down_grad_low], axis=1)
    summed_grads = lax.psum_scatter(
        jnp.concatenate(
            [
                weight_product(normed_low, normed_targets),
                weight_product(attention_low, mixed_low),
                weight_product(lifted_low, down_low),
                weight_product(first_low, gate_pre_low),
                weight_product(projected_low, gated_low),
                weight_product(unit_rows, gate_low),
                weight_product(unit_rows, up_low),
                weight_product(fed_rows, hidden_low),
            ],
            axis=1,
        ).astype(jnp.bfloat16),
        "blk",
        scatter_dimension=0,
        tiled=True,
    ).astype(jnp.float32)
    bounds = [0]
    for feature_width in (
        QUERY_HEAD_COUNT * HEAD_WIDTH,
        KEY_VALUE_HEADS * HEAD_WIDTH,
        KEY_VALUE_HEADS * HEAD_WIDTH,
        LAUREL_RANK,
        QUERY_HEAD_COUNT * HEAD_WIDTH,
        LAUREL_RANK,
        LAYER_INPUT_SIZE,
        LAYER_INPUT_SIZE,
    ):
        bounds.append(bounds[-1] + feature_width)
    attention_sum = lax.psum(summed_grads[:, : bounds[8]].astype(jnp.bfloat16), "heads").astype(
        jnp.float32
    )
    parts = [attention_sum[:, bounds[place] : bounds[place + 1]] for place in range(8)]
    unit_width = (summed_grads.shape[1] - bounds[8]) // 3
    gate_part = summed_grads[:, bounds[8] : bounds[8] + unit_width]
    up_part = summed_grads[:, bounds[8] + unit_width : bounds[8] + 2 * unit_width]
    down_part = summed_grads[:, bounds[8] + 2 * unit_width :]
    return (
        result.astype(narrow),
        version_grad.astype(narrow),
        layer_grad.astype(narrow),
        small[0],
        small[1],
        small[2],
        small[3],
        parts[0],
        parts[1],
        parts[2],
        parts[4],
        jnp.concatenate([parts[3], parts[5]], axis=1),
        parts[6],
        parts[7],
        gate_part,
        up_part,
        down_part,
    )


CORES = 2
LINE = 4
CHIPS = 4


def along_heads(x, step):
    return lax.ppermute(x, "heads", [(i, (i + step) % LINE) for i in range(LINE)])


def across_blk(x, mask):
    return lax.ppermute(x, "blk", [(i, i ^ mask) for i in range(CORES * CHIPS)])


def other_core(x):
    return across_blk(x, 1)


def gather_chip(x):
    half = x.shape[0] // 2
    before = along_heads(x, 1)
    after = along_heads(x, -1)
    far = jnp.concatenate([along_heads(before[:half], 1), along_heads(after[half:], -1)], axis=0)
    own = [before, x, after, far]
    return jnp.concatenate(own + [other_core(part) for part in own], axis=0)


def scatter_chip(y):
    wide = jnp.float32
    n = y.shape[0] // 8
    half = n // 2
    before, own, after, far = (
        y[k * n : (k + 1) * n].astype(wide) + other_core(y[(k + 4) * n : (k + 5) * n]).astype(wide)
        for k in range(4)
    )
    far = far.astype(jnp.bfloat16)
    first = along_heads(far[:half], 1).astype(wide)
    second = along_heads(far[half:], -1).astype(wide)
    after = jnp.concatenate([after[:half] + first, after[half:]], axis=0).astype(jnp.bfloat16)
    before = jnp.concatenate([before[:half], before[half:] + second], axis=0).astype(jnp.bfloat16)
    return own + along_heads(after, 1).astype(wide) + along_heads(before, -1).astype(wide)


def turn(x, blocks):
    rows = x.shape[0] // LINE
    twice = jnp.concatenate([x, x], axis=0)
    return lax.dynamic_slice_in_dim(twice, blocks * rows, x.shape[0])


def natural(x, core, line):
    half = x.shape[0] // 2
    own, other = (turn(part, (1 - line) % LINE) for part in (x[:half], x[half:]))
    first = core == 0
    return jnp.concatenate([jnp.where(first, own, other), jnp.where(first, other, own)], axis=0)


def arrival(x, core, line):
    half = x.shape[0] // 2
    first = core == 0
    own, other = jnp.where(first, x[:half], x[half:]), jnp.where(first, x[half:], x[:half])
    return jnp.concatenate([turn(part, (line - 1) % LINE) for part in (own, other)], axis=0)


def gather_chips(x):
    half = x.shape[0] // 2
    side = across_blk(x, 2)
    front = across_blk(x, 4)
    return side, front, across_blk(side[:half], 4), across_blk(front[half:], 2)


def scatter_chips(parts):
    wide = jnp.float32
    half = parts[0].shape[0] // 2
    own, side, front, far = parts
    low = across_blk(jnp.concatenate([side[:half], far[:half]], axis=0), 2)
    high = across_blk(jnp.concatenate([front[half:], far[half:]], axis=0), 4)
    front_sum = (front[:half].astype(wide) + low[half:].astype(wide)).astype(jnp.bfloat16)
    side_sum = (side[half:].astype(wide) + high[half:].astype(wide)).astype(jnp.bfloat16)
    upper = own[:half].astype(wide) + low[:half].astype(wide) + across_blk(front_sum, 4).astype(wide)
    lower = own[half:].astype(wide) + high[:half].astype(wide) + across_blk(side_sum, 2).astype(wide)
    return jnp.concatenate([upper, lower], axis=0)


def butterfly(x):
    for mask in (1, 2, 4):
        x = x + across_blk(x, mask)
    for mask in (1, 2):
        x = x + lax.ppermute(x, "heads", [(i, i ^ mask) for i in range(LINE)])
    return x


def chip_groups():
    return [[core + CORES * chip for chip in range(CHIPS)] for core in range(CORES)]


def weight_rows(keep, send, core):
    got = other_core(send)
    first = core == 0
    return jnp.concatenate([jnp.where(first, keep, got), jnp.where(first, got, keep)], axis=0)


def all_rows(x):
    return lax.all_gather(x, "blk", axis=0, tiled=True, axis_index_groups=chip_groups())


def own_rows(x):
    return lax.psum_scatter(
        x, "blk", scatter_dimension=0, tiled=True, axis_index_groups=chip_groups()
    )


def pick(x, start, size):
    return lax.dynamic_slice_in_dim(x, start, size, axis=1)


QUERY_ROWS = 512
KEY_ROWS = 512


def place_rows(target, parts, chip):
    own, side, front, near, far = parts
    size = own.shape[0]
    half = size // 2
    target[pl.ds(pl.multiple_of(chip * size, size), size), :] = own[...]
    target[pl.ds(pl.multiple_of((chip ^ 1) * size, size), size), :] = side[...]
    target[pl.ds(pl.multiple_of((chip ^ 2) * size, size), size), :] = front[...]
    base = (chip ^ 3) * size
    target[pl.ds(pl.multiple_of(base, size), half), :] = near[...]
    target[pl.ds(pl.multiple_of(base + half, half), half), :] = far[...]


def place_both(meta, mine, theirs, k_all, v_all):
    chip = meta[0]

    @pl.when(meta[1] == 0)
    def _():
        place_rows(k_all, mine, chip)
        place_rows(v_all, theirs, chip)

    @pl.when(meta[1] != 0)
    def _():
        place_rows(v_all, mine, chip)
        place_rows(k_all, theirs, chip)


def rows_times_rows(left, right):
    return lax.dot_general(
        left, right, (((1,), (1,)), ((), ())), preferred_element_type=jnp.float32
    )


def columns_times_columns(left, right):
    return lax.dot_general(
        left, right, (((0,), (0,)), ((), ())), preferred_element_type=jnp.float32
    )


def attend_kernel(meta, q_ref, lo_ref, *refs):
    mine, theirs = refs[:5], refs[5:10]
    out_ref, lse_ref, k_all, v_all, total, summed = refs[10:]
    place_both(meta, mine, theirs, k_all, v_all)
    own = q_ref.shape[0]
    for part in range(own // QUERY_ROWS):
        rows = pl.ds(part * QUERY_ROWS, QUERY_ROWS)
        first = meta[0] * own + part * QUERY_ROWS
        total[...] = jnp.zeros_like(total)
        summed[...] = jnp.zeros_like(summed)

        def visit(block, masked, rows=rows, first=first):
            at = pl.multiple_of(block * KEY_ROWS, KEY_ROWS)
            scores = rows_times_rows(q_ref[rows, :], k_all[pl.ds(at, KEY_ROWS), :])
            weights = jnp.exp(scores)
            if masked:
                key = at + lax.broadcasted_iota(jnp.int32, weights.shape, 1)
                query = first + lax.broadcasted_iota(jnp.int32, weights.shape, 0)
                weights = jnp.where((key >= lo_ref[rows, :]) & (key <= query), weights, 0.0)
            for lane in range(0, KEY_ROWS, 128):
                total[...] += weights[:, lane : lane + 128]
            summed[...] += jnp.dot(
                weights.astype(jnp.bfloat16),
                v_all[pl.ds(at, KEY_ROWS), :],
                preferred_element_type=jnp.float32,
            )

        start, full_from = meta[2 + 2 * part], meta[3 + 2 * part]
        end = (first + QUERY_ROWS - 1) // KEY_ROWS + 1
        full_from = jnp.minimum(full_from, end)
        full_to = jnp.maximum(jnp.minimum((first + 1) // KEY_ROWS, end), full_from)

        @pl.loop(start, full_from)
        def _(block, visit=visit):
            visit(block, True)

        @pl.loop(full_from, full_to)
        def _(block, visit=visit):
            visit(block, False)

        @pl.loop(full_to, end)
        def _(block, visit=visit):
            visit(block, True)

        denominator = jnp.sum(total[...], axis=1, keepdims=True)
        out_ref[rows, :] = summed[...] / denominator
        lse_ref[rows, :] = jnp.log(denominator)


def attend_back_kernel(meta, q_ref, grad_ref, lse_ref, delta_ref, lo_ref, *refs):
    mine, theirs = refs[:5], refs[5:10]
    dq_ref, keep_ref, send_ref, k_all, v_all, dk_sum, dv_sum = refs[10:]
    place_both(meta, mine, theirs, k_all, v_all)
    chip = meta[0]
    own = q_ref.shape[0]
    parts = own // QUERY_ROWS
    keep_ref[...] = jnp.zeros_like(keep_ref)
    send_ref[...] = jnp.zeros_like(send_ref)
    dq_ref[...] = jnp.zeros_like(dq_ref)
    per_chip = own // KEY_ROWS

    @pl.loop(meta[2], (chip + 1) * per_chip)
    def _(block):
        at = pl.multiple_of(block * KEY_ROWS, KEY_ROWS)
        dk_sum[...] = jnp.zeros_like(dk_sum)
        dv_sum[...] = jnp.zeros_like(dv_sum)
        for part in range(parts):
            rows = pl.ds(part * QUERY_ROWS, QUERY_ROWS)
            first = chip * own + part * QUERY_ROWS

            def visit(masked, rows=rows, first=first):
                keys = k_all[pl.ds(at, KEY_ROWS), :]
                queries = q_ref[rows, :]
                grads = grad_ref[rows, :]
                shares = jnp.exp(rows_times_rows(keys, queries) - lse_ref[:, rows])
                if masked:
                    key = at + lax.broadcasted_iota(jnp.int32, shares.shape, 0)
                    query = first + lax.broadcasted_iota(jnp.int32, shares.shape, 1)
                    shares = jnp.where((key >= lo_ref[:, rows]) & (key <= query), shares, 0.0)
                share_grad = rows_times_rows(v_all[pl.ds(at, KEY_ROWS), :], grads)
                score_grad = (shares * (share_grad - delta_ref[:, rows])).astype(jnp.bfloat16)
                dv_sum[...] += jnp.dot(
                    shares.astype(jnp.bfloat16), grads, preferred_element_type=jnp.float32
                )
                dk_sum[...] += jnp.dot(score_grad, queries, preferred_element_type=jnp.float32)
                dq_ref[rows, :] += columns_times_columns(score_grad, keys)

            start, full_from = meta[2 + 2 * part], meta[3 + 2 * part]
            full = (block >= full_from) & ((block + 1) * KEY_ROWS <= first + 1)
            needed = (block >= start) & (block * KEY_ROWS < first + QUERY_ROWS)

            @pl.when(full)
            def _(visit=visit):
                visit(False)

            @pl.when(needed & jnp.logical_not(full))
            def _(visit=visit):
                visit(True)

        place = (block // per_chip) ^ chip
        inner = pl.multiple_of((block % per_chip) * KEY_ROWS, KEY_ROWS)
        dk_low = dk_sum[...].astype(jnp.bfloat16)
        dv_low = dv_sum[...].astype(jnp.bfloat16)

        @pl.when(meta[1] == 0)
        def _():
            keep_ref[place, pl.ds(inner, KEY_ROWS), :] = dk_low
            send_ref[place, pl.ds(inner, KEY_ROWS), :] = dv_low

        @pl.when(meta[1] != 0)
        def _():
            keep_ref[place, pl.ds(inner, KEY_ROWS), :] = dv_low
            send_ref[place, pl.ds(inner, KEY_ROWS), :] = dk_low


def in_vmem(count):
    return [pl.BlockSpec(memory_space=pltpu.VMEM)] * count


def attend_here(meta, q, lo, mine, theirs):
    own, width = q.shape
    row = own * CHIPS
    return pl.pallas_call(
        attend_kernel,
        out_shape=(
            jax.ShapeDtypeStruct((own, width), jnp.float32),
            jax.ShapeDtypeStruct((own, 1), jnp.float32),
        ),
        in_specs=[pl.BlockSpec(memory_space=pltpu.SMEM)] + in_vmem(12),
        out_specs=tuple(in_vmem(2)),
        scratch_shapes=[
            pltpu.VMEM((row, width), jnp.bfloat16),
            pltpu.VMEM((row, width), jnp.bfloat16),
            pltpu.VMEM((QUERY_ROWS, 128), jnp.float32),
            pltpu.VMEM((QUERY_ROWS, width), jnp.float32),
        ],
        compiler_params=pltpu.CompilerParams(vmem_limit_bytes=40 << 20),
        cost_estimate=pl.CostEstimate(
            flops=2 * own * row * width, bytes_accessed=6 * row * width, transcendentals=own * row // 2
        ),
    )(meta, q, lo.reshape(own, 1), *mine, *theirs)


def attend_back_here(meta, q, grad, lse, delta, lo, mine, theirs):
    own, width = q.shape
    row = own * CHIPS
    return pl.pallas_call(
        attend_back_kernel,
        out_shape=(
            jax.ShapeDtypeStruct((own, width), jnp.float32),
            jax.ShapeDtypeStruct((CHIPS, own, width), jnp.bfloat16),
            jax.ShapeDtypeStruct((CHIPS, own, width), jnp.bfloat16),
        ),
        in_specs=[pl.BlockSpec(memory_space=pltpu.SMEM)] + in_vmem(15),
        out_specs=tuple(in_vmem(3)),
        scratch_shapes=[
            pltpu.VMEM((row, width), jnp.bfloat16),
            pltpu.VMEM((row, width), jnp.bfloat16),
            pltpu.VMEM((KEY_ROWS, width), jnp.float32),
            pltpu.VMEM((KEY_ROWS, width), jnp.float32),
        ],
        compiler_params=pltpu.CompilerParams(vmem_limit_bytes=48 << 20),
        cost_estimate=pl.CostEstimate(
            flops=5 * own * row * width, bytes_accessed=12 * row * width, transcendentals=own * row // 2
        ),
    )(
        meta, q, grad, lse.reshape(1, own), delta.reshape(1, own), lo.reshape(1, own), *mine, *theirs
    )


def predict_list(versions, gain_rows, router, coefficients):
    table = jnp.dot(
        modes(versions[0], gain_rows[0], router), coefficients[:, :16], precision=highest
    )
    predicted = []
    for i in range(4):
        value = versions[i]
        for j in range(4):
            value = value + table[:, 4 * i + j : 4 * i + j + 1] * versions[j]
        predicted.append(value)
    return (tuple(predicted), rms_norm_apply(predicted[0], gain_rows[1]))


def correct_list(merged, fed, predicted, gain_rows, router, coefficients):
    activated = merged + rms_norm_apply(fed, gain_rows[5])
    scale = (
        jnp.dot(modes(activated, gain_rows[0], router), coefficients[:, 16:], precision=highest)
        + 1.0
    )
    change = activated - predicted[0]
    corrected = tuple(predicted[i] + scale[:, i : i + 1] * change for i in range(4))
    return (corrected, corrected[0] * gain_rows[6])


def head_apply(x, gain, cosine, sine):
    normed = x * lax.rsqrt(jnp.mean(x * x, axis=-1, keepdims=True) + epsilon) * gain
    half = x.shape[-1] // 2
    turned = jnp.concatenate([-normed[:, half:], normed[:, :half]], axis=-1)
    return normed * cosine + turned * sine


def chip_device(
    versions,
    layer_input,
    positions,
    documents,
    cotangent,
    norm_gains,
    router_weight,
    coefficients,
    query_key_gains,
    query_weight,
    key_matrix,
    value_matrix,
    out_weight,
    laurel_weight,
    input_gate,
    input_projection,
    gate_weight,
    up_weight,
    down_weight,
):
    narrow = jnp.bfloat16
    wide = jnp.float32
    line = lax.axis_index("heads")
    piece = lax.axis_index("blk")
    core = piece % CORES
    chip = piece // CORES
    first_core = core == 0
    tokens = versions.shape[1]
    own = 8 * tokens
    width = versions.shape[2]
    rows_here = query_weight.shape[0]
    hidden = gate_weight.shape[1] // CORES
    head = CORES * line + core
    group = head // (QUERY_HEAD_COUNT // KEY_VALUE_HEADS)

    def head_columns(index, kv):
        return jnp.concatenate(
            [
                pick(query_weight, index * HEAD_WIDTH, HEAD_WIDTH),
                pick(kv, group * HEAD_WIDTH, HEAD_WIDTH),
                pick(out_weight, index * HEAD_WIDTH, HEAD_WIDTH),
            ],
            axis=1,
        )

    kv_mine = jnp.where(first_core, key_matrix, value_matrix)
    kv_theirs = jnp.where(first_core, value_matrix, key_matrix)
    head_full = all_rows(
        weight_rows(head_columns(head, kv_mine), head_columns(head ^ 1, kv_theirs), core)
    )
    small_full = lax.all_gather(
        jnp.concatenate([laurel_weight, input_gate, input_projection], axis=1),
        "blk",
        axis=0,
        tiled=True,
    )

    def hidden_columns(index):
        return jnp.concatenate(
            [pick(w, index * hidden, hidden) for w in (gate_weight, up_weight, down_weight)], axis=1
        )

    unit_full = all_rows(weight_rows(hidden_columns(core), hidden_columns(1 - core), core))
    query_kv_full = head_full[:, : 2 * HEAD_WIDTH]
    out_full = head_full[:, 2 * HEAD_WIDTH :]
    laurel_full = small_full[:, : 2 * LAUREL_RANK]
    gate_full = small_full[:, 2 * LAUREL_RANK : 2 * LAUREL_RANK + LAYER_INPUT_SIZE]
    projection_full = small_full[:, 2 * LAUREL_RANK + LAYER_INPUT_SIZE :]
    unit_gate = unit_full[:, :hidden]
    unit_up = unit_full[:, hidden : 2 * hidden]
    unit_down = unit_full[:, 2 * hidden :]

    gain_rows = norm_gains.astype(wide)
    router_wide = router_weight.astype(wide)
    coef_wide = coefficients.astype(wide)
    head_wide = query_key_gains.astype(wide)
    (predicted, normed), pull_predict = jax.vjp(
        predict_list,
        tuple(versions[i].astype(wide) for i in range(4)),
        gain_rows,
        router_wide,
        coef_wide,
    )
    normed_low = normed.astype(narrow)

    digits = jnp.stack([positions // 128, positions % 128], axis=1).astype(narrow)
    sent = jnp.concatenate([normed_low, jnp.pad(digits, ((0, 0), (0, 126)))], axis=1)
    gathered = gather_chip(sent)
    normed_rows = gathered[:, :width]
    digits_all = natural(gathered[:, width : width + 2].astype(wide), core, line)
    phase_position = digits_all[:, :1] * 128.0 + digits_all[:, 1:2]
    frequency = rotary_base ** (-2.0 * jnp.arange(HEAD_WIDTH // 2, dtype=wide) / HEAD_WIDTH)
    phase = phase_position * frequency[None, :]
    phase = jnp.concatenate([phase, phase], axis=-1)
    cosine, sine = jnp.cos(phase), jnp.sin(phase)
    cosine_kv = jnp.where(first_core, cosine, 1.0)
    sine_kv = jnp.where(first_core, sine, 0.0)

    def kv_gain(gains):
        return jnp.where(first_core, gains[1], 1.0)

    query_kv = natural(forward_product(normed_rows, query_kv_full), core, line)
    query_pre = query_kv[:, :HEAD_WIDTH]
    kv_pre = query_kv[:, HEAD_WIDTH:]
    rotated = head_apply(query_pre, head_wide[0], cosine, sine).astype(narrow)
    kv_own = head_apply(kv_pre, kv_gain(head_wide), cosine_kv, sine_kv).astype(narrow)
    mine = (kv_own, *gather_chips(kv_own))
    theirs = tuple(other_core(part) for part in mine)

    first_row = chip * own
    row_docs = lax.dynamic_slice_in_dim(documents, first_row, own)
    begin_one = jnp.sum(documents < 1)
    begin_two = jnp.sum(documents < 2)
    lo = jnp.where(row_docs == 0, 0, jnp.where(row_docs == 1, begin_one, begin_two)).astype(jnp.int32)
    bounds = []
    for part in range(own // QUERY_ROWS):
        bounds.append(lo[part * QUERY_ROWS] // KEY_ROWS)
        bounds.append((lo[(part + 1) * QUERY_ROWS - 1] + KEY_ROWS - 1) // KEY_ROWS)
    meta = jnp.stack([chip, core, *bounds]).astype(jnp.int32)
    attended, lse = attend_here(meta, rotated, lo, mine, theirs)
    mixed_rows = arrival(attended.astype(narrow), core, line)
    attention_out = scatter_chip(transposed_product(mixed_rows, out_full).astype(narrow))

    down_low = forward_product(normed_low, laurel_full[:, :LAUREL_RANK]).astype(narrow)
    lifted = transposed_product(down_low, laurel_full[:, LAUREL_RANK:])
    (merged, feed_in), pull_combine = jax.vjp(
        combine, predicted[0], attention_out, normed_low.astype(wide), lifted, gain_rows
    )
    unit_rows = gather_chip(feed_in.astype(narrow))
    hidden_units, pull_activate = jax.vjp(
        activate, forward_product(unit_rows, unit_gate), forward_product(unit_rows, unit_up)
    )
    hidden_low = hidden_units.astype(narrow)
    fed = scatter_chip(transposed_product(hidden_low, unit_down).astype(narrow))
    (corrected, first), pull_correct = jax.vjp(
        correct_list, merged, fed, predicted, gain_rows, router_wide, coef_wide
    )
    first_low = first.astype(narrow)
    gated, pull_gate = jax.vjp(
        activate, forward_product(first_low, gate_full), layer_input.astype(wide)
    )
    gated_low = gated.astype(narrow)
    projected = transposed_product(gated_low, projection_full)
    extra, pull_extra = jax.vjp(rms_norm_apply, projected, gain_rows[7])
    result = jnp.stack(
        [corrected[0].astype(narrow)] + [(corrected[i] + extra).astype(narrow) for i in (1, 2, 3)]
    )

    corrected_grad = tuple(cotangent[i].astype(wide) for i in range(4))
    projected_grad, gain_seven = pull_extra(
        corrected_grad[1] + corrected_grad[2] + corrected_grad[3]
    )
    projected_low = projected_grad.astype(narrow)
    gate_pre_grad, layer_grad = pull_gate(forward_product(projected_low, projection_full))
    gate_pre_low = gate_pre_grad.astype(narrow)
    merged_grad, fed_grad, predicted_grad, gains_correct, router_correct, coef_correct = (
        pull_correct((corrected_grad, transposed_product(gate_pre_low, gate_full)))
    )
    fed_rows = gather_chip(fed_grad.astype(narrow))
    gate_grad, up_grad = pull_activate(forward_product(fed_rows, unit_down))
    gate_low = gate_grad.astype(narrow)
    up_low = up_grad.astype(narrow)
    feed_grad = scatter_chip(
        (transposed_product(gate_low, unit_gate) + transposed_product(up_low, unit_up)).astype(narrow)
    )
    unit_sum = own_rows(
        jnp.concatenate(
            [
                weight_product(unit_rows, gate_low).astype(narrow),
                weight_product(unit_rows, up_low).astype(narrow),
                weight_product(fed_rows, hidden_low).astype(narrow),
            ],
            axis=1,
        )
    )
    active_grad, attention_grad, normed_combine, lifted_grad, gains_combine = pull_combine(
        (merged_grad, feed_grad)
    )
    lifted_low = lifted_grad.astype(narrow)
    down_grad_low = forward_product(lifted_low, laurel_full[:, LAUREL_RANK:]).astype(narrow)
    attention_rows = gather_chip(attention_grad.astype(narrow))
    mixed_grad_rows = forward_product(attention_rows, out_full).astype(narrow)
    mixed_grad = natural(mixed_grad_rows, core, line)
    delta = jnp.sum(mixed_grad.astype(wide) * attended, axis=-1)
    query_grad, kv_keep, kv_send = attend_back_here(
        meta, rotated, mixed_grad, lse, delta, lo, mine, theirs
    )
    kv_got = other_core(kv_send)
    kv_sum = scatter_chips(
        [(kv_keep[m].astype(wide) + kv_got[m].astype(wide)).astype(narrow) for m in range(CHIPS)]
    )
    half = own // 2
    mine_first = line % 2 == 0
    kv_sum_low = kv_sum.astype(narrow)
    kv_away = jnp.where(mine_first, kv_sum_low[half:], kv_sum_low[:half])
    kv_back = jnp.where(mine_first, kv_sum[:half], kv_sum[half:]) + lax.ppermute(
        kv_away, "heads", [(i, i ^ 1) for i in range(LINE)]
    ).astype(wide)

    def own_half(x):
        return jnp.where(mine_first, x[:half], x[half:])

    _, pull_query = jax.vjp(
        lambda x, g: head_apply(x, g, cosine, sine), query_pre, head_wide[0]
    )
    query_pre_grad, query_gain_grad = pull_query(query_grad.astype(narrow).astype(wide))
    _, pull_kv = jax.vjp(
        lambda x, g: head_apply(x, kv_gain(g), own_half(cosine_kv), own_half(sine_kv)),
        own_half(kv_pre),
        head_wide,
    )
    kv_pre_grad, kv_gain_grad = pull_kv(kv_back)
    kv_low = kv_pre_grad.astype(narrow)
    nothing = jnp.zeros_like(kv_low)
    kv_both = jnp.concatenate(
        [jnp.where(mine_first, kv_low, nothing), jnp.where(mine_first, nothing, kv_low)], axis=0
    )
    head_grads = arrival(
        jnp.concatenate([query_pre_grad.astype(narrow), kv_both], axis=1), core, line
    )
    normed_sum = scatter_chip(transposed_product(head_grads, query_kv_full).astype(narrow))
    normed_grad = (
        normed_combine
        + normed_sum
        + transposed_product(down_grad_low, laurel_full[:, :LAUREL_RANK])
    )
    predicted_grad = (predicted_grad[0] + active_grad, *predicted_grad[1:])
    version_grad, gains_predict, router_predict, coef_predict = pull_predict(
        (predicted_grad, normed_grad)
    )

    gains_grad = (gains_correct + gains_combine + gains_predict).at[7].add(gain_seven)
    head_gain_grad = kv_gain_grad.at[0].add(query_gain_grad)
    coef_grad = coef_correct + coef_predict
    packed = jnp.concatenate(
        [
            gains_grad,
            router_correct + router_predict,
            jnp.pad(
                jnp.concatenate([head_gain_grad.reshape(1, -1), coef_grad.reshape(1, -1)], axis=1),
                ((0, 3), (0, width - head_gain_grad.size - coef_grad.size)),
            ),
        ],
        axis=0,
    )
    packed = butterfly(packed)
    head_gain_sum = packed[12, : head_gain_grad.size].reshape(head_gain_grad.shape)
    coef_sum = packed[12, head_gain_grad.size : head_gain_grad.size + coef_grad.size].reshape(
        coef_grad.shape
    )

    small_sum = lax.psum(
        lax.psum_scatter(
            jnp.concatenate(
                [
                    weight_product(normed_low, down_grad_low),
                    weight_product(lifted_low, down_low),
                    weight_product(first_low, gate_pre_low),
                    weight_product(projected_low, gated_low),
                ],
                axis=1,
            ).astype(narrow),
            "blk",
            scatter_dimension=0,
            tiled=True,
        ),
        "heads",
    ).astype(wide)
    head_sum = own_rows(
        jnp.concatenate(
            [
                weight_product(normed_rows, head_grads).astype(narrow),
                weight_product(attention_rows, mixed_rows).astype(narrow),
            ],
            axis=1,
        )
    )

    def core_columns(x):
        top, bottom = x[:rows_here], x[rows_here:]
        keep = jnp.where(first_core, top, bottom)
        got = other_core(jnp.where(first_core, bottom, top))
        return jnp.where(first_core, keep, got), jnp.where(first_core, got, keep)

    head_first, head_second = core_columns(head_sum)
    unit_first, unit_second = core_columns(unit_sum)

    def both(index):
        columns = slice(index * HEAD_WIDTH, (index + 1) * HEAD_WIDTH)
        return [head_first[:, columns], head_second[:, columns]]

    line_all = lax.all_gather(
        jnp.concatenate(both(0) + both(2) + both(1), axis=1), "heads", axis=0, tiled=False
    ).astype(wide)
    pair = CORES * HEAD_WIDTH
    query_sum = jnp.concatenate([line_all[i, :, :pair] for i in range(LINE)], axis=1)
    out_sum = jnp.concatenate([line_all[i, :, pair : 2 * pair] for i in range(LINE)], axis=1)
    kv_lines = line_all[:, :, 2 * pair :]
    kv_groups = [kv_lines[0] + kv_lines[1], kv_lines[2] + kv_lines[3]]
    key_sum = jnp.concatenate([g[:, :HEAD_WIDTH] for g in kv_groups], axis=1)
    value_sum = jnp.concatenate([g[:, HEAD_WIDTH:] for g in kv_groups], axis=1)

    def unit(index):
        columns = slice(index * hidden, (index + 1) * hidden)
        return jnp.concatenate([unit_first[:, columns], unit_second[:, columns]], axis=1).astype(wide)

    ranks = 2 * LAUREL_RANK
    return (
        result,
        jnp.stack([g.astype(narrow) for g in version_grad]),
        layer_grad.astype(narrow),
        packed[:8],
        packed[8:12],
        coef_sum,
        head_gain_sum,
        query_sum,
        key_sum,
        value_sum,
        out_sum,
        small_sum[:, :ranks],
        small_sum[:, ranks : ranks + LAYER_INPUT_SIZE],
        small_sum[:, ranks + LAYER_INPUT_SIZE :],
        unit(0),
        unit(1),
        unit(2),
    )


def solution(mesh):
    by_chip = mesh.shape["heads"] == LINE and mesh.shape["blk"] == CORES * CHIPS
    on_device = chip_device if by_chip else general_device

    in_specs = (
        P(None, ("blk", "heads"), None),
        P(("blk", "heads"), None),
        P(("blk", "heads")),
        P(),
        P(None, ("blk", "heads"), None),
        P(),
        P(),
        P(),
        P(),
        P("blk", None),
        P("blk", None),
        P("blk", None),
        P("blk", None),
        P("blk", None),
        P("blk", None),
        P("blk", None),
        P("blk", "heads"),
        P("blk", "heads"),
        P("blk", "heads"),
    )
    out_specs = (
        P(None, ("blk", "heads"), None),
        P(None, ("blk", "heads"), None),
        P(("blk", "heads"), None),
        P(),
        P(),
        P(),
        P(),
        P("blk", None),
        P("blk", None),
        P("blk", None),
        P("blk", None),
        P("blk", None),
        P("blk", None),
        P("blk", None),
        P("blk", "heads"),
        P("blk", "heads"),
        P("blk", "heads"),
    )
    return jax.shard_map(
        on_device, mesh=mesh, in_specs=in_specs, out_specs=out_specs, check_vma=False
    )
```

```python
import jax
import jax.numpy as jnp
from jax import lax
from jax.experimental import pallas as pl
from jax.experimental.pallas import tpu as pltpu
from jax.sharding import PartitionSpec as P

QUERY_HEAD_COUNT = 8
KEY_VALUE_HEADS = 2
HEAD_WIDTH = 256
LAUREL_RANK = 64
LAYER_INPUT_SIZE = 256
KEYB = 2048


epsilon = 1e-06
rotary_base = 1000000.0
highest = lax.Precision.HIGHEST
root_half = 0.5**0.5


def rms_norm_apply(value_states, gain):
    return (
        value_states
        * lax.rsqrt(jnp.mean(value_states * value_states, axis=-1, keepdims=True) + epsilon)
        * gain
    )


def rotary_apply(value_states, cosine_table, sine_table):
    half = value_states.shape[-1] // 2
    turned = jnp.concatenate([-value_states[..., half:], value_states[..., :half]], axis=-1)
    return value_states * cosine_table + turned * sine_table


def angles(positions):
    frequency = rotary_base ** (-2.0 * jnp.arange(HEAD_WIDTH // 2, dtype=jnp.float32) / HEAD_WIDTH)
    phase = positions.astype(jnp.float32)[:, None] * frequency[None, :]
    phase = jnp.concatenate([phase, phase], axis=-1)[:, None, :]
    return (jnp.cos(phase), jnp.sin(phase))


def modes(value_states, gain, router):
    return jnp.tanh(jnp.dot(rms_norm_apply(value_states, gain), router.T, precision=highest))


def predict(versions, gain_rows, router, coefficients):
    token_count = versions.shape[1]
    table = jnp.dot(
        modes(versions[0], gain_rows[0], router), coefficients[:, :16], precision=highest
    ).reshape(token_count, 4, 4)
    predicted = versions + jnp.einsum("tij,jtd->itd", table, versions, precision=highest)
    return (predicted, rms_norm_apply(predicted[0], gain_rows[1]))


def prepare(query_states, key, value_states, query_key_gains, cosine_table, sine_table):
    token_count = query_states.shape[0]
    query_states = rotary_apply(
        rms_norm_apply(
            query_states.reshape(token_count, QUERY_HEAD_COUNT, HEAD_WIDTH), query_key_gains[0]
        ),
        cosine_table,
        sine_table,
    )
    key = rotary_apply(
        rms_norm_apply(key.reshape(token_count, KEY_VALUE_HEADS, HEAD_WIDTH), query_key_gains[1]),
        cosine_table,
        sine_table,
    )
    value_states = value_states.reshape(token_count, KEY_VALUE_HEADS, HEAD_WIDTH)
    value_states = value_states * lax.rsqrt(
        jnp.mean(value_states * value_states, axis=-1, keepdims=True) + epsilon
    )
    return (
        query_states,
        jnp.repeat(key, QUERY_HEAD_COUNT // KEY_VALUE_HEADS, axis=1),
        jnp.repeat(value_states, QUERY_HEAD_COUNT // KEY_VALUE_HEADS, axis=1),
    )


def combine(active, attention_out, normed, lifted, gain_rows):
    merged = (
        active
        + rms_norm_apply(attention_out, gain_rows[2])
        + normed
        + rms_norm_apply(lifted, gain_rows[3])
    ) * root_half
    return (merged, rms_norm_apply(merged, gain_rows[4]))


def activate(gate, up):
    return jax.nn.gelu(gate, approximate=True) * up


def correct(merged, fed, predicted, gain_rows, router, coefficients):
    activated = merged + rms_norm_apply(fed, gain_rows[5])
    scale = (
        jnp.dot(modes(activated, gain_rows[0], router), coefficients[:, 16:], precision=highest)
        + 1.0
    )
    corrected = predicted + scale.T[:, :, None] * (activated - predicted[0])[None]
    return (corrected, corrected[0] * gain_rows[6])


def finish(corrected, projected, gain_rows):
    extra = rms_norm_apply(projected, gain_rows[7])
    return corrected + jnp.stack([jnp.zeros_like(extra), extra, extra, extra])


def forward_product(left, right):
    return jnp.dot(left, right, preferred_element_type=jnp.float32)


def transposed_product(left, right):
    return lax.dot_general(
        left, right, (((1,), (1,)), ((), ())), preferred_element_type=jnp.float32
    )


def weight_product(left, right):
    return lax.dot_general(
        left, right, (((0,), (0,)), ((), ())), preferred_element_type=jnp.float32
    )


def general_device(
    versions,
    layer_input,
    positions,
    documents,
    cotangent,
    norm_gains,
    router_weight,
    coefficients,
    query_key_gains,
    query_weight,
    key_matrix,
    value_matrix,
    out_weight,
    laurel_weight,
    input_gate,
    input_projection,
    gate_weight,
    up_weight,
    down_weight,
):
    narrow = jnp.bfloat16
    wide = jnp.float32
    (
        query_full,
        key_full,
        value_full,
        out_full,
        laurel_full,
        gate_full,
        projection_full,
        unit_gate,
        unit_up,
        unit_down,
    ) = (
        lax.all_gather(query_weight, "blk", axis=0, tiled=True),
        lax.all_gather(key_matrix, "blk", axis=0, tiled=True),
        lax.all_gather(value_matrix, "blk", axis=0, tiled=True),
        lax.all_gather(out_weight, "blk", axis=0, tiled=True),
        lax.all_gather(laurel_weight, "blk", axis=0, tiled=True),
        lax.all_gather(input_gate, "blk", axis=0, tiled=True),
        lax.all_gather(input_projection, "blk", axis=0, tiled=True),
        lax.all_gather(gate_weight, "blk", axis=0, tiled=True),
        lax.all_gather(up_weight, "blk", axis=0, tiled=True),
        lax.all_gather(down_weight, "blk", axis=0, tiled=True),
    )
    gain_rows = norm_gains.astype(wide)
    router_wide = router_weight.astype(wide)
    coef_wide = coefficients.astype(wide)
    head_wide = query_key_gains.astype(wide)
    (predicted, normed), pull_predict = jax.vjp(
        predict, versions.astype(wide), gain_rows, router_wide, coef_wide
    )
    normed_low = normed.astype(narrow)
    cosine_table, sine_table = angles(positions)

    def prepare_here(query_states, key, value_states, gains_here):
        return prepare(query_states, key, value_states, gains_here, cosine_table, sine_table)

    (rotated, keys_rep, values_rep), pull_prepare = jax.vjp(
        prepare_here,
        forward_product(normed_low, query_full),
        forward_product(normed_low, key_full),
        forward_product(normed_low, value_full),
        head_wide,
    )
    query_heads, key_heads, value_heads = (
        lax.all_to_all(rotated.astype(narrow), "heads", split_axis=1, concat_axis=0, tiled=True),
        lax.all_to_all(keys_rep.astype(narrow), "heads", split_axis=1, concat_axis=0, tiled=True),
        lax.all_to_all(values_rep.astype(narrow), "heads", split_axis=1, concat_axis=0, tiled=True),
    )
    keys_all, values_all = (
        lax.all_gather(key_heads, "blk", axis=0, tiled=True),
        lax.all_gather(value_heads, "blk", axis=0, tiled=True),
    )
    piece, local_heads, head_size = query_heads.shape
    first_row = lax.axis_index("blk") * piece
    last_row = first_row + piece - 1
    query_rows = first_row + jnp.arange(piece, dtype=jnp.int32)
    query_docs = lax.dynamic_slice_in_dim(documents, first_row, piece)
    block_starts = jnp.arange(keys_all.shape[0] // KEYB, dtype=jnp.int32) * KEYB

    def block_scores(offset):
        key_block = lax.dynamic_slice_in_dim(keys_all, offset, KEYB)
        value_block = lax.dynamic_slice_in_dim(values_all, offset, KEYB)
        key_rows = offset + jnp.arange(KEYB, dtype=jnp.int32)
        key_docs = lax.dynamic_slice_in_dim(documents, offset, KEYB)
        allowed = (key_rows[None, :] <= query_rows[:, None]) & (
            key_docs[None, :] == query_docs[:, None]
        )
        scores = jnp.einsum("qhd,khd->hqk", query_heads, key_block, preferred_element_type=wide)
        return (key_block, value_block, allowed[None], jnp.where(allowed[None], scores, -1e30))

    def attend(state, offset):

        def visit(carry):
            top, total, summed = carry
            key_block, value_block, allowed, scores = block_scores(offset)
            new_top = jnp.maximum(top, jnp.max(scores, axis=-1))
            weights = jnp.where(allowed, jnp.exp(scores - new_top[:, :, None]), 0.0)
            decay = jnp.exp(top - new_top)
            summed = summed * decay.T[:, :, None] + jnp.einsum(
                "hqk,khd->qhd", weights.astype(narrow), value_block, preferred_element_type=wide
            )
            return (new_top, total * decay + jnp.sum(weights, axis=-1), summed)

        def keep(carry):
            return carry

        return (lax.cond(offset <= last_row, visit, keep, state), None)

    start_state = (
        jnp.full((local_heads, piece), -1e30, wide),
        jnp.zeros((local_heads, piece), wide),
        jnp.zeros((piece, local_heads, head_size), wide),
    )
    (top, total, summed), unused = lax.scan(attend, start_state, block_starts)
    log_total = top + jnp.log(total)
    attended = summed / total.T[:, :, None]
    mixed = lax.all_to_all(
        attended.astype(narrow), "heads", split_axis=0, concat_axis=1, tiled=True
    )
    mixed_low = mixed.reshape(mixed.shape[0], -1)
    attention_out = transposed_product(mixed_low, out_full)
    down_low = forward_product(normed_low, laurel_full[:, :LAUREL_RANK]).astype(narrow)
    lifted = transposed_product(down_low, laurel_full[:, LAUREL_RANK:])
    (merged, feed_in), pull_combine = jax.vjp(
        combine, predicted[0], attention_out, normed_low.astype(wide), lifted, gain_rows
    )
    feed_low = feed_in.astype(narrow)
    unit_rows = lax.all_gather(feed_low, "heads", axis=0, tiled=True)
    hidden, pull_activate = jax.vjp(
        activate, forward_product(unit_rows, unit_gate), forward_product(unit_rows, unit_up)
    )
    hidden_low = hidden.astype(narrow)
    fed = transposed_product(hidden_low, unit_down)
    fed = lax.psum_scatter(
        fed.astype(jnp.bfloat16), "heads", scatter_dimension=0, tiled=True
    ).astype(jnp.float32)
    (corrected, first), pull_correct = jax.vjp(
        correct, merged, fed, predicted, gain_rows, router_wide, coef_wide
    )
    first_low = first.astype(narrow)
    gated, pull_gate = jax.vjp(
        activate, forward_product(first_low, gate_full), layer_input.astype(wide)
    )
    gated_low = gated.astype(narrow)
    projected = transposed_product(gated_low, projection_full)
    result, pull_finish = jax.vjp(finish, corrected, projected, gain_rows)
    corrected_grad, projected_grad, gains_finish = pull_finish(cotangent.astype(wide))
    projected_low = projected_grad.astype(narrow)
    gate_pre_grad, layer_grad = pull_gate(forward_product(projected_low, projection_full))
    gate_pre_low = gate_pre_grad.astype(narrow)
    merged_grad, fed_grad, predicted_grad, gains_correct, router_correct, coef_correct = (
        pull_correct((corrected_grad, transposed_product(gate_pre_low, gate_full)))
    )
    fed_low = fed_grad.astype(narrow)
    fed_rows = lax.all_gather(fed_low, "heads", axis=0, tiled=True)
    gate_grad, up_grad = pull_activate(forward_product(fed_rows, unit_down))
    gate_low = gate_grad.astype(narrow)
    up_low = up_grad.astype(narrow)
    feed_grad = transposed_product(gate_low, unit_gate) + transposed_product(up_low, unit_up)
    feed_grad = lax.psum_scatter(
        feed_grad.astype(jnp.bfloat16), "heads", scatter_dimension=0, tiled=True
    ).astype(jnp.float32)
    active_grad, attention_grad, normed_combine, lifted_grad, gains_combine = pull_combine(
        (merged_grad, feed_grad)
    )
    lifted_low = lifted_grad.astype(narrow)
    down_grad_low = forward_product(lifted_low, laurel_full[:, LAUREL_RANK:]).astype(narrow)
    attention_low = attention_grad.astype(narrow)
    mixed_grad = forward_product(attention_low, out_full).astype(narrow).reshape(mixed.shape)
    attended_grad = lax.all_to_all(mixed_grad, "heads", split_axis=1, concat_axis=0, tiled=True)
    delta = jnp.sum(attended_grad.astype(wide) * attended, axis=-1).T

    def attend_back(query_grad, offset):

        def visit(query_grad):
            key_block, value_block, allowed, scores = block_scores(offset)
            shares = jnp.where(allowed, jnp.exp(scores - log_total[:, :, None]), 0.0)
            share_grad = jnp.einsum(
                "qhd,khd->hqk", attended_grad, value_block, preferred_element_type=wide
            )
            score_low = (shares * (share_grad - delta[:, :, None])).astype(narrow)
            query_grad = query_grad + jnp.einsum(
                "hqk,khd->qhd", score_low, key_block, preferred_element_type=wide
            )
            key_grad = jnp.einsum(
                "hqk,qhd->khd", score_low, query_heads, preferred_element_type=wide
            )
            value_grad = jnp.einsum(
                "hqk,qhd->khd", shares.astype(narrow), attended_grad, preferred_element_type=wide
            )
            return (query_grad, (key_grad, value_grad))

        def skip(query_grad):
            empty = jnp.zeros((KEYB, local_heads, head_size), wide)
            return (query_grad, (empty, empty))

        return lax.cond(offset <= last_row, visit, skip, query_grad)

    query_grad, (key_grads, value_grads) = lax.scan(
        attend_back, jnp.zeros((piece, local_heads, head_size), wide), block_starts
    )
    key_own, value_own = (
        lax.psum_scatter(
            key_grads.reshape(keys_all.shape).astype(jnp.bfloat16),
            "blk",
            scatter_dimension=0,
            tiled=True,
        ).astype(jnp.float32),
        lax.psum_scatter(
            value_grads.reshape(keys_all.shape).astype(jnp.bfloat16),
            "blk",
            scatter_dimension=0,
            tiled=True,
        ).astype(jnp.float32),
    )
    query_back, key_back, value_back = (
        lax.all_to_all(query_grad.astype(narrow), "heads", split_axis=0, concat_axis=1, tiled=True),
        lax.all_to_all(key_own.astype(narrow), "heads", split_axis=0, concat_axis=1, tiled=True),
        lax.all_to_all(value_own.astype(narrow), "heads", split_axis=0, concat_axis=1, tiled=True),
    )
    query_pre, key_pre, value_pre, head_grad = pull_prepare(
        (query_back.astype(wide), key_back.astype(wide), value_back.astype(wide))
    )
    query_low = query_pre.astype(narrow)
    key_low = key_pre.astype(narrow)
    value_low = value_pre.astype(narrow)
    normed_grad = (
        normed_combine
        + transposed_product(query_low, query_full)
        + transposed_product(key_low, key_full)
        + transposed_product(value_low, value_full)
        + transposed_product(down_grad_low, laurel_full[:, :LAUREL_RANK])
    )
    predicted_grad = predicted_grad.at[0].add(active_grad)
    version_grad, gains_predict, router_predict, coef_predict = pull_predict(
        (predicted_grad, normed_grad)
    )
    small = lax.psum(
        (
            gains_finish + gains_correct + gains_combine + gains_predict,
            router_correct + router_predict,
            coef_correct + coef_predict,
            head_grad,
        ),
        ("heads", "blk"),
    )
    normed_targets = jnp.concatenate([query_low, key_low, value_low, down_grad_low], axis=1)
    summed_grads = lax.psum_scatter(
        jnp.concatenate(
            [
                weight_product(normed_low, normed_targets),
                weight_product(attention_low, mixed_low),
                weight_product(lifted_low, down_low),
                weight_product(first_low, gate_pre_low),
                weight_product(projected_low, gated_low),
                weight_product(unit_rows, gate_low),
                weight_product(unit_rows, up_low),
                weight_product(fed_rows, hidden_low),
            ],
            axis=1,
        ).astype(jnp.bfloat16),
        "blk",
        scatter_dimension=0,
        tiled=True,
    ).astype(jnp.float32)
    bounds = [0]
    for feature_width in (
        QUERY_HEAD_COUNT * HEAD_WIDTH,
        KEY_VALUE_HEADS * HEAD_WIDTH,
        KEY_VALUE_HEADS * HEAD_WIDTH,
        LAUREL_RANK,
        QUERY_HEAD_COUNT * HEAD_WIDTH,
        LAUREL_RANK,
        LAYER_INPUT_SIZE,
        LAYER_INPUT_SIZE,
    ):
        bounds.append(bounds[-1] + feature_width)
    attention_sum = lax.psum(summed_grads[:, : bounds[8]].astype(jnp.bfloat16), "heads").astype(
        jnp.float32
    )
    parts = [attention_sum[:, bounds[place] : bounds[place + 1]] for place in range(8)]
    unit_width = (summed_grads.shape[1] - bounds[8]) // 3
    gate_part = summed_grads[:, bounds[8] : bounds[8] + unit_width]
    up_part = summed_grads[:, bounds[8] + unit_width : bounds[8] + 2 * unit_width]
    down_part = summed_grads[:, bounds[8] + 2 * unit_width :]
    return (
        result.astype(narrow),
        version_grad.astype(narrow),
        layer_grad.astype(narrow),
        small[0],
        small[1],
        small[2],
        small[3],
        parts[0],
        parts[1],
        parts[2],
        parts[4],
        jnp.concatenate([parts[3], parts[5]], axis=1),
        parts[6],
        parts[7],
        gate_part,
        up_part,
        down_part,
    )


CORES = 2
LINE = 4
CHIPS = 4


def along_heads(x, step):
    return lax.ppermute(x, "heads", [(i, (i + step) % LINE) for i in range(LINE)])


def across_blk(x, mask):
    return lax.ppermute(x, "blk", [(i, i ^ mask) for i in range(CORES * CHIPS)])


def other_core(x):
    return across_blk(x, 1)


def gather_chip(x):
    half = x.shape[0] // 2
    before = along_heads(x, 1)
    after = along_heads(x, -1)
    far = jnp.concatenate([along_heads(before[:half], 1), along_heads(after[half:], -1)], axis=0)
    own = [before, x, after, far]
    return jnp.concatenate(own + [other_core(part) for part in own], axis=0)


def scatter_chip(y):
    wide = jnp.float32
    n = y.shape[0] // 8
    half = n // 2
    before, own, after, far = (
        y[k * n : (k + 1) * n].astype(wide) + other_core(y[(k + 4) * n : (k + 5) * n]).astype(wide)
        for k in range(4)
    )
    far = far.astype(jnp.bfloat16)
    first = along_heads(far[:half], 1).astype(wide)
    second = along_heads(far[half:], -1).astype(wide)
    after = jnp.concatenate([after[:half] + first, after[half:]], axis=0).astype(jnp.bfloat16)
    before = jnp.concatenate([before[:half], before[half:] + second], axis=0).astype(jnp.bfloat16)
    return own + along_heads(after, 1).astype(wide) + along_heads(before, -1).astype(wide)


def in_line(parts):
    line = lax.axis_index("heads")
    rows = parts[0].shape[0]
    turned = turn(jnp.concatenate(parts, axis=0), (1 - line) % LINE)
    return [turned[k * rows : (k + 1) * rows] for k in range(LINE)]


def gather_line(x):
    half = x.shape[0] // 2
    before = along_heads(x, 1)
    after_ = along_heads(x, -1)
    far = jnp.concatenate([along_heads(before[:half], 1), along_heads(after_[half:], -1)], axis=0)
    return in_line([before, x, after_, far])


def share_line(x):
    line = lax.axis_index("heads")
    rows = x.shape[0] // LINE
    total = lax.dynamic_slice_in_dim(x, line * rows, rows).astype(jnp.float32)
    for step in range(1, LINE):
        piece = lax.dynamic_slice_in_dim(x, ((line + step) % LINE) * rows, rows)
        total = total + along_heads(piece, step).astype(jnp.float32)
    return total


def turn(x, blocks):
    rows = x.shape[0] // LINE
    twice = jnp.concatenate([x, x], axis=0)
    return lax.dynamic_slice_in_dim(twice, blocks * rows, x.shape[0])


def natural(x, core, line):
    half = x.shape[0] // 2
    own, other = (turn(part, (1 - line) % LINE) for part in (x[:half], x[half:]))
    first = core == 0
    return jnp.concatenate([jnp.where(first, own, other), jnp.where(first, other, own)], axis=0)


def arrival(x, core, line):
    half = x.shape[0] // 2
    first = core == 0
    own, other = jnp.where(first, x[:half], x[half:]), jnp.where(first, x[half:], x[:half])
    return jnp.concatenate([turn(part, (line - 1) % LINE) for part in (own, other)], axis=0)


def gather_chips(x):
    half = x.shape[0] // 2
    side = across_blk(x, 2)
    front = across_blk(x, 4)
    return side, front, across_blk(side[:half], 4), across_blk(front[half:], 2)


def scatter_chips(parts, *others):
    wide = jnp.float32
    half = parts[0].shape[0] // 2
    own, side, front, far = parts
    low = across_blk(jnp.concatenate([side[:half], far[:half]], axis=0), 2)
    high = across_blk(jnp.concatenate([front[half:], far[half:]], axis=0), 4)
    front_sum = (front[:half].astype(wide) + low[half:].astype(wide)).astype(jnp.bfloat16)
    side_sum = (side[half:].astype(wide) + high[half:].astype(wide)).astype(jnp.bfloat16)
    front_sum, side_sum, *others = together(front_sum, side_sum, *others)
    upper = own[:half].astype(wide) + low[:half].astype(wide) + across_blk(front_sum, 4).astype(wide)
    lower = own[half:].astype(wide) + high[:half].astype(wide) + across_blk(side_sum, 2).astype(wide)
    return jnp.concatenate([upper, lower], axis=0), *others


def butterfly(x):
    for mask in (1, 2, 4):
        x = x + across_blk(x, mask)
    for mask in (1, 2):
        x = x + lax.ppermute(x, "heads", [(i, i ^ mask) for i in range(LINE)])
    return x


def chip_groups():
    return [[core + CORES * chip for chip in range(CHIPS)] for core in range(CORES)]


def weight_rows(keep, send, core):
    got = other_core(send)
    first = core == 0
    return jnp.concatenate([jnp.where(first, keep, got), jnp.where(first, got, keep)], axis=0)


def all_rows(x):
    return lax.all_gather(x, "blk", axis=0, tiled=True, axis_index_groups=chip_groups())


def own_rows(x):
    return lax.psum_scatter(
        x, "blk", scatter_dimension=0, tiled=True, axis_index_groups=chip_groups()
    )


def together(*values):
    return lax.optimization_barrier(values)


def pick(x, start, size):
    return lax.dynamic_slice_in_dim(x, start, size, axis=1)


QUERY_ROWS = 512
KEY_ROWS = 512


def place_rows(target, parts, chip):
    own, side, front, near, far = parts
    size = own.shape[0]
    half = size // 2
    target[pl.ds(pl.multiple_of(chip * size, size), size), :] = own[...]
    target[pl.ds(pl.multiple_of((chip ^ 1) * size, size), size), :] = side[...]
    target[pl.ds(pl.multiple_of((chip ^ 2) * size, size), size), :] = front[...]
    base = (chip ^ 3) * size
    target[pl.ds(pl.multiple_of(base, size), half), :] = near[...]
    target[pl.ds(pl.multiple_of(base + half, half), half), :] = far[...]


def place_both(meta, mine, theirs, k_all, v_all):
    chip = meta[0]

    @pl.when(meta[1] == 0)
    def _():
        place_rows(k_all, mine, chip)
        place_rows(v_all, theirs, chip)

    @pl.when(meta[1] != 0)
    def _():
        place_rows(v_all, mine, chip)
        place_rows(k_all, theirs, chip)


def rows_times_rows(left, right):
    return lax.dot_general(
        left, right, (((1,), (1,)), ((), ())), preferred_element_type=jnp.float32
    )


def columns_times_columns(left, right):
    return lax.dot_general(
        left, right, (((0,), (0,)), ((), ())), preferred_element_type=jnp.float32
    )


def attend_kernel(meta, q_ref, lo_ref, *refs):
    mine, theirs = refs[:5], refs[5:10]
    out_ref, lse_ref, k_all, v_all, total, summed = refs[10:]
    place_both(meta, mine, theirs, k_all, v_all)
    own = q_ref.shape[0]
    for part in range(own // QUERY_ROWS):
        rows = pl.ds(part * QUERY_ROWS, QUERY_ROWS)
        first = meta[0] * own + part * QUERY_ROWS
        total[...] = jnp.zeros_like(total)
        summed[...] = jnp.zeros_like(summed)

        def visit(block, masked, rows=rows, first=first):
            at = pl.multiple_of(block * KEY_ROWS, KEY_ROWS)
            scores = rows_times_rows(q_ref[rows, :], k_all[pl.ds(at, KEY_ROWS), :])
            weights = jnp.exp(scores)
            if masked:
                key = at + lax.broadcasted_iota(jnp.int32, weights.shape, 1)
                query = first + lax.broadcasted_iota(jnp.int32, weights.shape, 0)
                weights = jnp.where((key >= lo_ref[rows, :]) & (key <= query), weights, 0.0)
            for lane in range(0, KEY_ROWS, 128):
                total[...] += weights[:, lane : lane + 128]
            summed[...] += jnp.dot(
                weights.astype(jnp.bfloat16),
                v_all[pl.ds(at, KEY_ROWS), :],
                preferred_element_type=jnp.float32,
            )

        start, full_from = meta[2 + 2 * part], meta[3 + 2 * part]
        end = (first + QUERY_ROWS - 1) // KEY_ROWS + 1
        full_from = jnp.minimum(full_from, end)
        full_to = jnp.maximum(jnp.minimum((first + 1) // KEY_ROWS, end), full_from)

        @pl.loop(start, full_from)
        def _(block, visit=visit):
            visit(block, True)

        @pl.loop(full_from, full_to)
        def _(block, visit=visit):
            visit(block, False)

        @pl.loop(full_to, end)
        def _(block, visit=visit):
            visit(block, True)

        denominator = jnp.sum(total[...], axis=1, keepdims=True)
        out_ref[rows, :] = summed[...] / denominator
        lse_ref[rows, :] = jnp.log(denominator)


def attend_back_kernel(meta, q_ref, grad_ref, lse_ref, delta_ref, lo_ref, *refs):
    mine, theirs = refs[:5], refs[5:10]
    dq_ref, keep_ref, send_ref, k_all, v_all, dk_sum, dv_sum = refs[10:]
    place_both(meta, mine, theirs, k_all, v_all)
    chip = meta[0]
    own = q_ref.shape[0]
    parts = own // QUERY_ROWS
    keep_ref[...] = jnp.zeros_like(keep_ref)
    send_ref[...] = jnp.zeros_like(send_ref)
    dq_ref[...] = jnp.zeros_like(dq_ref)
    per_chip = own // KEY_ROWS

    @pl.loop(meta[2], (chip + 1) * per_chip)
    def _(block):
        at = pl.multiple_of(block * KEY_ROWS, KEY_ROWS)
        dk_sum[...] = jnp.zeros_like(dk_sum)
        dv_sum[...] = jnp.zeros_like(dv_sum)
        for part in range(parts):
            rows = pl.ds(part * QUERY_ROWS, QUERY_ROWS)
            first = chip * own + part * QUERY_ROWS

            def visit(masked, rows=rows, first=first):
                keys = k_all[pl.ds(at, KEY_ROWS), :]
                queries = q_ref[rows, :]
                grads = grad_ref[rows, :]
                shares = jnp.exp(rows_times_rows(keys, queries) - lse_ref[:, rows])
                if masked:
                    key = at + lax.broadcasted_iota(jnp.int32, shares.shape, 0)
                    query = first + lax.broadcasted_iota(jnp.int32, shares.shape, 1)
                    shares = jnp.where((key >= lo_ref[:, rows]) & (key <= query), shares, 0.0)
                share_grad = rows_times_rows(v_all[pl.ds(at, KEY_ROWS), :], grads)
                score_grad = (shares * (share_grad - delta_ref[:, rows])).astype(jnp.bfloat16)
                dv_sum[...] += jnp.dot(
                    shares.astype(jnp.bfloat16), grads, preferred_element_type=jnp.float32
                )
                dk_sum[...] += jnp.dot(score_grad, queries, preferred_element_type=jnp.float32)
                dq_ref[rows, :] += columns_times_columns(score_grad, keys)

            start, full_from = meta[2 + 2 * part], meta[3 + 2 * part]
            full = (block >= full_from) & ((block + 1) * KEY_ROWS <= first + 1)
            needed = (block >= start) & (block * KEY_ROWS < first + QUERY_ROWS)

            @pl.when(full)
            def _(visit=visit):
                visit(False)

            @pl.when(needed & jnp.logical_not(full))
            def _(visit=visit):
                visit(True)

        place = (block // per_chip) ^ chip
        inner = pl.multiple_of((block % per_chip) * KEY_ROWS, KEY_ROWS)
        dk_low = dk_sum[...].astype(jnp.bfloat16)
        dv_low = dv_sum[...].astype(jnp.bfloat16)

        @pl.when(meta[1] == 0)
        def _():
            keep_ref[place, pl.ds(inner, KEY_ROWS), :] = dk_low
            send_ref[place, pl.ds(inner, KEY_ROWS), :] = dv_low

        @pl.when(meta[1] != 0)
        def _():
            keep_ref[place, pl.ds(inner, KEY_ROWS), :] = dv_low
            send_ref[place, pl.ds(inner, KEY_ROWS), :] = dk_low


def in_vmem(count):
    return [pl.BlockSpec(memory_space=pltpu.VMEM)] * count


def attend_here(meta, q, lo, mine, theirs):
    own, width = q.shape
    row = own * CHIPS
    return pl.pallas_call(
        attend_kernel,
        out_shape=(
            jax.ShapeDtypeStruct((own, width), jnp.float32),
            jax.ShapeDtypeStruct((own, 1), jnp.float32),
        ),
        in_specs=[pl.BlockSpec(memory_space=pltpu.SMEM)] + in_vmem(12),
        out_specs=tuple(in_vmem(2)),
        scratch_shapes=[
            pltpu.VMEM((row, width), jnp.bfloat16),
            pltpu.VMEM((row, width), jnp.bfloat16),
            pltpu.VMEM((QUERY_ROWS, 128), jnp.float32),
            pltpu.VMEM((QUERY_ROWS, width), jnp.float32),
        ],
        compiler_params=pltpu.CompilerParams(vmem_limit_bytes=40 << 20),
        cost_estimate=pl.CostEstimate(
            flops=2 * own * row * width, bytes_accessed=6 * row * width, transcendentals=own * row // 2
        ),
    )(meta, q, lo.reshape(own, 1), *mine, *theirs)


def attend_back_here(meta, q, grad, lse, delta, lo, mine, theirs):
    own, width = q.shape
    row = own * CHIPS
    return pl.pallas_call(
        attend_back_kernel,
        out_shape=(
            jax.ShapeDtypeStruct((own, width), jnp.float32),
            jax.ShapeDtypeStruct((CHIPS, own, width), jnp.bfloat16),
            jax.ShapeDtypeStruct((CHIPS, own, width), jnp.bfloat16),
        ),
        in_specs=[pl.BlockSpec(memory_space=pltpu.SMEM)] + in_vmem(15),
        out_specs=tuple(in_vmem(3)),
        scratch_shapes=[
            pltpu.VMEM((row, width), jnp.bfloat16),
            pltpu.VMEM((row, width), jnp.bfloat16),
            pltpu.VMEM((KEY_ROWS, width), jnp.float32),
            pltpu.VMEM((KEY_ROWS, width), jnp.float32),
        ],
        compiler_params=pltpu.CompilerParams(vmem_limit_bytes=48 << 20),
        cost_estimate=pl.CostEstimate(
            flops=5 * own * row * width, bytes_accessed=12 * row * width, transcendentals=own * row // 2
        ),
    )(
        meta, q, grad, lse.reshape(1, own), delta.reshape(1, own), lo.reshape(1, own), *mine, *theirs
    )


def predict_list(versions, gain_rows, router, coefficients):
    table = jnp.dot(
        modes(versions[0], gain_rows[0], router), coefficients[:, :16], precision=highest
    )
    predicted = []
    for i in range(4):
        value = versions[i]
        for j in range(4):
            value = value + table[:, 4 * i + j : 4 * i + j + 1] * versions[j]
        predicted.append(value)
    return (tuple(predicted), rms_norm_apply(predicted[0], gain_rows[1]))


def correct_list(merged, fed, predicted, gain_rows, router, coefficients):
    activated = merged + rms_norm_apply(fed, gain_rows[5])
    scale = (
        jnp.dot(modes(activated, gain_rows[0], router), coefficients[:, 16:], precision=highest)
        + 1.0
    )
    change = activated - predicted[0]
    corrected = tuple(predicted[i] + scale[:, i : i + 1] * change for i in range(4))
    return (corrected, corrected[0] * gain_rows[6])


def head_apply(x, gain, cosine, sine):
    normed = x * lax.rsqrt(jnp.mean(x * x, axis=-1, keepdims=True) + epsilon) * gain
    half = x.shape[-1] // 2
    turned = jnp.concatenate([-normed[:, half:], normed[:, :half]], axis=-1)
    return normed * cosine + turned * sine


def chip_device(
    versions,
    layer_input,
    positions,
    documents,
    cotangent,
    norm_gains,
    router_weight,
    coefficients,
    query_key_gains,
    query_weight,
    key_matrix,
    value_matrix,
    out_weight,
    laurel_weight,
    input_gate,
    input_projection,
    gate_weight,
    up_weight,
    down_weight,
):
    narrow = jnp.bfloat16
    wide = jnp.float32
    line = lax.axis_index("heads")
    piece = lax.axis_index("blk")
    core = piece % CORES
    chip = piece // CORES
    first_core = core == 0
    tokens = versions.shape[1]
    own = 8 * tokens
    width = versions.shape[2]
    rows_here = query_weight.shape[0]
    hidden = gate_weight.shape[1] // CORES
    head = CORES * line + core
    group = head // (QUERY_HEAD_COUNT // KEY_VALUE_HEADS)

    def head_columns(index, kv):
        return jnp.concatenate(
            [
                pick(query_weight, index * HEAD_WIDTH, HEAD_WIDTH),
                pick(kv, group * HEAD_WIDTH, HEAD_WIDTH),
                pick(out_weight, index * HEAD_WIDTH, HEAD_WIDTH),
            ],
            axis=1,
        )

    kv_mine = jnp.where(first_core, key_matrix, value_matrix)
    kv_theirs = jnp.where(first_core, value_matrix, key_matrix)
    head_full = all_rows(
        weight_rows(head_columns(head, kv_mine), head_columns(head ^ 1, kv_theirs), core)
    )
    small_full = lax.all_gather(
        jnp.concatenate([laurel_weight, input_gate, input_projection], axis=1),
        "blk",
        axis=0,
        tiled=True,
    )

    query_kv_full = head_full[:, : 2 * HEAD_WIDTH]
    out_full = head_full[:, 2 * HEAD_WIDTH :]
    laurel_full = small_full[:, : 2 * LAUREL_RANK]
    gate_full = small_full[:, 2 * LAUREL_RANK : 2 * LAUREL_RANK + LAYER_INPUT_SIZE]
    projection_full = small_full[:, 2 * LAUREL_RANK + LAYER_INPUT_SIZE :]
    gain_rows = norm_gains.astype(wide)
    router_wide = router_weight.astype(wide)
    coef_wide = coefficients.astype(wide)
    head_wide = query_key_gains.astype(wide)
    (predicted, normed), pull_predict = jax.vjp(
        predict_list,
        tuple(versions[i].astype(wide) for i in range(4)),
        gain_rows,
        router_wide,
        coef_wide,
    )
    normed_low = normed.astype(narrow)
    *unit_weights, normed_low = together(gate_weight, up_weight, down_weight, normed_low)

    def hidden_columns(index):
        return jnp.concatenate([pick(w, index * hidden, hidden) for w in unit_weights], axis=1)

    unit_full = all_rows(weight_rows(hidden_columns(core), hidden_columns(1 - core), core))
    unit_two = unit_full[:, : 2 * hidden]
    unit_gate = unit_full[:, :hidden]
    unit_up = unit_full[:, hidden : 2 * hidden]
    unit_down = unit_full[:, 2 * hidden :]

    digits = jnp.stack([positions // 128, positions % 128], axis=1).astype(narrow)
    sent = jnp.concatenate([normed_low, jnp.pad(digits, ((0, 0), (0, 126)))], axis=1)
    gathered = gather_chip(sent)
    normed_rows = gathered[:, :width]
    digits_all = natural(gathered[:, width : width + 2].astype(wide), core, line)
    phase_position = digits_all[:, :1] * 128.0 + digits_all[:, 1:2]
    frequency = rotary_base ** (-2.0 * jnp.arange(HEAD_WIDTH // 2, dtype=wide) / HEAD_WIDTH)
    phase = phase_position * frequency[None, :]
    phase = jnp.concatenate([phase, phase], axis=-1)
    cosine, sine = jnp.cos(phase), jnp.sin(phase)
    cosine_kv = jnp.where(first_core, cosine, 1.0)
    sine_kv = jnp.where(first_core, sine, 0.0)

    def kv_gain(gains):
        return jnp.where(first_core, gains[1], 1.0)

    query_kv = natural(forward_product(normed_rows, query_kv_full), core, line)
    query_pre = query_kv[:, :HEAD_WIDTH]
    kv_pre = query_kv[:, HEAD_WIDTH:]
    rotated = head_apply(query_pre, head_wide[0], cosine, sine).astype(narrow)
    kv_own = head_apply(kv_pre, kv_gain(head_wide), cosine_kv, sine_kv).astype(narrow)
    mine = (kv_own, *gather_chips(kv_own))
    theirs = tuple(other_core(part) for part in mine)

    first_row = chip * own
    row_docs = lax.dynamic_slice_in_dim(documents, first_row, own)
    begin_one = jnp.sum(documents < 1)
    begin_two = jnp.sum(documents < 2)
    lo = jnp.where(row_docs == 0, 0, jnp.where(row_docs == 1, begin_one, begin_two)).astype(jnp.int32)
    bounds = []
    for part in range(own // QUERY_ROWS):
        bounds.append(lo[part * QUERY_ROWS] // KEY_ROWS)
        bounds.append((lo[(part + 1) * QUERY_ROWS - 1] + KEY_ROWS - 1) // KEY_ROWS)
    meta = jnp.stack([chip, core, *bounds]).astype(jnp.int32)
    attended, lse = attend_here(meta, rotated, lo, mine, theirs)
    mixed_rows = arrival(attended.astype(narrow), core, line)
    attention_out = scatter_chip(transposed_product(mixed_rows, out_full).astype(narrow))

    down_low = forward_product(normed_low, laurel_full[:, :LAUREL_RANK]).astype(narrow)
    lifted = transposed_product(down_low, laurel_full[:, LAUREL_RANK:])
    (merged, feed_in), pull_combine = jax.vjp(
        combine, predicted[0], attention_out, normed_low.astype(wide), lifted, gain_rows
    )
    unit_rows = gather_chip(feed_in.astype(narrow))
    hidden_units, pull_activate = jax.vjp(
        activate, forward_product(unit_rows, unit_gate), forward_product(unit_rows, unit_up)
    )
    hidden_low = hidden_units.astype(narrow)
    fed = scatter_chip(transposed_product(hidden_low, unit_down).astype(narrow))
    (corrected, first), pull_correct = jax.vjp(
        correct_list, merged, fed, predicted, gain_rows, router_wide, coef_wide
    )
    first_low = first.astype(narrow)
    gated, pull_gate = jax.vjp(
        activate, forward_product(first_low, gate_full), layer_input.astype(wide)
    )
    gated_low = gated.astype(narrow)
    projected = transposed_product(gated_low, projection_full)
    extra, pull_extra = jax.vjp(rms_norm_apply, projected, gain_rows[7])
    result = jnp.stack(
        [corrected[0].astype(narrow)] + [(corrected[i] + extra).astype(narrow) for i in (1, 2, 3)]
    )

    def core_columns(x):
        top, bottom = x[:rows_here], x[rows_here:]
        keep = jnp.where(first_core, top, bottom)
        got = other_core(jnp.where(first_core, bottom, top))
        return jnp.where(first_core, keep, got), jnp.where(first_core, got, keep)

    def pairs(x, count):
        first, second = core_columns(x)
        parts = []
        for index in range(count):
            columns = slice(index * HEAD_WIDTH, (index + 1) * HEAD_WIDTH)
            parts += [first[:, columns], second[:, columns]]
        return jnp.concatenate(parts, axis=1)

    corrected_grad = tuple(cotangent[i].astype(wide) for i in range(4))
    projected_grad, gain_seven = pull_extra(
        corrected_grad[1] + corrected_grad[2] + corrected_grad[3]
    )
    projected_low = projected_grad.astype(narrow)
    gate_pre_grad, layer_grad = pull_gate(forward_product(projected_low, projection_full))
    gate_pre_low = gate_pre_grad.astype(narrow)
    merged_grad, fed_grad, predicted_grad, gains_correct, router_correct, coef_correct = (
        pull_correct((corrected_grad, transposed_product(gate_pre_low, gate_full)))
    )
    io_sum = lax.psum_scatter(
        jnp.concatenate(
            [weight_product(first_low, gate_pre_low), weight_product(projected_low, gated_low)],
            axis=1,
        ).astype(narrow),
        "blk",
        scatter_dimension=0,
        tiled=True,
    )
    fed_rows = gather_chip(fed_grad.astype(narrow))
    fed_rows, io_sum = together(fed_rows, io_sum)
    io_share = share_line(io_sum).astype(narrow)
    gate_grad, up_grad = pull_activate(forward_product(fed_rows, unit_down))
    two_low = jnp.concatenate([gate_grad.astype(narrow), up_grad.astype(narrow)], axis=1)
    feed_grad = scatter_chip(transposed_product(two_low, unit_two).astype(narrow))
    down_part = weight_product(fed_rows, hidden_low).astype(narrow)
    two_part = weight_product(unit_rows, two_low).astype(narrow)
    down_sum = own_rows(down_part)
    two_sum = own_rows(two_part)
    active_grad, attention_grad, normed_combine, lifted_grad, gains_combine = pull_combine(
        (merged_grad, feed_grad)
    )
    attention_low = attention_grad.astype(narrow)
    lifted_low = lifted_grad.astype(narrow)
    down_grad_low = forward_product(lifted_low, laurel_full[:, LAUREL_RANK:]).astype(narrow)
    laurel_part = jnp.concatenate(
        [weight_product(normed_low, down_grad_low), weight_product(lifted_low, down_low)], axis=1
    ).astype(narrow)
    laurel_part = laurel_part + other_core(laurel_part)
    attention_rows = gather_chip(attention_low)
    out_part = jnp.concatenate(
        [weight_product(attention_rows, mixed_rows).astype(narrow), laurel_part], axis=1
    )
    mixed_grad_rows = forward_product(attention_rows, out_full).astype(narrow)
    mixed_grad_rows, down_sum, two_sum, io_share, out_part = together(
        mixed_grad_rows, down_sum, two_sum, io_share, out_part
    )
    out_sum = own_rows(out_part)
    mixed_grad = natural(mixed_grad_rows, core, line)
    delta = jnp.sum(mixed_grad.astype(wide) * attended, axis=-1)
    query_grad, kv_keep, kv_send = attend_back_here(
        meta, rotated, mixed_grad, lse, delta, lo, mine, theirs
    )
    _, pull_query = jax.vjp(
        lambda x, g: head_apply(x, g, cosine, sine), query_pre, head_wide[0]
    )
    query_pre_grad, query_gain_grad = pull_query(query_grad.astype(narrow).astype(wide))
    query_rows_grad = arrival(query_pre_grad.astype(narrow), core, line)
    query_part = weight_product(normed_rows, query_rows_grad).astype(narrow)
    kv_got = other_core(kv_send)
    *kv_parts, out_sum = together(
        *[(kv_keep[m].astype(wide) + kv_got[m].astype(wide)).astype(narrow) for m in range(CHIPS)],
        out_sum,
    )
    kv_grad, query_part = scatter_chips(kv_parts, query_part)
    query_sum = own_rows(query_part)

    _, pull_kv = jax.vjp(
        lambda x, g: head_apply(x, kv_gain(g), cosine_kv, sine_kv), kv_pre, head_wide
    )
    kv_pre_grad, kv_gain_grad = pull_kv(kv_grad)
    kv_rows_grad = arrival(kv_pre_grad.astype(narrow), core, line)
    head_grads = jnp.concatenate([query_rows_grad, kv_rows_grad], axis=1)
    kv_part = weight_product(normed_rows, kv_rows_grad).astype(narrow)
    normed_part = transposed_product(head_grads, query_kv_full).astype(narrow)
    normed_part, kv_part, query_sum, down_sum, two_sum = together(
        normed_part, kv_part, query_sum, down_sum, two_sum
    )
    kv_weight_sum = own_rows(kv_part)
    normed_sum = scatter_chip(normed_part)
    normed_sum, query_sum = together(normed_sum, query_sum)
    normed_grad = (
        normed_combine
        + normed_sum
        + transposed_product(down_grad_low, laurel_full[:, :LAUREL_RANK])
    )
    predicted_grad = (predicted_grad[0] + active_grad, *predicted_grad[1:])
    version_grad, gains_predict, router_predict, coef_predict = pull_predict(
        (predicted_grad, normed_grad)
    )

    gains_grad = (gains_correct + gains_combine + gains_predict).at[7].add(gain_seven)
    head_gain_grad = kv_gain_grad.at[0].add(query_gain_grad)
    coef_grad = coef_correct + coef_predict
    packed = jnp.concatenate(
        [
            gains_grad,
            router_correct + router_predict,
            jnp.pad(
                jnp.concatenate([head_gain_grad.reshape(1, -1), coef_grad.reshape(1, -1)], axis=1),
                ((0, 3), (0, width - head_gain_grad.size - coef_grad.size)),
            ),
        ],
        axis=0,
    )
    packed = butterfly(packed)
    head_gain_sum = packed[12, : head_gain_grad.size].reshape(head_gain_grad.shape)
    coef_sum = packed[12, head_gain_grad.size : head_gain_grad.size + coef_grad.size].reshape(
        coef_grad.shape
    )

    down_first, down_second = core_columns(down_sum)
    two_first, two_second = core_columns(two_sum)
    pair = CORES * HEAD_WIDTH
    ranks = 2 * LAUREL_RANK
    laurel_here = jnp.where(
        first_core, out_sum[:rows_here, HEAD_WIDTH:], out_sum[rows_here:, HEAD_WIDTH:]
    )
    out_lines = gather_line(
        jnp.concatenate([pairs(out_sum, 1), laurel_here, io_share.reshape(rows_here, -1)], axis=1)
    )
    query_lines = gather_line(pairs(query_sum, 1))
    kv_lines = gather_line(pairs(kv_weight_sum, 1))
    query_all = jnp.concatenate(query_lines, axis=1).astype(wide)
    out_all = jnp.concatenate([part[:, :pair] for part in out_lines], axis=1).astype(wide)
    laurel_all = sum(part[:, pair : pair + ranks].astype(wide) for part in out_lines)
    io_all = jnp.concatenate(
        [
            part[:, pair + ranks :].reshape(rows_here // LINE, 2 * LAYER_INPUT_SIZE)
            for part in out_lines
        ],
        axis=0,
    ).astype(wide)
    kv_groups = [
        kv_lines[k].astype(wide) + kv_lines[k + 1].astype(wide) for k in range(0, LINE, 2)
    ]
    key_sum = jnp.concatenate([g[:, :HEAD_WIDTH] for g in kv_groups], axis=1)
    value_sum = jnp.concatenate([g[:, HEAD_WIDTH:] for g in kv_groups], axis=1)

    def unit(index):
        columns = slice(index * hidden, (index + 1) * hidden)
        return jnp.concatenate([two_first[:, columns], two_second[:, columns]], axis=1).astype(wide)

    return (
        result,
        jnp.stack([g.astype(narrow) for g in version_grad]),
        layer_grad.astype(narrow),
        packed[:8],
        packed[8:12],
        coef_sum,
        head_gain_sum,
        query_all,
        key_sum,
        value_sum,
        out_all,
        laurel_all,
        io_all[:, :LAYER_INPUT_SIZE],
        io_all[:, LAYER_INPUT_SIZE:],
        unit(0),
        unit(1),
        jnp.concatenate([down_first, down_second], axis=1).astype(wide),
    )


def solution(mesh):
    by_chip = mesh.shape["heads"] == LINE and mesh.shape["blk"] == CORES * CHIPS
    on_device = chip_device if by_chip else general_device

    in_specs = (
        P(None, ("blk", "heads"), None),
        P(("blk", "heads"), None),
        P(("blk", "heads")),
        P(),
        P(None, ("blk", "heads"), None),
        P(),
        P(),
        P(),
        P(),
        P("blk", None),
        P("blk", None),
        P("blk", None),
        P("blk", None),
        P("blk", None),
        P("blk", None),
        P("blk", None),
        P("blk", "heads"),
        P("blk", "heads"),
        P("blk", "heads"),
    )
    out_specs = (
        P(None, ("blk", "heads"), None),
        P(None, ("blk", "heads"), None),
        P(("blk", "heads"), None),
        P(),
        P(),
        P(),
        P(),
        P("blk", None),
        P("blk", None),
        P("blk", None),
        P("blk", None),
        P("blk", None),
        P("blk", None),
        P("blk", None),
        P("blk", "heads"),
        P("blk", "heads"),
        P("blk", "heads"),
    )
    return jax.shard_map(
        on_device, mesh=mesh, in_specs=in_specs, out_specs=out_specs, check_vma=False
    )
```

```python
import jax
import jax.numpy as jnp
from jax import lax
from jax.experimental import pallas as pl
from jax.experimental.pallas import tpu as pltpu
from jax.sharding import PartitionSpec as P

QUERY_HEAD_COUNT = 8
KEY_VALUE_HEADS = 2
HEAD_WIDTH = 256
LAUREL_RANK = 64
LAYER_INPUT_SIZE = 256
KEYB = 2048


epsilon = 1e-06
rotary_base = 1000000.0
highest = lax.Precision.HIGHEST
root_half = 0.5**0.5


def rms_norm_apply(value_states, gain):
    return (
        value_states
        * lax.rsqrt(jnp.mean(value_states * value_states, axis=-1, keepdims=True) + epsilon)
        * gain
    )


def rotary_apply(value_states, cosine_table, sine_table):
    half = value_states.shape[-1] // 2
    turned = jnp.concatenate([-value_states[..., half:], value_states[..., :half]], axis=-1)
    return value_states * cosine_table + turned * sine_table


def angles(positions):
    frequency = rotary_base ** (-2.0 * jnp.arange(HEAD_WIDTH // 2, dtype=jnp.float32) / HEAD_WIDTH)
    phase = positions.astype(jnp.float32)[:, None] * frequency[None, :]
    phase = jnp.concatenate([phase, phase], axis=-1)[:, None, :]
    return (jnp.cos(phase), jnp.sin(phase))


def modes(value_states, gain, router):
    return jnp.tanh(jnp.dot(rms_norm_apply(value_states, gain), router.T, precision=highest))


def predict(versions, gain_rows, router, coefficients):
    token_count = versions.shape[1]
    table = jnp.dot(
        modes(versions[0], gain_rows[0], router), coefficients[:, :16], precision=highest
    ).reshape(token_count, 4, 4)
    predicted = versions + jnp.einsum("tij,jtd->itd", table, versions, precision=highest)
    return (predicted, rms_norm_apply(predicted[0], gain_rows[1]))


def prepare(query_states, key, value_states, query_key_gains, cosine_table, sine_table):
    token_count = query_states.shape[0]
    query_states = rotary_apply(
        rms_norm_apply(
            query_states.reshape(token_count, QUERY_HEAD_COUNT, HEAD_WIDTH), query_key_gains[0]
        ),
        cosine_table,
        sine_table,
    )
    key = rotary_apply(
        rms_norm_apply(key.reshape(token_count, KEY_VALUE_HEADS, HEAD_WIDTH), query_key_gains[1]),
        cosine_table,
        sine_table,
    )
    value_states = value_states.reshape(token_count, KEY_VALUE_HEADS, HEAD_WIDTH)
    value_states = value_states * lax.rsqrt(
        jnp.mean(value_states * value_states, axis=-1, keepdims=True) + epsilon
    )
    return (
        query_states,
        jnp.repeat(key, QUERY_HEAD_COUNT // KEY_VALUE_HEADS, axis=1),
        jnp.repeat(value_states, QUERY_HEAD_COUNT // KEY_VALUE_HEADS, axis=1),
    )


def combine(active, attention_out, normed, lifted, gain_rows):
    merged = (
        active
        + rms_norm_apply(attention_out, gain_rows[2])
        + normed
        + rms_norm_apply(lifted, gain_rows[3])
    ) * root_half
    return (merged, rms_norm_apply(merged, gain_rows[4]))


def activate(gate, up):
    return jax.nn.gelu(gate, approximate=True) * up


def correct(merged, fed, predicted, gain_rows, router, coefficients):
    activated = merged + rms_norm_apply(fed, gain_rows[5])
    scale = (
        jnp.dot(modes(activated, gain_rows[0], router), coefficients[:, 16:], precision=highest)
        + 1.0
    )
    corrected = predicted + scale.T[:, :, None] * (activated - predicted[0])[None]
    return (corrected, corrected[0] * gain_rows[6])


def finish(corrected, projected, gain_rows):
    extra = rms_norm_apply(projected, gain_rows[7])
    return corrected + jnp.stack([jnp.zeros_like(extra), extra, extra, extra])


def forward_product(left, right):
    return jnp.dot(left, right, preferred_element_type=jnp.float32)


def transposed_product(left, right):
    return lax.dot_general(
        left, right, (((1,), (1,)), ((), ())), preferred_element_type=jnp.float32
    )


def weight_product(left, right):
    return lax.dot_general(
        left, right, (((0,), (0,)), ((), ())), preferred_element_type=jnp.float32
    )


def general_device(
    versions,
    layer_input,
    positions,
    documents,
    cotangent,
    norm_gains,
    router_weight,
    coefficients,
    query_key_gains,
    query_weight,
    key_matrix,
    value_matrix,
    out_weight,
    laurel_weight,
    input_gate,
    input_projection,
    gate_weight,
    up_weight,
    down_weight,
):
    narrow = jnp.bfloat16
    wide = jnp.float32
    (
        query_full,
        key_full,
        value_full,
        out_full,
        laurel_full,
        gate_full,
        projection_full,
        unit_gate,
        unit_up,
        unit_down,
    ) = (
        lax.all_gather(query_weight, "blk", axis=0, tiled=True),
        lax.all_gather(key_matrix, "blk", axis=0, tiled=True),
        lax.all_gather(value_matrix, "blk", axis=0, tiled=True),
        lax.all_gather(out_weight, "blk", axis=0, tiled=True),
        lax.all_gather(laurel_weight, "blk", axis=0, tiled=True),
        lax.all_gather(input_gate, "blk", axis=0, tiled=True),
        lax.all_gather(input_projection, "blk", axis=0, tiled=True),
        lax.all_gather(gate_weight, "blk", axis=0, tiled=True),
        lax.all_gather(up_weight, "blk", axis=0, tiled=True),
        lax.all_gather(down_weight, "blk", axis=0, tiled=True),
    )
    gain_rows = norm_gains.astype(wide)
    router_wide = router_weight.astype(wide)
    coef_wide = coefficients.astype(wide)
    head_wide = query_key_gains.astype(wide)
    (predicted, normed), pull_predict = jax.vjp(
        predict, versions.astype(wide), gain_rows, router_wide, coef_wide
    )
    normed_low = normed.astype(narrow)
    cosine_table, sine_table = angles(positions)

    def prepare_here(query_states, key, value_states, gains_here):
        return prepare(query_states, key, value_states, gains_here, cosine_table, sine_table)

    (rotated, keys_rep, values_rep), pull_prepare = jax.vjp(
        prepare_here,
        forward_product(normed_low, query_full),
        forward_product(normed_low, key_full),
        forward_product(normed_low, value_full),
        head_wide,
    )
    query_heads, key_heads, value_heads = (
        lax.all_to_all(rotated.astype(narrow), "heads", split_axis=1, concat_axis=0, tiled=True),
        lax.all_to_all(keys_rep.astype(narrow), "heads", split_axis=1, concat_axis=0, tiled=True),
        lax.all_to_all(values_rep.astype(narrow), "heads", split_axis=1, concat_axis=0, tiled=True),
    )
    keys_all, values_all = (
        lax.all_gather(key_heads, "blk", axis=0, tiled=True),
        lax.all_gather(value_heads, "blk", axis=0, tiled=True),
    )
    piece, local_heads, head_size = query_heads.shape
    first_row = lax.axis_index("blk") * piece
    last_row = first_row + piece - 1
    query_rows = first_row + jnp.arange(piece, dtype=jnp.int32)
    query_docs = lax.dynamic_slice_in_dim(documents, first_row, piece)
    block_starts = jnp.arange(keys_all.shape[0] // KEYB, dtype=jnp.int32) * KEYB

    def block_scores(offset):
        key_block = lax.dynamic_slice_in_dim(keys_all, offset, KEYB)
        value_block = lax.dynamic_slice_in_dim(values_all, offset, KEYB)
        key_rows = offset + jnp.arange(KEYB, dtype=jnp.int32)
        key_docs = lax.dynamic_slice_in_dim(documents, offset, KEYB)
        allowed = (key_rows[None, :] <= query_rows[:, None]) & (
            key_docs[None, :] == query_docs[:, None]
        )
        scores = jnp.einsum("qhd,khd->hqk", query_heads, key_block, preferred_element_type=wide)
        return (key_block, value_block, allowed[None], jnp.where(allowed[None], scores, -1e30))

    def attend(state, offset):

        def visit(carry):
            top, total, summed = carry
            key_block, value_block, allowed, scores = block_scores(offset)
            new_top = jnp.maximum(top, jnp.max(scores, axis=-1))
            weights = jnp.where(allowed, jnp.exp(scores - new_top[:, :, None]), 0.0)
            decay = jnp.exp(top - new_top)
            summed = summed * decay.T[:, :, None] + jnp.einsum(
                "hqk,khd->qhd", weights.astype(narrow), value_block, preferred_element_type=wide
            )
            return (new_top, total * decay + jnp.sum(weights, axis=-1), summed)

        def keep(carry):
            return carry

        return (lax.cond(offset <= last_row, visit, keep, state), None)

    start_state = (
        jnp.full((local_heads, piece), -1e30, wide),
        jnp.zeros((local_heads, piece), wide),
        jnp.zeros((piece, local_heads, head_size), wide),
    )
    (top, total, summed), unused = lax.scan(attend, start_state, block_starts)
    log_total = top + jnp.log(total)
    attended = summed / total.T[:, :, None]
    mixed = lax.all_to_all(
        attended.astype(narrow), "heads", split_axis=0, concat_axis=1, tiled=True
    )
    mixed_low = mixed.reshape(mixed.shape[0], -1)
    attention_out = transposed_product(mixed_low, out_full)
    down_low = forward_product(normed_low, laurel_full[:, :LAUREL_RANK]).astype(narrow)
    lifted = transposed_product(down_low, laurel_full[:, LAUREL_RANK:])
    (merged, feed_in), pull_combine = jax.vjp(
        combine, predicted[0], attention_out, normed_low.astype(wide), lifted, gain_rows
    )
    feed_low = feed_in.astype(narrow)
    unit_rows = lax.all_gather(feed_low, "heads", axis=0, tiled=True)
    hidden, pull_activate = jax.vjp(
        activate, forward_product(unit_rows, unit_gate), forward_product(unit_rows, unit_up)
    )
    hidden_low = hidden.astype(narrow)
    fed = transposed_product(hidden_low, unit_down)
    fed = lax.psum_scatter(
        fed.astype(jnp.bfloat16), "heads", scatter_dimension=0, tiled=True
    ).astype(jnp.float32)
    (corrected, first), pull_correct = jax.vjp(
        correct, merged, fed, predicted, gain_rows, router_wide, coef_wide
    )
    first_low = first.astype(narrow)
    gated, pull_gate = jax.vjp(
        activate, forward_product(first_low, gate_full), layer_input.astype(wide)
    )
    gated_low = gated.astype(narrow)
    projected = transposed_product(gated_low, projection_full)
    result, pull_finish = jax.vjp(finish, corrected, projected, gain_rows)
    corrected_grad, projected_grad, gains_finish = pull_finish(cotangent.astype(wide))
    projected_low = projected_grad.astype(narrow)
    gate_pre_grad, layer_grad = pull_gate(forward_product(projected_low, projection_full))
    gate_pre_low = gate_pre_grad.astype(narrow)
    merged_grad, fed_grad, predicted_grad, gains_correct, router_correct, coef_correct = (
        pull_correct((corrected_grad, transposed_product(gate_pre_low, gate_full)))
    )
    fed_low = fed_grad.astype(narrow)
    fed_rows = lax.all_gather(fed_low, "heads", axis=0, tiled=True)
    gate_grad, up_grad = pull_activate(forward_product(fed_rows, unit_down))
    gate_low = gate_grad.astype(narrow)
    up_low = up_grad.astype(narrow)
    feed_grad = transposed_product(gate_low, unit_gate) + transposed_product(up_low, unit_up)
    feed_grad = lax.psum_scatter(
        feed_grad.astype(jnp.bfloat16), "heads", scatter_dimension=0, tiled=True
    ).astype(jnp.float32)
    active_grad, attention_grad, normed_combine, lifted_grad, gains_combine = pull_combine(
        (merged_grad, feed_grad)
    )
    lifted_low = lifted_grad.astype(narrow)
    down_grad_low = forward_product(lifted_low, laurel_full[:, LAUREL_RANK:]).astype(narrow)
    attention_low = attention_grad.astype(narrow)
    mixed_grad = forward_product(attention_low, out_full).astype(narrow).reshape(mixed.shape)
    attended_grad = lax.all_to_all(mixed_grad, "heads", split_axis=1, concat_axis=0, tiled=True)
    delta = jnp.sum(attended_grad.astype(wide) * attended, axis=-1).T

    def attend_back(query_grad, offset):

        def visit(query_grad):
            key_block, value_block, allowed, scores = block_scores(offset)
            shares = jnp.where(allowed, jnp.exp(scores - log_total[:, :, None]), 0.0)
            share_grad = jnp.einsum(
                "qhd,khd->hqk", attended_grad, value_block, preferred_element_type=wide
            )
            score_low = (shares * (share_grad - delta[:, :, None])).astype(narrow)
            query_grad = query_grad + jnp.einsum(
                "hqk,khd->qhd", score_low, key_block, preferred_element_type=wide
            )
            key_grad = jnp.einsum(
                "hqk,qhd->khd", score_low, query_heads, preferred_element_type=wide
            )
            value_grad = jnp.einsum(
                "hqk,qhd->khd", shares.astype(narrow), attended_grad, preferred_element_type=wide
            )
            return (query_grad, (key_grad, value_grad))

        def skip(query_grad):
            empty = jnp.zeros((KEYB, local_heads, head_size), wide)
            return (query_grad, (empty, empty))

        return lax.cond(offset <= last_row, visit, skip, query_grad)

    query_grad, (key_grads, value_grads) = lax.scan(
        attend_back, jnp.zeros((piece, local_heads, head_size), wide), block_starts
    )
    key_own, value_own = (
        lax.psum_scatter(
            key_grads.reshape(keys_all.shape).astype(jnp.bfloat16),
            "blk",
            scatter_dimension=0,
            tiled=True,
        ).astype(jnp.float32),
        lax.psum_scatter(
            value_grads.reshape(keys_all.shape).astype(jnp.bfloat16),
            "blk",
            scatter_dimension=0,
            tiled=True,
        ).astype(jnp.float32),
    )
    query_back, key_back, value_back = (
        lax.all_to_all(query_grad.astype(narrow), "heads", split_axis=0, concat_axis=1, tiled=True),
        lax.all_to_all(key_own.astype(narrow), "heads", split_axis=0, concat_axis=1, tiled=True),
        lax.all_to_all(value_own.astype(narrow), "heads", split_axis=0, concat_axis=1, tiled=True),
    )
    query_pre, key_pre, value_pre, head_grad = pull_prepare(
        (query_back.astype(wide), key_back.astype(wide), value_back.astype(wide))
    )
    query_low = query_pre.astype(narrow)
    key_low = key_pre.astype(narrow)
    value_low = value_pre.astype(narrow)
    normed_grad = (
        normed_combine
        + transposed_product(query_low, query_full)
        + transposed_product(key_low, key_full)
        + transposed_product(value_low, value_full)
        + transposed_product(down_grad_low, laurel_full[:, :LAUREL_RANK])
    )
    predicted_grad = predicted_grad.at[0].add(active_grad)
    version_grad, gains_predict, router_predict, coef_predict = pull_predict(
        (predicted_grad, normed_grad)
    )
    small = lax.psum(
        (
            gains_finish + gains_correct + gains_combine + gains_predict,
            router_correct + router_predict,
            coef_correct + coef_predict,
            head_grad,
        ),
        ("heads", "blk"),
    )
    normed_targets = jnp.concatenate([query_low, key_low, value_low, down_grad_low], axis=1)
    summed_grads = lax.psum_scatter(
        jnp.concatenate(
            [
                weight_product(normed_low, normed_targets),
                weight_product(attention_low, mixed_low),
                weight_product(lifted_low, down_low),
                weight_product(first_low, gate_pre_low),
                weight_product(projected_low, gated_low),
                weight_product(unit_rows, gate_low),
                weight_product(unit_rows, up_low),
                weight_product(fed_rows, hidden_low),
            ],
            axis=1,
        ).astype(jnp.bfloat16),
        "blk",
        scatter_dimension=0,
        tiled=True,
    ).astype(jnp.float32)
    bounds = [0]
    for feature_width in (
        QUERY_HEAD_COUNT * HEAD_WIDTH,
        KEY_VALUE_HEADS * HEAD_WIDTH,
        KEY_VALUE_HEADS * HEAD_WIDTH,
        LAUREL_RANK,
        QUERY_HEAD_COUNT * HEAD_WIDTH,
        LAUREL_RANK,
        LAYER_INPUT_SIZE,
        LAYER_INPUT_SIZE,
    ):
        bounds.append(bounds[-1] + feature_width)
    attention_sum = lax.psum(summed_grads[:, : bounds[8]].astype(jnp.bfloat16), "heads").astype(
        jnp.float32
    )
    parts = [attention_sum[:, bounds[place] : bounds[place + 1]] for place in range(8)]
    unit_width = (summed_grads.shape[1] - bounds[8]) // 3
    gate_part = summed_grads[:, bounds[8] : bounds[8] + unit_width]
    up_part = summed_grads[:, bounds[8] + unit_width : bounds[8] + 2 * unit_width]
    down_part = summed_grads[:, bounds[8] + 2 * unit_width :]
    return (
        result.astype(narrow),
        version_grad.astype(narrow),
        layer_grad.astype(narrow),
        small[0],
        small[1],
        small[2],
        small[3],
        parts[0],
        parts[1],
        parts[2],
        parts[4],
        jnp.concatenate([parts[3], parts[5]], axis=1),
        parts[6],
        parts[7],
        gate_part,
        up_part,
        down_part,
    )


CORES = 2
LINE = 4
CHIPS = 4


def along_heads(x, step):
    return lax.ppermute(x, "heads", [(i, (i + step) % LINE) for i in range(LINE)])


def across_blk(x, mask):
    return lax.ppermute(x, "blk", [(i, i ^ mask) for i in range(CORES * CHIPS)])


def other_core(x):
    return across_blk(x, 1)


def gather_chip(x, *others):
    half = x.shape[0] // 2
    before = along_heads(x, 1)
    after = along_heads(x, -1)
    if others:
        before, after, *others = together(before, after, *others)
    far = jnp.concatenate([along_heads(before[:half], 1), along_heads(after[half:], -1)], axis=0)
    own = [before, x, after, far]
    rows = jnp.concatenate(own + [other_core(part) for part in own], axis=0)
    return (rows, *others) if others else rows


def scatter_chip(y, *others):
    wide = jnp.float32
    n = y.shape[0] // 8
    half = n // 2
    before, own, after, far = (
        y[k * n : (k + 1) * n].astype(wide) + other_core(y[(k + 4) * n : (k + 5) * n]).astype(wide)
        for k in range(4)
    )
    far = far.astype(jnp.bfloat16)
    first = along_heads(far[:half], 1).astype(wide)
    second = along_heads(far[half:], -1).astype(wide)
    after = jnp.concatenate([after[:half] + first, after[half:]], axis=0).astype(jnp.bfloat16)
    before = jnp.concatenate([before[:half], before[half:] + second], axis=0).astype(jnp.bfloat16)
    if others:
        after, before, *others = together(after, before, *others)
    total = own + along_heads(after, 1).astype(wide) + along_heads(before, -1).astype(wide)
    return (total, *others) if others else total


def line_neighbours(x):
    return along_heads(x, 1), along_heads(x, -1)


def line_far(x, before, after):
    half = x.shape[0] // 2
    return along_heads(before[:half], 1), along_heads(after[half:], -1)


def share_line(x):
    line = lax.axis_index("heads")
    rows = x.shape[0] // LINE
    total = lax.dynamic_slice_in_dim(x, line * rows, rows).astype(jnp.float32)
    for step in range(1, LINE):
        piece = lax.dynamic_slice_in_dim(x, ((line + step) % LINE) * rows, rows)
        total = total + along_heads(piece, step).astype(jnp.float32)
    return total


def turn(x, blocks):
    rows = x.shape[0] // LINE
    twice = jnp.concatenate([x, x], axis=0)
    return lax.dynamic_slice_in_dim(twice, blocks * rows, x.shape[0])


def natural(x, core, line):
    half = x.shape[0] // 2
    own, other = (turn(part, (1 - line) % LINE) for part in (x[:half], x[half:]))
    first = core == 0
    return jnp.concatenate([jnp.where(first, own, other), jnp.where(first, other, own)], axis=0)


def arrival(x, core, line):
    half = x.shape[0] // 2
    first = core == 0
    own, other = jnp.where(first, x[:half], x[half:]), jnp.where(first, x[half:], x[:half])
    return jnp.concatenate([turn(part, (line - 1) % LINE) for part in (own, other)], axis=0)


def gather_chips(x):
    half = x.shape[0] // 2
    side = across_blk(x, 2)
    front = across_blk(x, 4)
    return side, front, across_blk(side[:half], 4), across_blk(front[half:], 2)


def scatter_chips(parts, *others):
    wide = jnp.float32
    half = parts[0].shape[0] // 2
    own, side, front, far = parts
    low = across_blk(jnp.concatenate([side[:half], far[:half]], axis=0), 2)
    high = across_blk(jnp.concatenate([front[half:], far[half:]], axis=0), 4)
    front_sum = (front[:half].astype(wide) + low[half:].astype(wide)).astype(jnp.bfloat16)
    side_sum = (side[half:].astype(wide) + high[half:].astype(wide)).astype(jnp.bfloat16)
    front_sum, side_sum, *others = together(front_sum, side_sum, *others)
    upper = own[:half].astype(wide) + low[:half].astype(wide) + across_blk(front_sum, 4).astype(wide)
    lower = own[half:].astype(wide) + high[:half].astype(wide) + across_blk(side_sum, 2).astype(wide)
    return jnp.concatenate([upper, lower], axis=0), *others


def butterfly(x):
    for mask in (1, 2, 4):
        x = x + across_blk(x, mask)
    for mask in (1, 2):
        x = x + lax.ppermute(x, "heads", [(i, i ^ mask) for i in range(LINE)])
    return x


def chip_groups():
    return [[core + CORES * chip for chip in range(CHIPS)] for core in range(CORES)]


def weight_rows(keep, send, core):
    got = other_core(send)
    first = core == 0
    return jnp.concatenate([jnp.where(first, keep, got), jnp.where(first, got, keep)], axis=0)


def all_rows(x):
    return lax.all_gather(x, "blk", axis=0, tiled=True, axis_index_groups=chip_groups())


def own_rows(x):
    return lax.psum_scatter(
        x, "blk", scatter_dimension=0, tiled=True, axis_index_groups=chip_groups()
    )


def together(*values):
    return lax.optimization_barrier(values)


def pick(x, start, size):
    return lax.dynamic_slice_in_dim(x, start, size, axis=1)


QUERY_ROWS = 512
KEY_ROWS = 512


def place_rows(target, parts, chip):
    own, side, front, near, far = parts
    size = own.shape[0]
    half = size // 2
    target[pl.ds(pl.multiple_of(chip * size, size), size), :] = own[...]
    target[pl.ds(pl.multiple_of((chip ^ 1) * size, size), size), :] = side[...]
    target[pl.ds(pl.multiple_of((chip ^ 2) * size, size), size), :] = front[...]
    base = (chip ^ 3) * size
    target[pl.ds(pl.multiple_of(base, size), half), :] = near[...]
    target[pl.ds(pl.multiple_of(base + half, half), half), :] = far[...]


def place_both(meta, mine, theirs, k_all, v_all):
    chip = meta[0]

    @pl.when(meta[1] == 0)
    def _():
        place_rows(k_all, mine, chip)
        place_rows(v_all, theirs, chip)

    @pl.when(meta[1] != 0)
    def _():
        place_rows(v_all, mine, chip)
        place_rows(k_all, theirs, chip)


def rows_times_rows(left, right):
    return lax.dot_general(
        left, right, (((1,), (1,)), ((), ())), preferred_element_type=jnp.float32
    )


def columns_times_columns(left, right):
    return lax.dot_general(
        left, right, (((0,), (0,)), ((), ())), preferred_element_type=jnp.float32
    )


def arrival_rows(meta, block, rows):
    place = lax.rem(block % LINE - meta[2] + 1 + LINE, LINE)
    place = place + jnp.where(meta[1] == block // LINE, 0, LINE)
    return pl.ds(pl.multiple_of(place * rows, rows), rows)


def head_forward(x, gain, cosine, sine):
    normed = x * lax.rsqrt(jnp.mean(x * x, axis=-1, keepdims=True) + epsilon) * gain
    half = x.shape[-1] // 2
    low, high = normed[:, :half], normed[:, half:]
    return jnp.concatenate([low * cosine - high * sine, high * cosine + low * sine], axis=-1)


def head_backward(x, grad, gain, cosine, sine):
    half = x.shape[-1] // 2
    low, high = grad[:, :half], grad[:, half:]
    turned = jnp.concatenate([low * cosine + high * sine, high * cosine - low * sine], axis=-1)
    scale = lax.rsqrt(jnp.mean(x * x, axis=-1, keepdims=True) + epsilon)
    normed = x * scale
    inner = turned * gain
    x_grad = scale * (inner - normed * jnp.mean(inner * normed, axis=-1, keepdims=True))
    return x_grad, jnp.sum(turned * normed, axis=0, keepdims=True)


def kv_tables(meta, gain, cosine, sine):
    is_key = meta[1] == 0
    return jnp.where(is_key, gain, 1.0), jnp.where(is_key, cosine, 1.0), jnp.where(is_key, sine, 0.0)


def heads_kernel(meta, x_ref, w_ref, cosine_ref, sine_ref, gain_ref, q_ref, kv_ref, pre_ref, total):
    own, width = q_ref.shape
    depth = w_ref.shape[0]
    for half in range(CORES):
        rows = pl.ds(half * (own // CORES), own // CORES)
        total[rows, :] = jnp.dot(
            x_ref[rows, :depth], w_ref[:, : 2 * width], preferred_element_type=jnp.float32
        )
    size = own // (CORES * LINE)
    for block in range(CORES * LINE):
        rows = pl.ds(block * size, size)
        pre = total[arrival_rows(meta, block, size), :]
        pre_ref[rows, :] = pre
        cosine, sine = cosine_ref[rows, :], sine_ref[rows, :]
        q_ref[rows, :] = head_forward(pre[:, :width], gain_ref[0:1, :], cosine, sine).astype(q_ref.dtype)
        kv_ref[rows, :] = head_forward(
            pre[:, width:], *kv_tables(meta, gain_ref[1:2, :], cosine, sine)
        ).astype(kv_ref.dtype)


def kv_back_kernel(meta, pre_ref, grad_ref, cosine_ref, sine_ref, gain_ref, out_ref, gain_grad_ref):
    own, width = grad_ref.shape
    size = own // (CORES * LINE)
    total = jnp.zeros((1, width), jnp.float32)
    for block in range(CORES * LINE):
        rows = pl.ds(block * size, size)
        x_grad, gain_grad = head_backward(
            pre_ref[rows, width:],
            grad_ref[rows, :],
            *kv_tables(meta, gain_ref[1:2, :], cosine_ref[rows, :], sine_ref[rows, :]),
        )
        out_ref[arrival_rows(meta, block, size), :] = x_grad.astype(out_ref.dtype)
        total = total + gain_grad
    gain_grad_ref[...] = jnp.where(meta[1] == 0, total, 0.0)


def attend_kernel(meta, q_ref, lo_ref, *refs):
    mine, theirs = refs[:5], refs[5:10]
    out_ref, lse_ref, k_all, v_all, total, summed = refs[10:]
    place_both(meta, mine, theirs, k_all, v_all)
    own = q_ref.shape[0]
    for part in range(own // QUERY_ROWS):
        rows = pl.ds(part * QUERY_ROWS, QUERY_ROWS)
        first = meta[0] * own + part * QUERY_ROWS
        total[...] = jnp.zeros_like(total)
        summed[...] = jnp.zeros_like(summed)

        def visit(block, masked, rows=rows, first=first):
            at = pl.multiple_of(block * KEY_ROWS, KEY_ROWS)
            scores = rows_times_rows(q_ref[rows, :], k_all[pl.ds(at, KEY_ROWS), :])
            weights = jnp.exp(scores)
            if masked:
                key = at + lax.broadcasted_iota(jnp.int32, weights.shape, 1)
                query = first + lax.broadcasted_iota(jnp.int32, weights.shape, 0)
                weights = jnp.where((key >= lo_ref[rows, :]) & (key <= query), weights, 0.0)
            for lane in range(0, KEY_ROWS, 128):
                total[...] += weights[:, lane : lane + 128]
            summed[...] += jnp.dot(
                weights.astype(jnp.bfloat16),
                v_all[pl.ds(at, KEY_ROWS), :],
                preferred_element_type=jnp.float32,
            )

        start, full_from = meta[3 + 2 * part], meta[4 + 2 * part]
        end = (first + QUERY_ROWS - 1) // KEY_ROWS + 1
        full_from = jnp.minimum(full_from, end)
        full_to = jnp.maximum(jnp.minimum((first + 1) // KEY_ROWS, end), full_from)

        @pl.loop(start, full_from)
        def _(block, visit=visit):
            visit(block, True)

        @pl.loop(full_from, full_to)
        def _(block, visit=visit):
            visit(block, False)

        @pl.loop(full_to, end)
        def _(block, visit=visit):
            visit(block, True)

        denominator = jnp.sum(total[...], axis=1, keepdims=True)
        out_ref[rows, :] = summed[...] / denominator
        lse_ref[rows, :] = jnp.log(denominator)


def attend_back_kernel(
    meta, q_ref, grad_ref, lse_ref, delta_ref, lo_ref, pre_ref, cosine_ref, sine_ref, gain_ref, *refs
):
    mine, theirs = refs[:5], refs[5:10]
    out_ref, gain_grad_ref, keep_ref, send_ref, k_all, v_all, dk_sum, dv_sum, dq_ref = refs[10:]
    place_both(meta, mine, theirs, k_all, v_all)
    chip = meta[0]
    own = q_ref.shape[0]
    parts = own // QUERY_ROWS
    keep_ref[...] = jnp.zeros_like(keep_ref)
    send_ref[...] = jnp.zeros_like(send_ref)
    dq_ref[...] = jnp.zeros_like(dq_ref)
    per_chip = own // KEY_ROWS

    @pl.loop(meta[3], (chip + 1) * per_chip)
    def _(block):
        at = pl.multiple_of(block * KEY_ROWS, KEY_ROWS)
        dk_sum[...] = jnp.zeros_like(dk_sum)
        dv_sum[...] = jnp.zeros_like(dv_sum)
        for part in range(parts):
            rows = pl.ds(part * QUERY_ROWS, QUERY_ROWS)
            first = chip * own + part * QUERY_ROWS

            def visit(masked, rows=rows, first=first):
                keys = k_all[pl.ds(at, KEY_ROWS), :]
                queries = q_ref[rows, :]
                grads = grad_ref[rows, :]
                shares = jnp.exp(rows_times_rows(keys, queries) - lse_ref[:, rows])
                if masked:
                    key = at + lax.broadcasted_iota(jnp.int32, shares.shape, 0)
                    query = first + lax.broadcasted_iota(jnp.int32, shares.shape, 1)
                    shares = jnp.where((key >= lo_ref[:, rows]) & (key <= query), shares, 0.0)
                share_grad = rows_times_rows(v_all[pl.ds(at, KEY_ROWS), :], grads)
                score_grad = (shares * (share_grad - delta_ref[:, rows])).astype(jnp.bfloat16)
                dv_sum[...] += jnp.dot(
                    shares.astype(jnp.bfloat16), grads, preferred_element_type=jnp.float32
                )
                dk_sum[...] += jnp.dot(score_grad, queries, preferred_element_type=jnp.float32)
                dq_ref[rows, :] += columns_times_columns(score_grad, keys)

            start, full_from = meta[3 + 2 * part], meta[4 + 2 * part]
            full = (block >= full_from) & ((block + 1) * KEY_ROWS <= first + 1)
            needed = (block >= start) & (block * KEY_ROWS < first + QUERY_ROWS)

            @pl.when(full)
            def _(visit=visit):
                visit(False)

            @pl.when(needed & jnp.logical_not(full))
            def _(visit=visit):
                visit(True)

        place = (block // per_chip) ^ chip
        inner = pl.multiple_of((block % per_chip) * KEY_ROWS, KEY_ROWS)
        dk_low = dk_sum[...].astype(jnp.bfloat16)
        dv_low = dv_sum[...].astype(jnp.bfloat16)

        @pl.when(meta[1] == 0)
        def _():
            keep_ref[place, pl.ds(inner, KEY_ROWS), :] = dk_low
            send_ref[place, pl.ds(inner, KEY_ROWS), :] = dv_low

        @pl.when(meta[1] != 0)
        def _():
            keep_ref[place, pl.ds(inner, KEY_ROWS), :] = dv_low
            send_ref[place, pl.ds(inner, KEY_ROWS), :] = dk_low

    width = q_ref.shape[1]
    size = own // (CORES * LINE)
    total = jnp.zeros((1, width), jnp.float32)
    for block in range(CORES * LINE):
        rows = pl.ds(block * size, size)
        x_grad, gain_grad = head_backward(
            pre_ref[rows, :width],
            dq_ref[rows, :].astype(jnp.bfloat16).astype(jnp.float32),
            gain_ref[0:1, :],
            cosine_ref[rows, :],
            sine_ref[rows, :],
        )
        out_ref[arrival_rows(meta, block, size), :] = x_grad.astype(out_ref.dtype)
        total = total + gain_grad
    gain_grad_ref[...] = total


def takes(microseconds):
    return pl.CostEstimate(
        flops=int(microseconds * 1e9), bytes_accessed=int(microseconds * 3.3e6), transcendentals=0
    )


def in_vmem(count):
    return [pl.BlockSpec(memory_space=pltpu.VMEM)] * count


def attend_here(meta, q, lo, mine, theirs):
    own, width = q.shape
    row = own * CHIPS
    return pl.pallas_call(
        attend_kernel,
        out_shape=(
            jax.ShapeDtypeStruct((own, width), jnp.float32),
            jax.ShapeDtypeStruct((own, 1), jnp.float32),
        ),
        in_specs=[pl.BlockSpec(memory_space=pltpu.SMEM)] + in_vmem(12),
        out_specs=tuple(in_vmem(2)),
        scratch_shapes=[
            pltpu.VMEM((row, width), jnp.bfloat16),
            pltpu.VMEM((row, width), jnp.bfloat16),
            pltpu.VMEM((QUERY_ROWS, 128), jnp.float32),
            pltpu.VMEM((QUERY_ROWS, width), jnp.float32),
        ],
        compiler_params=pltpu.CompilerParams(vmem_limit_bytes=40 << 20),
        cost_estimate=takes(11),
    )(meta, q, lo.reshape(own, 1), *mine, *theirs)


def attend_back_here(meta, q, grad, lse, delta, lo, tables, mine, theirs):
    own, width = q.shape
    row = own * CHIPS
    return pl.pallas_call(
        attend_back_kernel,
        out_shape=(
            jax.ShapeDtypeStruct((own, width), jnp.bfloat16),
            jax.ShapeDtypeStruct((1, width), jnp.float32),
            jax.ShapeDtypeStruct((CHIPS, own, width), jnp.bfloat16),
            jax.ShapeDtypeStruct((CHIPS, own, width), jnp.bfloat16),
        ),
        in_specs=[pl.BlockSpec(memory_space=pltpu.SMEM)] + in_vmem(19),
        out_specs=tuple(in_vmem(4)),
        scratch_shapes=[
            pltpu.VMEM((row, width), jnp.bfloat16),
            pltpu.VMEM((row, width), jnp.bfloat16),
            pltpu.VMEM((KEY_ROWS, width), jnp.float32),
            pltpu.VMEM((KEY_ROWS, width), jnp.float32),
            pltpu.VMEM((own, width), jnp.float32),
        ],
        compiler_params=pltpu.CompilerParams(vmem_limit_bytes=48 << 20),
        cost_estimate=takes(20.5),
    )(
        meta,
        q,
        grad,
        lse.reshape(1, own),
        delta.reshape(1, own),
        lo.reshape(1, own),
        *tables,
        *mine,
        *theirs,
    )


def heads_here(meta, x, weights, cosine, sine, gains):
    own, width = x.shape[0], gains.shape[1]
    return pl.pallas_call(
        heads_kernel,
        out_shape=(
            jax.ShapeDtypeStruct((own, width), jnp.bfloat16),
            jax.ShapeDtypeStruct((own, width), jnp.bfloat16),
            jax.ShapeDtypeStruct((own, 2 * width), jnp.float32),
        ),
        in_specs=[pl.BlockSpec(memory_space=pltpu.SMEM)] + in_vmem(5),
        out_specs=tuple(in_vmem(3)),
        scratch_shapes=[pltpu.VMEM((own, 2 * width), jnp.float32)],
        compiler_params=pltpu.CompilerParams(vmem_limit_bytes=48 << 20),
        cost_estimate=takes(7),
    )(meta, x, weights, cosine, sine, gains)


def kv_back_here(meta, grad, tables):
    own, width = grad.shape
    pre, *others = tables
    return pl.pallas_call(
        kv_back_kernel,
        out_shape=(
            jax.ShapeDtypeStruct((own, width), jnp.bfloat16),
            jax.ShapeDtypeStruct((1, width), jnp.float32),
        ),
        in_specs=[pl.BlockSpec(memory_space=pltpu.SMEM)] + in_vmem(5),
        out_specs=tuple(in_vmem(2)),
        compiler_params=pltpu.CompilerParams(vmem_limit_bytes=32 << 20),
        cost_estimate=takes(1.5),
    )(meta, pre, grad, *others)


TOKEN_ROWS = 16
COMBINE_TIME = 25


def scaled(x):
    return x * lax.rsqrt(jnp.mean(x * x, axis=-1, keepdims=True) + epsilon)


def scaled_back(x, grad):
    scale = lax.rsqrt(jnp.mean(x * x, axis=-1, keepdims=True) + epsilon)
    normed = x * scale
    return scale * (grad - normed * jnp.mean(grad * normed, axis=-1, keepdims=True))


def inner(left, right):
    return jnp.sum(left * right, axis=-1, keepdims=True)


def over_rows(x):
    return jnp.sum(x, axis=0, keepdims=True)


def mode_columns(aligned, router_ref):
    return [jnp.tanh(inner(aligned, router_ref[k : k + 1, :])) for k in range(4)]


def mixed_columns(mode, coef, column):
    return sum(mode[k] * coef[k, column] for k in range(4))


def predict_kernel(coef, x_ref, gain_ref, router_ref, predicted_ref, normed_ref):
    x = [x_ref[i].astype(jnp.float32) for i in range(4)]
    mode = mode_columns(scaled(x[0]) * gain_ref[0:1, :], router_ref)
    for i in range(4):
        value = x[i]
        for j in range(4):
            value = value + mixed_columns(mode, coef, 4 * i + j) * x[j]
        predicted_ref[i] = value
        if i == 0:
            normed_ref[...] = (scaled(value) * gain_ref[1:2, :]).astype(normed_ref.dtype)


def predict_back_kernel(
    coef, x_ref, first_ref, cotangent_ref, normed_ref, extra_ref, gain_ref, router_ref, early_ref,
    out_ref, packed_ref, mode_all, table_all,
):
    step = pl.program_id(0)

    @pl.when(step == 0)
    def _():
        packed_ref[...] = early_ref[...]
        mode_all[...] = jnp.zeros_like(mode_all)
        table_all[...] = jnp.zeros_like(table_all)

    rows = pl.ds(pl.multiple_of(step * TOKEN_ROWS, TOKEN_ROWS), TOKEN_ROWS)
    x = [x_ref[i].astype(jnp.float32) for i in range(4)]
    normed_zero = scaled(x[0])
    aligned = normed_zero * gain_ref[0:1, :]
    mode = mode_columns(aligned, router_ref)
    table = [[mixed_columns(mode, coef, 4 * i + j) for j in range(4)] for i in range(4)]
    predicted = x[0] + sum(table[0][j] * x[j] for j in range(4))
    normed_grad = normed_ref[...] + extra_ref[...]
    packed_ref[1:2, :] += over_rows(normed_grad * scaled(predicted))
    grads = [first_ref[...] + scaled_back(predicted, normed_grad * gain_ref[1:2, :])]
    grads += [cotangent_ref[i].astype(jnp.float32) for i in (1, 2, 3)]
    mode_grad = [0.0] * 4
    for i in range(4):
        for j in range(4):
            table_grad = inner(grads[i], x[j])
            table_all[rows, 4 * i + j : 4 * i + j + 1] = table_grad
            for k in range(4):
                mode_grad[k] = mode_grad[k] + table_grad * coef[k, 4 * i + j]
    aligned_grad = 0.0
    for k in range(4):
        mode_all[rows, k : k + 1] = mode[k]
        logit_grad = mode_grad[k] * (1.0 - mode[k] * mode[k])
        aligned_grad = aligned_grad + logit_grad * router_ref[k : k + 1, :]
        packed_ref[8 + k : 9 + k, :] += over_rows(logit_grad * aligned)
    packed_ref[0:1, :] += over_rows(aligned_grad * normed_zero)
    for j in range(4):
        value = grads[j] + sum(table[i][j] * grads[i] for i in range(4))
        if j == 0:
            value = value + scaled_back(x[0], aligned_grad * gain_ref[0:1, :])
        out_ref[j] = value.astype(out_ref.dtype)

    @pl.when(step == pl.num_programs(0) - 1)
    def _():
        products = lax.dot_general(
            mode_all[...],
            table_all[...],
            (((0,), (0,)), ((), ())),
            precision=highest,
            preferred_element_type=jnp.float32,
        )
        packed_ref[12:16, 0:128] += products[0:4, :]


def gelu_parts(x):
    slope = (2.0 / jnp.pi) ** 0.5
    bend = jnp.tanh(slope * (x + 0.044715 * x * x * x))
    value = 0.5 * x * (1.0 + bend)
    derivative = 0.5 * (1.0 + bend) + 0.5 * x * (1.0 - bend * bend) * slope * (
        1.0 + 3.0 * 0.044715 * x * x
    )
    return value, derivative


def middle_kernel(
    coef, merged_ref, fed_ref, predicted_ref, cotangent_ref, input_ref, gain_ref, router_ref, weight_ref,
    result_ref, layer_grad_ref, fed_grad_ref, merged_grad_ref, first_grad_ref, packed_ref,
    first_ref, gate_pre_ref, projected_ref, gated_ref,
    active, wide_rows, mode_all, scale_grads,
):
    tokens, width = merged_ref.shape
    small = input_ref.shape[1]
    ranks = weight_ref.shape[1] - 2 * small
    gate_columns = pl.ds(ranks, small)
    projection_columns = pl.ds(ranks + small, small)
    packed_ref[...] = jnp.zeros_like(packed_ref)
    mode_all[...] = jnp.zeros_like(mode_all)
    scale_grads[...] = jnp.zeros_like(scale_grads)

    def scales(value):
        normed = scaled(value)
        aligned = normed * gain_ref[0:1, :]
        mode = mode_columns(aligned, router_ref)
        return normed, aligned, mode, [mixed_columns(mode, coef, 16 + i) + 1.0 for i in range(4)]

    @pl.loop(0, tokens // TOKEN_ROWS)
    def _(step):
        rows = pl.ds(pl.multiple_of(step * TOKEN_ROWS, TOKEN_ROWS), TOKEN_ROWS)
        value = merged_ref[rows, :] + scaled(fed_ref[rows, :]) * gain_ref[5:6, :]
        active[rows, :] = value
        _, _, _, scale = scales(value)
        start = predicted_ref[0, rows, :]
        corrected = start + scale[0] * (value - start)
        first_ref[rows, :] = (corrected * gain_ref[6:7, :]).astype(first_ref.dtype)

    gate_pre = jnp.dot(first_ref[...], weight_ref[:, gate_columns], preferred_element_type=jnp.float32)
    gelu, slope = gelu_parts(gate_pre)
    layer_input = input_ref[...].astype(jnp.float32)
    gated_ref[...] = (gelu * layer_input).astype(gated_ref.dtype)
    wide_rows[...] = rows_times_rows(gated_ref[...], weight_ref[:, projection_columns])

    @pl.loop(0, tokens // TOKEN_ROWS)
    def _(step):
        rows = pl.ds(pl.multiple_of(step * TOKEN_ROWS, TOKEN_ROWS), TOKEN_ROWS)
        projected = wide_rows[rows, :]
        normed = scaled(projected)
        extra = normed * gain_ref[7:8, :]
        value = active[rows, :]
        _, _, _, scale = scales(value)
        change = value - predicted_ref[0, rows, :]
        extra_grad = 0.0
        for i in range(4):
            corrected = predicted_ref[i, rows, :] + scale[i] * change
            if i:
                corrected = corrected + extra
                extra_grad = extra_grad + cotangent_ref[i, rows, :].astype(jnp.float32)
            result_ref[i, rows, :] = corrected.astype(result_ref.dtype)
        packed_ref[7:8, :] += over_rows(extra_grad * normed)
        projected_ref[rows, :] = scaled_back(projected, extra_grad * gain_ref[7:8, :]).astype(
            projected_ref.dtype
        )

    gated_grad = jnp.dot(
        projected_ref[...], weight_ref[:, projection_columns], preferred_element_type=jnp.float32
    )
    layer_grad_ref[...] = (gated_grad * gelu).astype(layer_grad_ref.dtype)
    gate_pre_ref[...] = (gated_grad * layer_input * slope).astype(gate_pre_ref.dtype)
    wide_rows[...] = rows_times_rows(gate_pre_ref[...], weight_ref[:, gate_columns])

    @pl.loop(0, tokens // TOKEN_ROWS)
    def _(step):
        rows = pl.ds(pl.multiple_of(step * TOKEN_ROWS, TOKEN_ROWS), TOKEN_ROWS)
        value = active[rows, :]
        normed, aligned, mode, scale = scales(value)
        start = predicted_ref[0, rows, :]
        change = value - start
        first_grad = wide_rows[rows, :]
        packed_ref[6:7, :] += over_rows(first_grad * (start + scale[0] * change))
        grads = [cotangent_ref[i, rows, :].astype(jnp.float32) for i in range(4)]
        grads[0] = grads[0] + first_grad * gain_ref[6:7, :]
        change_grad = sum(scale[i] * grads[i] for i in range(4))
        mode_grad = [0.0] * 4
        for i in range(4):
            scale_grad = inner(grads[i], change)
            scale_grads[rows, 16 + i : 17 + i] = scale_grad
            for k in range(4):
                mode_grad[k] = mode_grad[k] + scale_grad * coef[k, 16 + i]
        aligned_grad = 0.0
        for k in range(4):
            mode_all[rows, k : k + 1] = mode[k]
            logit_grad = mode_grad[k] * (1.0 - mode[k] * mode[k])
            aligned_grad = aligned_grad + logit_grad * router_ref[k : k + 1, :]
            packed_ref[8 + k : 9 + k, :] += over_rows(logit_grad * aligned)
        packed_ref[0:1, :] += over_rows(aligned_grad * normed)
        active_grad = change_grad + scaled_back(value, aligned_grad * gain_ref[0:1, :])
        first_grad_ref[rows, :] = grads[0] - change_grad
        merged_grad_ref[rows, :] = active_grad
        fed = fed_ref[rows, :]
        packed_ref[5:6, :] += over_rows(active_grad * scaled(fed))
        fed_grad_ref[rows, :] = scaled_back(fed, active_grad * gain_ref[5:6, :]).astype(
            fed_grad_ref.dtype
        )

    products = lax.dot_general(
        mode_all[...],
        scale_grads[...],
        (((0,), (0,)), ((), ())),
        precision=highest,
        preferred_element_type=jnp.float32,
    )
    packed_ref[12:16, 0:128] += products[0:4, :]


def combine_back_kernel(
    merged_ref, attention_ref, lifted_ref, merged_grad_ref, feed_ref, first_ref, gain_ref, early_ref,
    total_ref, active_ref, attention_grad_ref, lifted_grad_ref, packed_ref,
):
    @pl.when(pl.program_id(0) == 0)
    def _():
        packed_ref[...] = early_ref[...]

    merged, feed_grad = merged_ref[...], feed_ref[...]
    packed_ref[4:5, :] += over_rows(feed_grad * scaled(merged))
    grad = (merged_grad_ref[...] + scaled_back(merged, feed_grad * gain_ref[4:5, :])) * root_half
    active_ref[...] = grad
    total_ref[...] = first_ref[...] + grad
    for value_ref, row, out_ref in ((attention_ref, 2, attention_grad_ref), (lifted_ref, 3, lifted_grad_ref)):
        value = value_ref[...]
        packed_ref[row : row + 1, :] += over_rows(grad * scaled(value))
        out_ref[...] = scaled_back(value, grad * gain_ref[row : row + 1, :]).astype(out_ref.dtype)


def combine_back_here(merged, attention, lifted, merged_grad, feed_grad, first, gains, early):
    tokens, width = merged.shape
    rows = token_rows(width)
    full = jax.ShapeDtypeStruct((tokens, width), jnp.float32)
    low = jax.ShapeDtypeStruct((tokens, width), jnp.bfloat16)
    return pl.pallas_call(
        combine_back_kernel,
        grid=(tokens // TOKEN_ROWS,),
        out_shape=(full, full, low, low, jax.ShapeDtypeStruct(early.shape, jnp.float32)),
        in_specs=[rows] * 6 + [whole(gains.shape), whole(early.shape)],
        out_specs=(rows, rows, rows, rows, whole(early.shape)),
        compiler_params=pltpu.CompilerParams(vmem_limit_bytes=32 << 20),
        cost_estimate=takes(COMBINE_TIME),
    )(merged, attention, lifted, merged_grad, feed_grad, first, gains, early)


def assemble_kernel(meta, *refs):
    query, kv, out = refs[:5], refs[5:10], refs[10:15]
    query_ref, out_ref, key_ref, value_ref, laurel_ref, io_ref = refs[15:]
    rows = key_ref.shape[0]
    pair = query[0].shape[1]
    head = pair // CORES
    part = io_ref.shape[0] // LINE
    key_ref[...] = jnp.zeros_like(key_ref)
    value_ref[...] = jnp.zeros_like(value_ref)
    laurel_ref[...] = jnp.zeros_like(laurel_ref)

    def put(sender, query_part, kv_part, to):
        columns = pl.ds(pl.multiple_of(sender * pair, pair), pair)
        query_ref[to, columns] = query_part.astype(jnp.float32)
        group = pl.ds(pl.multiple_of(sender // (LINE // KEY_VALUE_HEADS) * head, head), head)
        key_ref[to, group] += kv_part[:, :head].astype(jnp.float32)
        value_ref[to, group] += kv_part[:, head:].astype(jnp.float32)

    def put_out(sender, value, at):
        columns = pl.ds(pl.multiple_of(sender * pair, pair), pair)
        count = min(rows - at, value.shape[0])
        to = pl.ds(at, count)
        out_ref[to, columns] = value[:count, :pair].astype(jnp.float32)
        laurel_ref[to, :] += value[:count, pair:].astype(jnp.float32)
        if value.shape[0] > count:
            start = pl.multiple_of(sender * part, part)
            io_ref[pl.ds(start, part), :] = value[count:, : io_ref.shape[1]].astype(jnp.float32)

    for step, place in ((0, 0), (-1, 1), (1, 2)):
        sender = lax.rem(meta[2] + step + LINE, LINE)
        put(sender, query[place][...], kv[place][...], pl.ds(0, rows))
        put_out(sender, out[place][...], 0)
    sender = lax.rem(meta[2] + 2, LINE)
    put(sender, query[3][...], kv[3][...], pl.ds(0, rows // 2))
    put(sender, query[4][...], kv[4][...], pl.ds(rows // 2, rows // 2))
    put_out(sender, out[3][...], 0)
    put_out(sender, out[4][...], out[3].shape[0])


def assemble_here(meta, query, kv, out):
    rows, pair = query[0].shape
    small = 2 * LAYER_INPUT_SIZE
    shapes = (
        (rows, LINE * pair),
        (rows, LINE * pair),
        (rows, KEY_VALUE_HEADS * HEAD_WIDTH),
        (rows, KEY_VALUE_HEADS * HEAD_WIDTH),
        (rows, 2 * LAUREL_RANK),
        (rows, small),
    )
    return pl.pallas_call(
        assemble_kernel,
        out_shape=tuple(jax.ShapeDtypeStruct(shape, jnp.float32) for shape in shapes),
        in_specs=[in_smem()] + in_vmem(15),
        out_specs=tuple(in_vmem(len(shapes))),
        compiler_params=pltpu.CompilerParams(vmem_limit_bytes=32 << 20),
        cost_estimate=takes(4),
    )(meta, *query, *kv, *out)


def in_smem():
    return pl.BlockSpec(memory_space=pltpu.SMEM)


def token_block(count, width):
    return pl.BlockSpec((count, TOKEN_ROWS, width), lambda i: (0, i, 0))


def token_rows(width):
    return pl.BlockSpec((TOKEN_ROWS, width), lambda i: (i, 0))


def whole(shape):
    return pl.BlockSpec(shape, lambda i: (0,) * len(shape))


def predict_here(versions, gains, router, coef):
    tokens, width = versions.shape[1:]
    return pl.pallas_call(
        predict_kernel,
        grid=(tokens // TOKEN_ROWS,),
        out_shape=(
            jax.ShapeDtypeStruct(versions.shape, jnp.float32),
            jax.ShapeDtypeStruct((tokens, width), jnp.bfloat16),
        ),
        in_specs=[in_smem(), token_block(4, width), whole(gains.shape), whole(router.shape)],
        out_specs=(token_block(4, width), token_rows(width)),
        compiler_params=pltpu.CompilerParams(vmem_limit_bytes=32 << 20),
        cost_estimate=takes(4.5),
    )(coef, versions, gains, router)


def predict_back_here(versions, first, cotangent, normed, extra, gains, router, coef, early):
    tokens, width = first.shape
    return pl.pallas_call(
        predict_back_kernel,
        grid=(tokens // TOKEN_ROWS,),
        out_shape=(
            jax.ShapeDtypeStruct(versions.shape, jnp.bfloat16),
            jax.ShapeDtypeStruct(early.shape, jnp.float32),
        ),
        in_specs=[
            in_smem(),
            token_block(4, width),
            token_rows(width),
            token_block(4, width),
            token_rows(width),
            token_rows(width),
            whole(gains.shape),
            whole(router.shape),
            whole(early.shape),
        ],
        out_specs=(token_block(4, width), whole(early.shape)),
        scratch_shapes=[
            pltpu.VMEM((tokens, 128), jnp.float32),
            pltpu.VMEM((tokens, 128), jnp.float32),
        ],
        compiler_params=pltpu.CompilerParams(vmem_limit_bytes=32 << 20),
        cost_estimate=takes(10),
    )(coef, versions, first, cotangent, normed, extra, gains, router, early)


def middle_here(merged, fed, predicted, cotangent, layer_input, gains, router, coef, weights):
    tokens, width = merged.shape
    small = layer_input.shape[1]
    narrow, wide = jnp.bfloat16, jnp.float32
    shapes = (
        (predicted.shape, narrow),
        ((tokens, small), narrow),
        ((tokens, width), narrow),
        ((tokens, width), wide),
        ((tokens, width), wide),
        ((16, width), wide),
        ((tokens, width), narrow),
        ((tokens, small), narrow),
        ((tokens, width), narrow),
        ((tokens, small), narrow),
    )
    return pl.pallas_call(
        middle_kernel,
        out_shape=tuple(jax.ShapeDtypeStruct(*shape) for shape in shapes),
        in_specs=[in_smem()] + in_vmem(8),
        out_specs=tuple(in_vmem(len(shapes))),
        scratch_shapes=[
            pltpu.VMEM((tokens, width), wide),
            pltpu.VMEM((tokens, width), wide),
            pltpu.VMEM((tokens, 128), wide),
            pltpu.VMEM((tokens, 128), wide),
        ],
        compiler_params=pltpu.CompilerParams(vmem_limit_bytes=48 << 20),
        cost_estimate=takes(17),
    )(coef, merged, fed, predicted, cotangent, layer_input, gains, router, weights)


def chip_device(
    versions,
    layer_input,
    positions,
    documents,
    cotangent,
    norm_gains,
    router_weight,
    coefficients,
    query_key_gains,
    query_weight,
    key_matrix,
    value_matrix,
    out_weight,
    laurel_weight,
    input_gate,
    input_projection,
    gate_weight,
    up_weight,
    down_weight,
):
    narrow = jnp.bfloat16
    wide = jnp.float32
    line = lax.axis_index("heads")
    piece = lax.axis_index("blk")
    core = piece % CORES
    chip = piece // CORES
    first_core = core == 0
    tokens = versions.shape[1]
    own = 8 * tokens
    width = versions.shape[2]
    rows_here = query_weight.shape[0]
    hidden = gate_weight.shape[1] // CORES
    head = CORES * line + core
    group = head // (QUERY_HEAD_COUNT // KEY_VALUE_HEADS)

    def head_columns(index, kv):
        return jnp.concatenate(
            [
                pick(query_weight, index * HEAD_WIDTH, HEAD_WIDTH),
                pick(kv, group * HEAD_WIDTH, HEAD_WIDTH),
                pick(out_weight, index * HEAD_WIDTH, HEAD_WIDTH),
            ],
            axis=1,
        )

    kv_mine = jnp.where(first_core, key_matrix, value_matrix)
    kv_theirs = jnp.where(first_core, value_matrix, key_matrix)
    head_full = all_rows(
        weight_rows(head_columns(head, kv_mine), head_columns(head ^ 1, kv_theirs), core)
    )
    small_full = lax.all_gather(
        jnp.concatenate([laurel_weight, input_gate, input_projection], axis=1),
        "blk",
        axis=0,
        tiled=True,
    )

    query_kv_full = head_full[:, : 2 * HEAD_WIDTH]
    out_full = head_full[:, 2 * HEAD_WIDTH :]
    laurel_full = small_full[:, : 2 * LAUREL_RANK]
    gain_rows = norm_gains.astype(wide)
    router_wide = router_weight.astype(wide)
    coef_wide = coefficients.astype(wide)
    head_wide = query_key_gains.astype(wide)
    predicted, normed_low = predict_here(versions, gain_rows, router_wide, coef_wide)
    *unit_weights, normed_low = together(gate_weight, up_weight, down_weight, normed_low)

    def hidden_columns(index):
        return jnp.concatenate([pick(w, index * hidden, hidden) for w in unit_weights], axis=1)

    unit_full = all_rows(weight_rows(hidden_columns(core), hidden_columns(1 - core), core))
    unit_two = unit_full[:, : 2 * hidden]
    unit_gate = unit_full[:, :hidden]
    unit_up = unit_full[:, hidden : 2 * hidden]
    unit_down = unit_full[:, 2 * hidden :]

    digits = jnp.stack([positions // 128, positions % 128], axis=1).astype(narrow)
    sent = jnp.concatenate([normed_low, jnp.pad(digits, ((0, 0), (0, 126)))], axis=1)
    gathered = gather_chip(sent)
    normed_rows = gathered[:, :width]
    digits_all = natural(gathered[:, width : width + 2].astype(wide), core, line)
    phase_position = digits_all[:, :1] * 128.0 + digits_all[:, 1:2]
    frequency = rotary_base ** (-2.0 * jnp.arange(HEAD_WIDTH // 2, dtype=wide) / HEAD_WIDTH)
    phase = phase_position * frequency[None, :]
    cosine, sine = jnp.cos(phase), jnp.sin(phase)
    first_row = chip * own
    row_docs = lax.dynamic_slice_in_dim(documents, first_row, own)
    begin_one = jnp.sum(documents < 1)
    begin_two = jnp.sum(documents < 2)
    lo = jnp.where(row_docs == 0, 0, jnp.where(row_docs == 1, begin_one, begin_two)).astype(jnp.int32)
    bounds = []
    for part in range(own // QUERY_ROWS):
        bounds.append(lo[part * QUERY_ROWS] // KEY_ROWS)
        bounds.append((lo[(part + 1) * QUERY_ROWS - 1] + KEY_ROWS - 1) // KEY_ROWS)
    meta = jnp.stack([chip, core, line, *bounds]).astype(jnp.int32)
    rotated, kv_own, heads_pre = heads_here(meta, gathered, head_full, cosine, sine, head_wide)
    tables = (heads_pre, cosine, sine, head_wide)
    mine = (kv_own, *gather_chips(kv_own))
    theirs = tuple(other_core(part) for part in mine)

    attended, lse = attend_here(meta, rotated, lo, mine, theirs)
    mixed_rows = arrival(attended.astype(narrow), core, line)
    attention_out = scatter_chip(transposed_product(mixed_rows, out_full).astype(narrow))

    down_low = forward_product(normed_low, laurel_full[:, :LAUREL_RANK]).astype(narrow)
    lifted = transposed_product(down_low, laurel_full[:, LAUREL_RANK:])
    merged, feed_in = combine(
        predicted[0], attention_out, normed_low.astype(wide), lifted, gain_rows
    )
    unit_rows = gather_chip(feed_in.astype(narrow))
    hidden_units, pull_activate = jax.vjp(
        activate, forward_product(unit_rows, unit_gate), forward_product(unit_rows, unit_up)
    )
    hidden_low = hidden_units.astype(narrow)
    fed = scatter_chip(transposed_product(hidden_low, unit_down).astype(narrow))
    def core_columns(x):
        top, bottom = x[:rows_here], x[rows_here:]
        keep = jnp.where(first_core, top, bottom)
        got = other_core(jnp.where(first_core, bottom, top))
        return jnp.where(first_core, keep, got), jnp.where(first_core, got, keep)

    def pairs(x, count):
        first, second = core_columns(x)
        parts = []
        for index in range(count):
            columns = slice(index * HEAD_WIDTH, (index + 1) * HEAD_WIDTH)
            parts += [first[:, columns], second[:, columns]]
        return jnp.concatenate(parts, axis=1)

    (
        result,
        layer_grad,
        fed_grad,
        merged_grad,
        first_grad,
        packed_middle,
        first_low,
        gate_pre_low,
        projected_low,
        gated_low,
    ) = middle_here(
        merged, fed, predicted, cotangent, layer_input, gain_rows, router_wide, coef_wide, small_full
    )

    io_sum = lax.psum_scatter(
        jnp.concatenate(
            [weight_product(first_low, gate_pre_low), weight_product(projected_low, gated_low)],
            axis=1,
        ).astype(narrow),
        "blk",
        scatter_dimension=0,
        tiled=True,
    )
    fed_rows = gather_chip(fed_grad)
    fed_rows, io_sum = together(fed_rows, io_sum)
    io_share = share_line(io_sum).astype(narrow)
    gate_grad, up_grad = pull_activate(forward_product(fed_rows, unit_down))
    down_sum = own_rows(weight_product(fed_rows, hidden_low).astype(narrow))
    two_low = jnp.concatenate([gate_grad.astype(narrow), up_grad.astype(narrow)], axis=1)
    feed_grad = scatter_chip(transposed_product(two_low, unit_two).astype(narrow))
    two_sum = own_rows(weight_product(unit_rows, two_low).astype(narrow))
    first_total, active_grad, attention_low, lifted_low, packed_combine = combine_back_here(
        merged, attention_out, lifted, merged_grad, feed_grad, first_grad, gain_rows, packed_middle
    )
    down_grad_low = forward_product(lifted_low, laurel_full[:, LAUREL_RANK:]).astype(narrow)
    laurel_part = jnp.concatenate(
        [weight_product(normed_low, down_grad_low), weight_product(lifted_low, down_low)], axis=1
    ).astype(narrow)
    laurel_part = laurel_part + other_core(laurel_part)
    attention_rows = gather_chip(attention_low)
    out_part = jnp.concatenate(
        [weight_product(attention_rows, mixed_rows).astype(narrow), laurel_part], axis=1
    )
    mixed_grad_rows = forward_product(attention_rows, out_full).astype(narrow)
    mixed_grad_rows, down_sum, two_sum, io_share, out_part = together(
        mixed_grad_rows, down_sum, two_sum, io_share, out_part
    )
    out_sum = own_rows(out_part)
    mixed_grad = natural(mixed_grad_rows, core, line)
    delta = jnp.sum(mixed_grad.astype(wide) * attended, axis=-1)
    query_rows_grad, query_gain_grad, kv_keep, kv_send = attend_back_here(
        meta, rotated, mixed_grad, lse, delta, lo, tables, mine, theirs
    )
    query_part = weight_product(normed_rows, query_rows_grad).astype(narrow)
    kv_got = other_core(kv_send)
    *kv_parts, out_sum, query_part = together(
        *[(kv_keep[m].astype(wide) + kv_got[m].astype(wide)).astype(narrow) for m in range(CHIPS)],
        out_sum,
        query_part,
    )
    laurel_here = jnp.where(
        first_core, out_sum[:rows_here, HEAD_WIDTH:], out_sum[rows_here:, HEAD_WIDTH:]
    )
    out_here = jnp.concatenate(
        [
            jnp.concatenate([pairs(out_sum, 1), laurel_here], axis=1),
            jnp.pad(io_share, ((0, 0), (0, 2 * LAUREL_RANK))),
        ],
        axis=0,
    )
    out_near = line_neighbours(out_here)
    out_far = line_far(out_here, *out_near)
    query_sum = own_rows(query_part)
    (kv_grad,) = scatter_chips(kv_parts)
    kv_grad, out_here, *out_others = together(kv_grad, out_here, *out_near, *out_far)

    kv_rows_grad, kv_gain_grad = kv_back_here(meta, kv_grad, tables)
    head_grads = jnp.concatenate([query_rows_grad, kv_rows_grad], axis=1)
    kv_part = weight_product(normed_rows, kv_rows_grad).astype(narrow)
    normed_part = transposed_product(head_grads, query_kv_full).astype(narrow)
    kv_weight_sum = own_rows(kv_part)
    normed_sum = scatter_chip(normed_part)
    normed_sum, query_sum, kv_weight_sum, down_sum, two_sum, out_here = together(
        normed_sum, query_sum, kv_weight_sum, down_sum, two_sum, out_here
    )
    query_here, kv_here = pairs(query_sum, 1), pairs(kv_weight_sum, 1)
    query_near, kv_near = line_neighbours(query_here), line_neighbours(kv_here)
    head_gain_grad = jnp.concatenate([query_gain_grad, kv_gain_grad], axis=0)
    packed_early = packed_combine + jnp.pad(
        head_gain_grad, ((12, 2), (128, width - 128 - HEAD_WIDTH))
    )
    version_grad, packed = predict_back_here(
        versions,
        first_total,
        cotangent,
        normed_sum,
        active_grad + transposed_product(down_grad_low, laurel_full[:, :LAUREL_RANK]),
        gain_rows,
        router_wide,
        coef_wide,
        packed_early,
    )
    packed = butterfly(packed)
    query_far, kv_far = line_far(query_here, *query_near), line_far(kv_here, *kv_near)
    down_first, down_second = core_columns(down_sum)
    two_first, two_second = core_columns(two_sum)

    def unit(index):
        columns = slice(index * hidden, (index + 1) * hidden)
        return jnp.concatenate([two_first[:, columns], two_second[:, columns]], axis=1).astype(wide)

    units = (unit(0), unit(1), jnp.concatenate([down_first, down_second], axis=1).astype(wide))
    packed, *far = together(packed, *query_far, *kv_far, *units)
    query_far, kv_far, units = far[:2], far[2:4], far[4:]
    query_all, out_all, key_all, value_all, laurel_all, io_all = assemble_here(
        meta,
        (query_here, *query_near, *query_far),
        (kv_here, *kv_near, *kv_far),
        (out_here, *out_others),
    )
    heads_from, heads_to = 128, 128 + HEAD_WIDTH

    return (
        result,
        version_grad,
        layer_grad,
        packed[:8],
        packed[8:12],
        packed[12:16, :20],
        packed[12:14, heads_from:heads_to],
        query_all,
        key_all,
        value_all,
        out_all,
        laurel_all,
        io_all[:, :LAYER_INPUT_SIZE],
        io_all[:, LAYER_INPUT_SIZE:],
        *units,
    )


def solution(mesh):
    by_chip = mesh.shape["heads"] == LINE and mesh.shape["blk"] == CORES * CHIPS
    on_device = chip_device if by_chip else general_device

    in_specs = (
        P(None, ("blk", "heads"), None),
        P(("blk", "heads"), None),
        P(("blk", "heads")),
        P(),
        P(None, ("blk", "heads"), None),
        P(),
        P(),
        P(),
        P(),
        P("blk", None),
        P("blk", None),
        P("blk", None),
        P("blk", None),
        P("blk", None),
        P("blk", None),
        P("blk", None),
        P("blk", "heads"),
        P("blk", "heads"),
        P("blk", "heads"),
    )
    out_specs = (
        P(None, ("blk", "heads"), None),
        P(None, ("blk", "heads"), None),
        P(("blk", "heads"), None),
        P(),
        P(),
        P(),
        P(),
        P("blk", None),
        P("blk", None),
        P("blk", None),
        P("blk", None),
        P("blk", None),
        P("blk", None),
        P("blk", None),
        P("blk", "heads"),
        P("blk", "heads"),
        P("blk", "heads"),
    )
    return jax.shard_map(
        on_device, mesh=mesh, in_specs=in_specs, out_specs=out_specs, check_vma=False
    )
```

```python
import jax
import jax.numpy as jnp
from jax import lax
from jax.experimental import pallas as pl
from jax.experimental.pallas import tpu as pltpu
from jax.sharding import PartitionSpec as P

QUERY_HEAD_COUNT = 8
KEY_VALUE_HEADS = 2
HEAD_WIDTH = 256
LAUREL_RANK = 64
LAYER_INPUT_SIZE = 256
KEYB = 2048


epsilon = 1e-06
rotary_base = 1000000.0
highest = lax.Precision.HIGHEST
root_half = 0.5**0.5


def rms_norm_apply(value_states, gain):
    return (
        value_states
        * lax.rsqrt(jnp.mean(value_states * value_states, axis=-1, keepdims=True) + epsilon)
        * gain
    )


def rotary_apply(value_states, cosine_table, sine_table):
    half = value_states.shape[-1] // 2
    turned = jnp.concatenate([-value_states[..., half:], value_states[..., :half]], axis=-1)
    return value_states * cosine_table + turned * sine_table


def angles(positions):
    frequency = rotary_base ** (-2.0 * jnp.arange(HEAD_WIDTH // 2, dtype=jnp.float32) / HEAD_WIDTH)
    phase = positions.astype(jnp.float32)[:, None] * frequency[None, :]
    phase = jnp.concatenate([phase, phase], axis=-1)[:, None, :]
    return (jnp.cos(phase), jnp.sin(phase))


def modes(value_states, gain, router):
    return jnp.tanh(jnp.dot(rms_norm_apply(value_states, gain), router.T, precision=highest))


def predict(versions, gain_rows, router, coefficients):
    token_count = versions.shape[1]
    table = jnp.dot(
        modes(versions[0], gain_rows[0], router), coefficients[:, :16], precision=highest
    ).reshape(token_count, 4, 4)
    predicted = versions + jnp.einsum("tij,jtd->itd", table, versions, precision=highest)
    return (predicted, rms_norm_apply(predicted[0], gain_rows[1]))


def prepare(query_states, key, value_states, query_key_gains, cosine_table, sine_table):
    token_count = query_states.shape[0]
    query_states = rotary_apply(
        rms_norm_apply(
            query_states.reshape(token_count, QUERY_HEAD_COUNT, HEAD_WIDTH), query_key_gains[0]
        ),
        cosine_table,
        sine_table,
    )
    key = rotary_apply(
        rms_norm_apply(key.reshape(token_count, KEY_VALUE_HEADS, HEAD_WIDTH), query_key_gains[1]),
        cosine_table,
        sine_table,
    )
    value_states = value_states.reshape(token_count, KEY_VALUE_HEADS, HEAD_WIDTH)
    value_states = value_states * lax.rsqrt(
        jnp.mean(value_states * value_states, axis=-1, keepdims=True) + epsilon
    )
    return (
        query_states,
        jnp.repeat(key, QUERY_HEAD_COUNT // KEY_VALUE_HEADS, axis=1),
        jnp.repeat(value_states, QUERY_HEAD_COUNT // KEY_VALUE_HEADS, axis=1),
    )


def combine(active, attention_out, normed, lifted, gain_rows):
    merged = (
        active
        + rms_norm_apply(attention_out, gain_rows[2])
        + normed
        + rms_norm_apply(lifted, gain_rows[3])
    ) * root_half
    return (merged, rms_norm_apply(merged, gain_rows[4]))


def activate(gate, up):
    return jax.nn.gelu(gate, approximate=True) * up


def correct(merged, fed, predicted, gain_rows, router, coefficients):
    activated = merged + rms_norm_apply(fed, gain_rows[5])
    scale = (
        jnp.dot(modes(activated, gain_rows[0], router), coefficients[:, 16:], precision=highest)
        + 1.0
    )
    corrected = predicted + scale.T[:, :, None] * (activated - predicted[0])[None]
    return (corrected, corrected[0] * gain_rows[6])


def finish(corrected, projected, gain_rows):
    extra = rms_norm_apply(projected, gain_rows[7])
    return corrected + jnp.stack([jnp.zeros_like(extra), extra, extra, extra])


def forward_product(left, right):
    return jnp.dot(left, right, preferred_element_type=jnp.float32)


def transposed_product(left, right):
    return lax.dot_general(
        left, right, (((1,), (1,)), ((), ())), preferred_element_type=jnp.float32
    )


def weight_product(left, right):
    return lax.dot_general(
        left, right, (((0,), (0,)), ((), ())), preferred_element_type=jnp.float32
    )


def general_device(
    versions,
    layer_input,
    positions,
    documents,
    cotangent,
    norm_gains,
    router_weight,
    coefficients,
    query_key_gains,
    query_weight,
    key_matrix,
    value_matrix,
    out_weight,
    laurel_weight,
    input_gate,
    input_projection,
    gate_weight,
    up_weight,
    down_weight,
):
    narrow = jnp.bfloat16
    wide = jnp.float32
    (
        query_full,
        key_full,
        value_full,
        out_full,
        laurel_full,
        gate_full,
        projection_full,
        unit_gate,
        unit_up,
        unit_down,
    ) = (
        lax.all_gather(query_weight, "blk", axis=0, tiled=True),
        lax.all_gather(key_matrix, "blk", axis=0, tiled=True),
        lax.all_gather(value_matrix, "blk", axis=0, tiled=True),
        lax.all_gather(out_weight, "blk", axis=0, tiled=True),
        lax.all_gather(laurel_weight, "blk", axis=0, tiled=True),
        lax.all_gather(input_gate, "blk", axis=0, tiled=True),
        lax.all_gather(input_projection, "blk", axis=0, tiled=True),
        lax.all_gather(gate_weight, "blk", axis=0, tiled=True),
        lax.all_gather(up_weight, "blk", axis=0, tiled=True),
        lax.all_gather(down_weight, "blk", axis=0, tiled=True),
    )
    gain_rows = norm_gains.astype(wide)
    router_wide = router_weight.astype(wide)
    coef_wide = coefficients.astype(wide)
    head_wide = query_key_gains.astype(wide)
    (predicted, normed), pull_predict = jax.vjp(
        predict, versions.astype(wide), gain_rows, router_wide, coef_wide
    )
    normed_low = normed.astype(narrow)
    cosine_table, sine_table = angles(positions)

    def prepare_here(query_states, key, value_states, gains_here):
        return prepare(query_states, key, value_states, gains_here, cosine_table, sine_table)

    (rotated, keys_rep, values_rep), pull_prepare = jax.vjp(
        prepare_here,
        forward_product(normed_low, query_full),
        forward_product(normed_low, key_full),
        forward_product(normed_low, value_full),
        head_wide,
    )
    query_heads, key_heads, value_heads = (
        lax.all_to_all(rotated.astype(narrow), "heads", split_axis=1, concat_axis=0, tiled=True),
        lax.all_to_all(keys_rep.astype(narrow), "heads", split_axis=1, concat_axis=0, tiled=True),
        lax.all_to_all(values_rep.astype(narrow), "heads", split_axis=1, concat_axis=0, tiled=True),
    )
    keys_all, values_all = (
        lax.all_gather(key_heads, "blk", axis=0, tiled=True),
        lax.all_gather(value_heads, "blk", axis=0, tiled=True),
    )
    piece, local_heads, head_size = query_heads.shape
    first_row = lax.axis_index("blk") * piece
    last_row = first_row + piece - 1
    query_rows = first_row + jnp.arange(piece, dtype=jnp.int32)
    query_docs = lax.dynamic_slice_in_dim(documents, first_row, piece)
    block_starts = jnp.arange(keys_all.shape[0] // KEYB, dtype=jnp.int32) * KEYB

    def block_scores(offset):
        key_block = lax.dynamic_slice_in_dim(keys_all, offset, KEYB)
        value_block = lax.dynamic_slice_in_dim(values_all, offset, KEYB)
        key_rows = offset + jnp.arange(KEYB, dtype=jnp.int32)
        key_docs = lax.dynamic_slice_in_dim(documents, offset, KEYB)
        allowed = (key_rows[None, :] <= query_rows[:, None]) & (
            key_docs[None, :] == query_docs[:, None]
        )
        scores = jnp.einsum("qhd,khd->hqk", query_heads, key_block, preferred_element_type=wide)
        return (key_block, value_block, allowed[None], jnp.where(allowed[None], scores, -1e30))

    def attend(state, offset):

        def visit(carry):
            top, total, summed = carry
            key_block, value_block, allowed, scores = block_scores(offset)
            new_top = jnp.maximum(top, jnp.max(scores, axis=-1))
            weights = jnp.where(allowed, jnp.exp(scores - new_top[:, :, None]), 0.0)
            decay = jnp.exp(top - new_top)
            summed = summed * decay.T[:, :, None] + jnp.einsum(
                "hqk,khd->qhd", weights.astype(narrow), value_block, preferred_element_type=wide
            )
            return (new_top, total * decay + jnp.sum(weights, axis=-1), summed)

        def keep(carry):
            return carry

        return (lax.cond(offset <= last_row, visit, keep, state), None)

    start_state = (
        jnp.full((local_heads, piece), -1e30, wide),
        jnp.zeros((local_heads, piece), wide),
        jnp.zeros((piece, local_heads, head_size), wide),
    )
    (top, total, summed), unused = lax.scan(attend, start_state, block_starts)
    log_total = top + jnp.log(total)
    attended = summed / total.T[:, :, None]
    mixed = lax.all_to_all(
        attended.astype(narrow), "heads", split_axis=0, concat_axis=1, tiled=True
    )
    mixed_low = mixed.reshape(mixed.shape[0], -1)
    attention_out = transposed_product(mixed_low, out_full)
    down_low = forward_product(normed_low, laurel_full[:, :LAUREL_RANK]).astype(narrow)
    lifted = transposed_product(down_low, laurel_full[:, LAUREL_RANK:])
    (merged, feed_in), pull_combine = jax.vjp(
        combine, predicted[0], attention_out, normed_low.astype(wide), lifted, gain_rows
    )
    feed_low = feed_in.astype(narrow)
    unit_rows = lax.all_gather(feed_low, "heads", axis=0, tiled=True)
    hidden, pull_activate = jax.vjp(
        activate, forward_product(unit_rows, unit_gate), forward_product(unit_rows, unit_up)
    )
    hidden_low = hidden.astype(narrow)
    fed = transposed_product(hidden_low, unit_down)
    fed = lax.psum_scatter(
        fed.astype(jnp.bfloat16), "heads", scatter_dimension=0, tiled=True
    ).astype(jnp.float32)
    (corrected, first), pull_correct = jax.vjp(
        correct, merged, fed, predicted, gain_rows, router_wide, coef_wide
    )
    first_low = first.astype(narrow)
    gated, pull_gate = jax.vjp(
        activate, forward_product(first_low, gate_full), layer_input.astype(wide)
    )
    gated_low = gated.astype(narrow)
    projected = transposed_product(gated_low, projection_full)
    result, pull_finish = jax.vjp(finish, corrected, projected, gain_rows)
    corrected_grad, projected_grad, gains_finish = pull_finish(cotangent.astype(wide))
    projected_low = projected_grad.astype(narrow)
    gate_pre_grad, layer_grad = pull_gate(forward_product(projected_low, projection_full))
    gate_pre_low = gate_pre_grad.astype(narrow)
    merged_grad, fed_grad, predicted_grad, gains_correct, router_correct, coef_correct = (
        pull_correct((corrected_grad, transposed_product(gate_pre_low, gate_full)))
    )
    fed_low = fed_grad.astype(narrow)
    fed_rows = lax.all_gather(fed_low, "heads", axis=0, tiled=True)
    gate_grad, up_grad = pull_activate(forward_product(fed_rows, unit_down))
    gate_low = gate_grad.astype(narrow)
    up_low = up_grad.astype(narrow)
    feed_grad = transposed_product(gate_low, unit_gate) + transposed_product(up_low, unit_up)
    feed_grad = lax.psum_scatter(
        feed_grad.astype(jnp.bfloat16), "heads", scatter_dimension=0, tiled=True
    ).astype(jnp.float32)
    active_grad, attention_grad, normed_combine, lifted_grad, gains_combine = pull_combine(
        (merged_grad, feed_grad)
    )
    lifted_low = lifted_grad.astype(narrow)
    down_grad_low = forward_product(lifted_low, laurel_full[:, LAUREL_RANK:]).astype(narrow)
    attention_low = attention_grad.astype(narrow)
    mixed_grad = forward_product(attention_low, out_full).astype(narrow).reshape(mixed.shape)
    attended_grad = lax.all_to_all(mixed_grad, "heads", split_axis=1, concat_axis=0, tiled=True)
    delta = jnp.sum(attended_grad.astype(wide) * attended, axis=-1).T

    def attend_back(query_grad, offset):

        def visit(query_grad):
            key_block, value_block, allowed, scores = block_scores(offset)
            shares = jnp.where(allowed, jnp.exp(scores - log_total[:, :, None]), 0.0)
            share_grad = jnp.einsum(
                "qhd,khd->hqk", attended_grad, value_block, preferred_element_type=wide
            )
            score_low = (shares * (share_grad - delta[:, :, None])).astype(narrow)
            query_grad = query_grad + jnp.einsum(
                "hqk,khd->qhd", score_low, key_block, preferred_element_type=wide
            )
            key_grad = jnp.einsum(
                "hqk,qhd->khd", score_low, query_heads, preferred_element_type=wide
            )
            value_grad = jnp.einsum(
                "hqk,qhd->khd", shares.astype(narrow), attended_grad, preferred_element_type=wide
            )
            return (query_grad, (key_grad, value_grad))

        def skip(query_grad):
            empty = jnp.zeros((KEYB, local_heads, head_size), wide)
            return (query_grad, (empty, empty))

        return lax.cond(offset <= last_row, visit, skip, query_grad)

    query_grad, (key_grads, value_grads) = lax.scan(
        attend_back, jnp.zeros((piece, local_heads, head_size), wide), block_starts
    )
    key_own, value_own = (
        lax.psum_scatter(
            key_grads.reshape(keys_all.shape).astype(jnp.bfloat16),
            "blk",
            scatter_dimension=0,
            tiled=True,
        ).astype(jnp.float32),
        lax.psum_scatter(
            value_grads.reshape(keys_all.shape).astype(jnp.bfloat16),
            "blk",
            scatter_dimension=0,
            tiled=True,
        ).astype(jnp.float32),
    )
    query_back, key_back, value_back = (
        lax.all_to_all(query_grad.astype(narrow), "heads", split_axis=0, concat_axis=1, tiled=True),
        lax.all_to_all(key_own.astype(narrow), "heads", split_axis=0, concat_axis=1, tiled=True),
        lax.all_to_all(value_own.astype(narrow), "heads", split_axis=0, concat_axis=1, tiled=True),
    )
    query_pre, key_pre, value_pre, head_grad = pull_prepare(
        (query_back.astype(wide), key_back.astype(wide), value_back.astype(wide))
    )
    query_low = query_pre.astype(narrow)
    key_low = key_pre.astype(narrow)
    value_low = value_pre.astype(narrow)
    normed_grad = (
        normed_combine
        + transposed_product(query_low, query_full)
        + transposed_product(key_low, key_full)
        + transposed_product(value_low, value_full)
        + transposed_product(down_grad_low, laurel_full[:, :LAUREL_RANK])
    )
    predicted_grad = predicted_grad.at[0].add(active_grad)
    version_grad, gains_predict, router_predict, coef_predict = pull_predict(
        (predicted_grad, normed_grad)
    )
    small = lax.psum(
        (
            gains_finish + gains_correct + gains_combine + gains_predict,
            router_correct + router_predict,
            coef_correct + coef_predict,
            head_grad,
        ),
        ("heads", "blk"),
    )
    normed_targets = jnp.concatenate([query_low, key_low, value_low, down_grad_low], axis=1)
    summed_grads = lax.psum_scatter(
        jnp.concatenate(
            [
                weight_product(normed_low, normed_targets),
                weight_product(attention_low, mixed_low),
                weight_product(lifted_low, down_low),
                weight_product(first_low, gate_pre_low),
                weight_product(projected_low, gated_low),
                weight_product(unit_rows, gate_low),
                weight_product(unit_rows, up_low),
                weight_product(fed_rows, hidden_low),
            ],
            axis=1,
        ).astype(jnp.bfloat16),
        "blk",
        scatter_dimension=0,
        tiled=True,
    ).astype(jnp.float32)
    bounds = [0]
    for feature_width in (
        QUERY_HEAD_COUNT * HEAD_WIDTH,
        KEY_VALUE_HEADS * HEAD_WIDTH,
        KEY_VALUE_HEADS * HEAD_WIDTH,
        LAUREL_RANK,
        QUERY_HEAD_COUNT * HEAD_WIDTH,
        LAUREL_RANK,
        LAYER_INPUT_SIZE,
        LAYER_INPUT_SIZE,
    ):
        bounds.append(bounds[-1] + feature_width)
    attention_sum = lax.psum(summed_grads[:, : bounds[8]].astype(jnp.bfloat16), "heads").astype(
        jnp.float32
    )
    parts = [attention_sum[:, bounds[place] : bounds[place + 1]] for place in range(8)]
    unit_width = (summed_grads.shape[1] - bounds[8]) // 3
    gate_part = summed_grads[:, bounds[8] : bounds[8] + unit_width]
    up_part = summed_grads[:, bounds[8] + unit_width : bounds[8] + 2 * unit_width]
    down_part = summed_grads[:, bounds[8] + 2 * unit_width :]
    return (
        result.astype(narrow),
        version_grad.astype(narrow),
        layer_grad.astype(narrow),
        small[0],
        small[1],
        small[2],
        small[3],
        parts[0],
        parts[1],
        parts[2],
        parts[4],
        jnp.concatenate([parts[3], parts[5]], axis=1),
        parts[6],
        parts[7],
        gate_part,
        up_part,
        down_part,
    )


CORES = 2
LINE = 4
CHIPS = 4


def along_heads(x, step):
    return lax.ppermute(x, "heads", [(i, (i + step) % LINE) for i in range(LINE)])


def across_blk(x, mask):
    return lax.ppermute(x, "blk", [(i, i ^ mask) for i in range(CORES * CHIPS)])


def other_core(x):
    return across_blk(x, 1)


def gather_chip(x, *others):
    half = x.shape[0] // 2
    before = along_heads(x, 1)
    after = along_heads(x, -1)
    if others:
        before, after, *others = together(before, after, *others)
    far = jnp.concatenate([along_heads(before[:half], 1), along_heads(after[half:], -1)], axis=0)
    own = [before, x, after, far]
    rows = jnp.concatenate(own + [other_core(part) for part in own], axis=0)
    return (rows, *others) if others else rows


def scatter_chip(y, *others):
    wide = jnp.float32
    if not isinstance(y, (list, tuple)):
        n = y.shape[0] // 8
        y = [y[k * n : (k + 1) * n] for k in range(8)]
    half = y[0].shape[0] // 2
    before, own, after, far = (
        y[k].astype(wide) + other_core(y[k + 4]).astype(wide) for k in range(4)
    )
    far = far.astype(jnp.bfloat16)
    first = along_heads(far[:half], 1).astype(wide)
    second = along_heads(far[half:], -1).astype(wide)
    after = jnp.concatenate([after[:half] + first, after[half:]], axis=0).astype(jnp.bfloat16)
    before = jnp.concatenate([before[:half], before[half:] + second], axis=0).astype(jnp.bfloat16)
    if others:
        after, before, *others = together(after, before, *others)
    total = own + along_heads(after, 1).astype(wide) + along_heads(before, -1).astype(wide)
    return (total, *others) if others else total


def line_neighbours(x):
    return along_heads(x, 1), along_heads(x, -1)


def line_far(x, before, after):
    half = x.shape[0] // 2
    return along_heads(before[:half], 1), along_heads(after[half:], -1)


def share_line(x):
    line = lax.axis_index("heads")
    rows = x.shape[0] // LINE
    total = lax.dynamic_slice_in_dim(x, line * rows, rows).astype(jnp.float32)
    for step in range(1, LINE):
        piece = lax.dynamic_slice_in_dim(x, ((line + step) % LINE) * rows, rows)
        total = total + along_heads(piece, step).astype(jnp.float32)
    return total


def turn(x, blocks):
    rows = x.shape[0] // LINE
    twice = jnp.concatenate([x, x], axis=0)
    return lax.dynamic_slice_in_dim(twice, blocks * rows, x.shape[0])


def natural(x, core, line):
    half = x.shape[0] // 2
    own, other = (turn(part, (1 - line) % LINE) for part in (x[:half], x[half:]))
    first = core == 0
    return jnp.concatenate([jnp.where(first, own, other), jnp.where(first, other, own)], axis=0)


def arrival(x, core, line):
    half = x.shape[0] // 2
    first = core == 0
    own, other = jnp.where(first, x[:half], x[half:]), jnp.where(first, x[half:], x[:half])
    return jnp.concatenate([turn(part, (line - 1) % LINE) for part in (own, other)], axis=0)


def gather_chips(x):
    half = x.shape[0] // 2
    side = across_blk(x, 2)
    front = across_blk(x, 4)
    return side, front, across_blk(side[:half], 4), across_blk(front[half:], 2)


def scatter_chips(parts, *others):
    wide = jnp.float32
    half = parts[0].shape[0] // 2
    own, side, front, far = parts
    low = across_blk(jnp.concatenate([side[:half], far[:half]], axis=0), 2)
    high = across_blk(jnp.concatenate([front[half:], far[half:]], axis=0), 4)
    front_sum = (front[:half].astype(wide) + low[half:].astype(wide)).astype(jnp.bfloat16)
    side_sum = (side[half:].astype(wide) + high[half:].astype(wide)).astype(jnp.bfloat16)
    front_sum, side_sum, *others = together(front_sum, side_sum, *others)
    upper = own[:half].astype(wide) + low[:half].astype(wide) + across_blk(front_sum, 4).astype(wide)
    lower = own[half:].astype(wide) + high[:half].astype(wide) + across_blk(side_sum, 2).astype(wide)
    return jnp.concatenate([upper, lower], axis=0), *others


def butterfly(x):
    for mask in (1, 2, 4):
        x = x + across_blk(x, mask)
    for mask in (1, 2):
        x = x + lax.ppermute(x, "heads", [(i, i ^ mask) for i in range(LINE)])
    return x


def chip_groups():
    return [[core + CORES * chip for chip in range(CHIPS)] for core in range(CORES)]


def weight_rows(keep, send, core):
    got = other_core(send)
    first = core == 0
    return jnp.concatenate([jnp.where(first, keep, got), jnp.where(first, got, keep)], axis=0)


def all_rows(x):
    return lax.all_gather(x, "blk", axis=0, tiled=True, axis_index_groups=chip_groups())


def own_rows(x):
    return lax.psum_scatter(
        x, "blk", scatter_dimension=0, tiled=True, axis_index_groups=chip_groups()
    )


def together(*values):
    return lax.optimization_barrier(values)


def pick(x, start, size):
    return lax.dynamic_slice_in_dim(x, start, size, axis=1)


QUERY_ROWS = 512
FORWARD_ROWS = 1024
KEY_ROWS = 512


def place_rows(target, parts, chip):
    own, side, front, near, far = parts
    size = own.shape[0]
    half = size // 2
    target[pl.ds(pl.multiple_of(chip * size, size), size), :] = own[...]
    target[pl.ds(pl.multiple_of((chip ^ 1) * size, size), size), :] = side[...]
    target[pl.ds(pl.multiple_of((chip ^ 2) * size, size), size), :] = front[...]
    base = (chip ^ 3) * size
    target[pl.ds(pl.multiple_of(base, size), half), :] = near[...]
    target[pl.ds(pl.multiple_of(base + half, half), half), :] = far[...]


def place_both(meta, mine, theirs, k_all, v_all):
    chip = meta[0]

    @pl.when(meta[1] == 0)
    def _():
        place_rows(k_all, mine, chip)
        place_rows(v_all, theirs, chip)

    @pl.when(meta[1] != 0)
    def _():
        place_rows(v_all, mine, chip)
        place_rows(k_all, theirs, chip)


def rows_times_rows(left, right):
    return lax.dot_general(
        left, right, (((1,), (1,)), ((), ())), preferred_element_type=jnp.float32
    )


def columns_times_columns(left, right):
    return lax.dot_general(
        left, right, (((0,), (0,)), ((), ())), preferred_element_type=jnp.float32
    )


def arrival_rows(meta, block, rows):
    place = lax.rem(block % LINE - meta[2] + 1 + LINE, LINE)
    place = place + jnp.where(meta[1] == block // LINE, 0, LINE)
    return pl.ds(pl.multiple_of(place * rows, rows), rows)


def head_forward(x, gain, cosine, sine):
    normed = x * lax.rsqrt(jnp.mean(x * x, axis=-1, keepdims=True) + epsilon) * gain
    half = x.shape[-1] // 2
    low, high = normed[:, :half], normed[:, half:]
    return jnp.concatenate([low * cosine - high * sine, high * cosine + low * sine], axis=-1)


def head_backward(x, grad, gain, cosine, sine):
    half = x.shape[-1] // 2
    low, high = grad[:, :half], grad[:, half:]
    turned = jnp.concatenate([low * cosine + high * sine, high * cosine - low * sine], axis=-1)
    scale = lax.rsqrt(jnp.mean(x * x, axis=-1, keepdims=True) + epsilon)
    normed = x * scale
    inner = turned * gain
    x_grad = scale * (inner - normed * jnp.mean(inner * normed, axis=-1, keepdims=True))
    return x_grad, jnp.sum(turned * normed, axis=0, keepdims=True)


def kv_tables(meta, gain, cosine, sine):
    is_key = meta[1] == 0
    return jnp.where(is_key, gain, 1.0), jnp.where(is_key, cosine, 1.0), jnp.where(is_key, sine, 0.0)


def heads_kernel(meta, x_ref, w_ref, cosine_ref, sine_ref, gain_ref, q_ref, kv_ref, pre_ref, total):
    own, width = q_ref.shape
    depth = w_ref.shape[0]
    for half in range(CORES):
        rows = pl.ds(half * (own // CORES), own // CORES)
        total[rows, :] = jnp.dot(
            x_ref[rows, :depth], w_ref[:, : 2 * width], preferred_element_type=jnp.float32
        )
    size = own // (CORES * LINE)
    for block in range(CORES * LINE):
        rows = pl.ds(block * size, size)
        pre = total[arrival_rows(meta, block, size), :]
        pre_ref[rows, :] = pre
        cosine, sine = cosine_ref[rows, :], sine_ref[rows, :]
        q_ref[rows, :] = head_forward(pre[:, :width], gain_ref[0:1, :], cosine, sine).astype(q_ref.dtype)
        kv_ref[rows, :] = head_forward(
            pre[:, width:], *kv_tables(meta, gain_ref[1:2, :], cosine, sine)
        ).astype(kv_ref.dtype)


def kv_back_kernel(meta, pre_ref, grad_ref, cosine_ref, sine_ref, gain_ref, out_ref, gain_grad_ref):
    own, width = grad_ref.shape
    size = own // (CORES * LINE)
    total = jnp.zeros((1, width), jnp.float32)
    for block in range(CORES * LINE):
        rows = pl.ds(block * size, size)
        x_grad, gain_grad = head_backward(
            pre_ref[rows, width:],
            grad_ref[rows, :],
            *kv_tables(meta, gain_ref[1:2, :], cosine_ref[rows, :], sine_ref[rows, :]),
        )
        out_ref[arrival_rows(meta, block, size), :] = x_grad.astype(out_ref.dtype)
        total = total + gain_grad
    gain_grad_ref[...] = jnp.where(meta[1] == 0, total, 0.0)


def attend_kernel(meta, q_ref, lo_ref, *refs):
    mine, theirs = refs[:5], refs[5:10]
    out_ref, lse_ref, k_all, v_all, total, summed = refs[10:]
    place_both(meta, mine, theirs, k_all, v_all)
    own = q_ref.shape[0]
    for part in range(own // FORWARD_ROWS):
        rows = pl.ds(part * FORWARD_ROWS, FORWARD_ROWS)
        first = meta[0] * own + part * FORWARD_ROWS
        total[...] = jnp.zeros_like(total)
        summed[...] = jnp.zeros_like(summed)

        def visit(block, masked, rows=rows, first=first):
            at = pl.multiple_of(block * KEY_ROWS, KEY_ROWS)
            scores = rows_times_rows(q_ref[rows, :], k_all[pl.ds(at, KEY_ROWS), :])
            weights = jnp.exp(scores)
            if masked:
                key = at + lax.broadcasted_iota(jnp.int32, weights.shape, 1)
                query = first + lax.broadcasted_iota(jnp.int32, weights.shape, 0)
                weights = jnp.where((key >= lo_ref[rows, :]) & (key <= query), weights, 0.0)
            for lane in range(0, KEY_ROWS, 128):
                total[...] += weights[:, lane : lane + 128]
            summed[...] += jnp.dot(
                weights.astype(jnp.bfloat16),
                v_all[pl.ds(at, KEY_ROWS), :],
                preferred_element_type=jnp.float32,
            )

        start, full_from = meta[3 + 2 * part], meta[4 + 2 * part]
        end = (first + FORWARD_ROWS - 1) // KEY_ROWS + 1
        full_from = jnp.minimum(full_from, end)
        full_to = jnp.maximum(jnp.minimum((first + 1) // KEY_ROWS, end), full_from)

        @pl.loop(start, full_from)
        def _(block, visit=visit):
            visit(block, True)

        @pl.loop(full_from, full_to)
        def _(block, visit=visit):
            visit(block, False)

        @pl.loop(full_to, end)
        def _(block, visit=visit):
            visit(block, True)

        denominator = jnp.sum(total[...], axis=1, keepdims=True)
        out_ref[rows, :] = summed[...] / denominator
        lse_ref[rows, :] = jnp.log(denominator)


def attend_back_kernel(
    meta, q_ref, grad_ref, lse_ref, delta_ref, lo_ref, pre_ref, cosine_ref, sine_ref, gain_ref, *refs
):
    mine, theirs = refs[:5], refs[5:10]
    out_ref, gain_grad_ref, keep_ref, send_ref, k_all, v_all, dk_sum, dv_sum, dq_ref = refs[10:]
    place_both(meta, mine, theirs, k_all, v_all)
    chip = meta[0]
    own = q_ref.shape[0]
    parts = own // QUERY_ROWS
    keep_ref[...] = jnp.zeros_like(keep_ref)
    send_ref[...] = jnp.zeros_like(send_ref)
    dq_ref[...] = jnp.zeros_like(dq_ref)
    per_chip = own // KEY_ROWS

    @pl.loop(meta[3], (chip + 1) * per_chip)
    def _(block):
        at = pl.multiple_of(block * KEY_ROWS, KEY_ROWS)
        dk_sum[...] = jnp.zeros_like(dk_sum)
        dv_sum[...] = jnp.zeros_like(dv_sum)
        for part in range(parts):
            rows = pl.ds(part * QUERY_ROWS, QUERY_ROWS)
            first = chip * own + part * QUERY_ROWS

            def visit(masked, rows=rows, first=first):
                keys = k_all[pl.ds(at, KEY_ROWS), :]
                queries = q_ref[rows, :]
                grads = grad_ref[rows, :]
                shares = jnp.exp(rows_times_rows(keys, queries) - lse_ref[:, rows])
                if masked:
                    key = at + lax.broadcasted_iota(jnp.int32, shares.shape, 0)
                    query = first + lax.broadcasted_iota(jnp.int32, shares.shape, 1)
                    shares = jnp.where((key >= lo_ref[:, rows]) & (key <= query), shares, 0.0)
                share_grad = rows_times_rows(v_all[pl.ds(at, KEY_ROWS), :], grads)
                score_grad = (shares * (share_grad - delta_ref[:, rows])).astype(jnp.bfloat16)
                dv_sum[...] += jnp.dot(
                    shares.astype(jnp.bfloat16), grads, preferred_element_type=jnp.float32
                )
                dk_sum[...] += jnp.dot(score_grad, queries, preferred_element_type=jnp.float32)
                dq_ref[rows, :] += columns_times_columns(score_grad, keys)

            start, full_from = meta[3 + 2 * part], meta[4 + 2 * part]
            full = (block >= full_from) & ((block + 1) * KEY_ROWS <= first + 1)
            needed = (block >= start) & (block * KEY_ROWS < first + QUERY_ROWS)

            @pl.when(full)
            def _(visit=visit):
                visit(False)

            @pl.when(needed & jnp.logical_not(full))
            def _(visit=visit):
                visit(True)

        place = (block // per_chip) ^ chip
        inner = pl.multiple_of((block % per_chip) * KEY_ROWS, KEY_ROWS)
        dk_low = dk_sum[...].astype(jnp.bfloat16)
        dv_low = dv_sum[...].astype(jnp.bfloat16)

        @pl.when(meta[1] == 0)
        def _():
            keep_ref[place, pl.ds(inner, KEY_ROWS), :] = dk_low
            send_ref[place, pl.ds(inner, KEY_ROWS), :] = dv_low

        @pl.when(meta[1] != 0)
        def _():
            keep_ref[place, pl.ds(inner, KEY_ROWS), :] = dv_low
            send_ref[place, pl.ds(inner, KEY_ROWS), :] = dk_low

    width = q_ref.shape[1]
    size = own // (CORES * LINE)
    total = jnp.zeros((1, width), jnp.float32)
    for block in range(CORES * LINE):
        rows = pl.ds(block * size, size)
        x_grad, gain_grad = head_backward(
            pre_ref[rows, :width],
            dq_ref[rows, :].astype(jnp.bfloat16).astype(jnp.float32),
            gain_ref[0:1, :],
            cosine_ref[rows, :],
            sine_ref[rows, :],
        )
        out_ref[arrival_rows(meta, block, size), :] = x_grad.astype(out_ref.dtype)
        total = total + gain_grad
    gain_grad_ref[...] = total


def takes(microseconds):
    return pl.CostEstimate(
        flops=int(microseconds * 1e9), bytes_accessed=int(microseconds * 3.3e6), transcendentals=0
    )


def in_vmem(count):
    return [pl.BlockSpec(memory_space=pltpu.VMEM)] * count


def attend_here(meta, q, lo, mine, theirs):
    own, width = q.shape
    row = own * CHIPS
    return pl.pallas_call(
        attend_kernel,
        out_shape=(
            jax.ShapeDtypeStruct((own, width), jnp.float32),
            jax.ShapeDtypeStruct((own, 1), jnp.float32),
        ),
        in_specs=[pl.BlockSpec(memory_space=pltpu.SMEM)] + in_vmem(12),
        out_specs=tuple(in_vmem(2)),
        scratch_shapes=[
            pltpu.VMEM((row, width), jnp.bfloat16),
            pltpu.VMEM((row, width), jnp.bfloat16),
            pltpu.VMEM((FORWARD_ROWS, 128), jnp.float32),
            pltpu.VMEM((FORWARD_ROWS, width), jnp.float32),
        ],
        compiler_params=pltpu.CompilerParams(vmem_limit_bytes=40 << 20),
        cost_estimate=takes(9),
    )(meta, q, lo.reshape(own, 1), *mine, *theirs)


def attend_back_here(meta, q, grad, lse, delta, lo, tables, mine, theirs):
    own, width = q.shape
    row = own * CHIPS
    return pl.pallas_call(
        attend_back_kernel,
        out_shape=(
            jax.ShapeDtypeStruct((own, width), jnp.bfloat16),
            jax.ShapeDtypeStruct((1, width), jnp.float32),
            jax.ShapeDtypeStruct((CHIPS, own, width), jnp.bfloat16),
            jax.ShapeDtypeStruct((CHIPS, own, width), jnp.bfloat16),
        ),
        in_specs=[pl.BlockSpec(memory_space=pltpu.SMEM)] + in_vmem(19),
        out_specs=tuple(in_vmem(4)),
        scratch_shapes=[
            pltpu.VMEM((row, width), jnp.bfloat16),
            pltpu.VMEM((row, width), jnp.bfloat16),
            pltpu.VMEM((KEY_ROWS, width), jnp.float32),
            pltpu.VMEM((KEY_ROWS, width), jnp.float32),
            pltpu.VMEM((own, width), jnp.float32),
        ],
        compiler_params=pltpu.CompilerParams(vmem_limit_bytes=48 << 20),
        cost_estimate=takes(20.5),
    )(
        meta,
        q,
        grad,
        lse.reshape(1, own),
        delta.reshape(1, own),
        lo.reshape(1, own),
        *tables,
        *mine,
        *theirs,
    )


def heads_here(meta, x, weights, cosine, sine, gains):
    own, width = x.shape[0], gains.shape[1]
    return pl.pallas_call(
        heads_kernel,
        out_shape=(
            jax.ShapeDtypeStruct((own, width), jnp.bfloat16),
            jax.ShapeDtypeStruct((own, width), jnp.bfloat16),
            jax.ShapeDtypeStruct((own, 2 * width), jnp.float32),
        ),
        in_specs=[pl.BlockSpec(memory_space=pltpu.SMEM)] + in_vmem(5),
        out_specs=tuple(in_vmem(3)),
        scratch_shapes=[pltpu.VMEM((own, 2 * width), jnp.float32)],
        compiler_params=pltpu.CompilerParams(vmem_limit_bytes=48 << 20),
        cost_estimate=takes(7),
    )(meta, x, weights, cosine, sine, gains)


def kv_back_here(meta, grad, tables):
    own, width = grad.shape
    pre, *others = tables
    return pl.pallas_call(
        kv_back_kernel,
        out_shape=(
            jax.ShapeDtypeStruct((own, width), jnp.bfloat16),
            jax.ShapeDtypeStruct((1, width), jnp.float32),
        ),
        in_specs=[pl.BlockSpec(memory_space=pltpu.SMEM)] + in_vmem(5),
        out_specs=tuple(in_vmem(2)),
        compiler_params=pltpu.CompilerParams(vmem_limit_bytes=32 << 20),
        cost_estimate=takes(1.5),
    )(meta, pre, grad, *others)


TOKEN_ROWS = 16
COMBINE_TIME = 45


def scaled(x):
    return x * lax.rsqrt(jnp.mean(x * x, axis=-1, keepdims=True) + epsilon)


def scaled_back(x, grad):
    scale = lax.rsqrt(jnp.mean(x * x, axis=-1, keepdims=True) + epsilon)
    normed = x * scale
    return scale * (grad - normed * jnp.mean(grad * normed, axis=-1, keepdims=True))


def inner(left, right):
    return jnp.sum(left * right, axis=-1, keepdims=True)


def over_rows(x):
    return jnp.sum(x, axis=0, keepdims=True)


def mode_columns(aligned, router_ref):
    return [jnp.tanh(inner(aligned, router_ref[k : k + 1, :])) for k in range(4)]


def mixed_columns(mode, coef, column):
    return sum(mode[k] * coef[k, column] for k in range(4))


def predict_kernel(coef, x_ref, gain_ref, router_ref, predicted_ref, normed_ref):
    x = [x_ref[i].astype(jnp.float32) for i in range(4)]
    mode = mode_columns(scaled(x[0]) * gain_ref[0:1, :], router_ref)
    for i in range(4):
        value = x[i]
        for j in range(4):
            value = value + mixed_columns(mode, coef, 4 * i + j) * x[j]
        predicted_ref[i] = value
        if i == 0:
            normed_ref[...] = (scaled(value) * gain_ref[1:2, :]).astype(normed_ref.dtype)


def predict_back_kernel(
    coef, x_ref, first_ref, cotangent_ref, normed_ref, extra_ref, gain_ref, router_ref, early_ref,
    out_ref, packed_ref, mode_all, table_all,
):
    step = pl.program_id(0)

    @pl.when(step == 0)
    def _():
        packed_ref[...] = early_ref[...]
        mode_all[...] = jnp.zeros_like(mode_all)
        table_all[...] = jnp.zeros_like(table_all)

    rows = pl.ds(pl.multiple_of(step * TOKEN_ROWS, TOKEN_ROWS), TOKEN_ROWS)
    x = [x_ref[i].astype(jnp.float32) for i in range(4)]
    normed_zero = scaled(x[0])
    aligned = normed_zero * gain_ref[0:1, :]
    mode = mode_columns(aligned, router_ref)
    table = [[mixed_columns(mode, coef, 4 * i + j) for j in range(4)] for i in range(4)]
    predicted = x[0] + sum(table[0][j] * x[j] for j in range(4))
    normed_grad = normed_ref[...] + extra_ref[...]
    packed_ref[1:2, :] += over_rows(normed_grad * scaled(predicted))
    grads = [first_ref[...] + scaled_back(predicted, normed_grad * gain_ref[1:2, :])]
    grads += [cotangent_ref[i].astype(jnp.float32) for i in (1, 2, 3)]
    mode_grad = [0.0] * 4
    for i in range(4):
        for j in range(4):
            table_grad = inner(grads[i], x[j])
            table_all[rows, 4 * i + j : 4 * i + j + 1] = table_grad
            for k in range(4):
                mode_grad[k] = mode_grad[k] + table_grad * coef[k, 4 * i + j]
    aligned_grad = 0.0
    for k in range(4):
        mode_all[rows, k : k + 1] = mode[k]
        logit_grad = mode_grad[k] * (1.0 - mode[k] * mode[k])
        aligned_grad = aligned_grad + logit_grad * router_ref[k : k + 1, :]
        packed_ref[8 + k : 9 + k, :] += over_rows(logit_grad * aligned)
    packed_ref[0:1, :] += over_rows(aligned_grad * normed_zero)
    for j in range(4):
        value = grads[j] + sum(table[i][j] * grads[i] for i in range(4))
        if j == 0:
            value = value + scaled_back(x[0], aligned_grad * gain_ref[0:1, :])
        out_ref[j] = value.astype(out_ref.dtype)

    @pl.when(step == pl.num_programs(0) - 1)
    def _():
        products = lax.dot_general(
            mode_all[...],
            table_all[...],
            (((0,), (0,)), ((), ())),
            precision=highest,
            preferred_element_type=jnp.float32,
        )
        packed_ref[12:16, 0:128] += products[0:4, :]


def gelu_parts(x):
    slope = (2.0 / jnp.pi) ** 0.5
    bend = jnp.tanh(slope * (x + 0.044715 * x * x * x))
    value = 0.5 * x * (1.0 + bend)
    derivative = 0.5 * (1.0 + bend) + 0.5 * x * (1.0 - bend * bend) * slope * (
        1.0 + 3.0 * 0.044715 * x * x
    )
    return value, derivative


def middle_kernel(
    coef, merged_ref, fed_ref, predicted_ref, cotangent_ref, input_ref, gain_ref, router_ref, weight_ref,
    result_ref, layer_grad_ref, fed_grad_ref, merged_grad_ref, first_grad_ref, packed_ref,
    first_ref, gate_pre_ref, projected_ref, gated_ref,
    active, wide_rows, mode_all, scale_grads,
):
    tokens, width = merged_ref.shape
    small = input_ref.shape[1]
    ranks = weight_ref.shape[1] - 2 * small
    gate_columns = pl.ds(ranks, small)
    projection_columns = pl.ds(ranks + small, small)
    packed_ref[...] = jnp.zeros_like(packed_ref)
    mode_all[...] = jnp.zeros_like(mode_all)
    scale_grads[...] = jnp.zeros_like(scale_grads)

    def scales(value):
        normed = scaled(value)
        aligned = normed * gain_ref[0:1, :]
        mode = mode_columns(aligned, router_ref)
        return normed, aligned, mode, [mixed_columns(mode, coef, 16 + i) + 1.0 for i in range(4)]

    @pl.loop(0, tokens // TOKEN_ROWS)
    def _(step):
        rows = pl.ds(pl.multiple_of(step * TOKEN_ROWS, TOKEN_ROWS), TOKEN_ROWS)
        value = merged_ref[rows, :] + scaled(fed_ref[rows, :]) * gain_ref[5:6, :]
        active[rows, :] = value
        _, _, _, scale = scales(value)
        start = predicted_ref[0, rows, :]
        corrected = start + scale[0] * (value - start)
        first_ref[rows, :] = (corrected * gain_ref[6:7, :]).astype(first_ref.dtype)

    gate_pre = jnp.dot(first_ref[...], weight_ref[:, gate_columns], preferred_element_type=jnp.float32)
    gelu, slope = gelu_parts(gate_pre)
    layer_input = input_ref[...].astype(jnp.float32)
    gated_ref[...] = (gelu * layer_input).astype(gated_ref.dtype)
    wide_rows[...] = rows_times_rows(gated_ref[...], weight_ref[:, projection_columns])

    @pl.loop(0, tokens // TOKEN_ROWS)
    def _(step):
        rows = pl.ds(pl.multiple_of(step * TOKEN_ROWS, TOKEN_ROWS), TOKEN_ROWS)
        projected = wide_rows[rows, :]
        normed = scaled(projected)
        extra = normed * gain_ref[7:8, :]
        value = active[rows, :]
        _, _, _, scale = scales(value)
        change = value - predicted_ref[0, rows, :]
        extra_grad = 0.0
        for i in range(4):
            corrected = predicted_ref[i, rows, :] + scale[i] * change
            if i:
                corrected = corrected + extra
                extra_grad = extra_grad + cotangent_ref[i, rows, :].astype(jnp.float32)
            result_ref[i, rows, :] = corrected.astype(result_ref.dtype)
        packed_ref[7:8, :] += over_rows(extra_grad * normed)
        projected_ref[rows, :] = scaled_back(projected, extra_grad * gain_ref[7:8, :]).astype(
            projected_ref.dtype
        )

    gated_grad = jnp.dot(
        projected_ref[...], weight_ref[:, projection_columns], preferred_element_type=jnp.float32
    )
    layer_grad_ref[...] = (gated_grad * gelu).astype(layer_grad_ref.dtype)
    gate_pre_ref[...] = (gated_grad * layer_input * slope).astype(gate_pre_ref.dtype)
    wide_rows[...] = rows_times_rows(gate_pre_ref[...], weight_ref[:, gate_columns])

    @pl.loop(0, tokens // TOKEN_ROWS)
    def _(step):
        rows = pl.ds(pl.multiple_of(step * TOKEN_ROWS, TOKEN_ROWS), TOKEN_ROWS)
        value = active[rows, :]
        normed, aligned, mode, scale = scales(value)
        start = predicted_ref[0, rows, :]
        change = value - start
        first_grad = wide_rows[rows, :]
        packed_ref[6:7, :] += over_rows(first_grad * (start + scale[0] * change))
        grads = [cotangent_ref[i, rows, :].astype(jnp.float32) for i in range(4)]
        grads[0] = grads[0] + first_grad * gain_ref[6:7, :]
        change_grad = sum(scale[i] * grads[i] for i in range(4))
        mode_grad = [0.0] * 4
        for i in range(4):
            scale_grad = inner(grads[i], change)
            scale_grads[rows, 16 + i : 17 + i] = scale_grad
            for k in range(4):
                mode_grad[k] = mode_grad[k] + scale_grad * coef[k, 16 + i]
        aligned_grad = 0.0
        for k in range(4):
            mode_all[rows, k : k + 1] = mode[k]
            logit_grad = mode_grad[k] * (1.0 - mode[k] * mode[k])
            aligned_grad = aligned_grad + logit_grad * router_ref[k : k + 1, :]
            packed_ref[8 + k : 9 + k, :] += over_rows(logit_grad * aligned)
        packed_ref[0:1, :] += over_rows(aligned_grad * normed)
        active_grad = change_grad + scaled_back(value, aligned_grad * gain_ref[0:1, :])
        first_grad_ref[rows, :] = grads[0] - change_grad
        merged_grad_ref[rows, :] = active_grad
        fed = fed_ref[rows, :]
        packed_ref[5:6, :] += over_rows(active_grad * scaled(fed))
        fed_grad_ref[rows, :] = scaled_back(fed, active_grad * gain_ref[5:6, :]).astype(
            fed_grad_ref.dtype
        )

    products = lax.dot_general(
        mode_all[...],
        scale_grads[...],
        (((0,), (0,)), ((), ())),
        precision=highest,
        preferred_element_type=jnp.float32,
    )
    packed_ref[12:16, 0:128] += products[0:4, :]


def combine_back_kernel(
    merged_ref, attention_ref, lifted_ref, merged_grad_ref, feed_ref, first_ref, gain_ref, early_ref,
    total_ref, active_ref, attention_grad_ref, lifted_grad_ref, packed_ref,
):
    @pl.when(pl.program_id(0) == 0)
    def _():
        packed_ref[...] = early_ref[...]

    merged, feed_grad = merged_ref[...], feed_ref[...]
    packed_ref[4:5, :] += over_rows(feed_grad * scaled(merged))
    grad = (merged_grad_ref[...] + scaled_back(merged, feed_grad * gain_ref[4:5, :])) * root_half
    active_ref[...] = grad
    total_ref[...] = first_ref[...] + grad
    for value_ref, row, out_ref in ((attention_ref, 2, attention_grad_ref), (lifted_ref, 3, lifted_grad_ref)):
        value = value_ref[...]
        packed_ref[row : row + 1, :] += over_rows(grad * scaled(value))
        out_ref[...] = scaled_back(value, grad * gain_ref[row : row + 1, :]).astype(out_ref.dtype)


def combine_back_here(merged, attention, lifted, merged_grad, feed_grad, first, gains, early):
    tokens, width = merged.shape
    rows = token_rows(width)
    full = jax.ShapeDtypeStruct((tokens, width), jnp.float32)
    low = jax.ShapeDtypeStruct((tokens, width), jnp.bfloat16)
    return pl.pallas_call(
        combine_back_kernel,
        grid=(tokens // TOKEN_ROWS,),
        out_shape=(full, full, low, low, jax.ShapeDtypeStruct(early.shape, jnp.float32)),
        in_specs=[rows] * 6 + [whole(gains.shape), whole(early.shape)],
        out_specs=(rows, rows, rows, rows, whole(early.shape)),
        compiler_params=pltpu.CompilerParams(vmem_limit_bytes=32 << 20),
        cost_estimate=takes(COMBINE_TIME),
    )(merged, attention, lifted, merged_grad, feed_grad, first, gains, early)


HIDDEN_TILE = 256
WIDTH_TILE = 512


def gelu_of(x):
    return gelu_parts(x)[0]


def put_pieces(refs, value):
    rows = refs[0].shape[0]
    for place, ref in enumerate(refs):
        ref[...] = value[place * rows : (place + 1) * rows].astype(ref.dtype)


def unit_kernel(x_ref, gate_w_ref, up_w_ref, down_w_ref, gate_ref, up_ref, hidden_ref, *refs):
    *fed_refs, kept = refs
    step = pl.program_id(0)
    tiles = kept.shape[0]
    own = x_ref.shape[0]
    half = own // CORES

    @pl.when(step < tiles)
    def _():
        for part in range(CORES):
            rows = pl.ds(part * half, half)
            x = x_ref[rows, :]
            gate = jnp.dot(x, gate_w_ref[...], preferred_element_type=jnp.float32)
            up = jnp.dot(x, up_w_ref[...], preferred_element_type=jnp.float32)
            hidden = (gelu_of(gate) * up).astype(hidden_ref.dtype)
            gate_ref[rows, :] = gate.astype(gate_ref.dtype)
            up_ref[rows, :] = up.astype(up_ref.dtype)
            hidden_ref[rows, :] = hidden
            kept[step, rows, :] = hidden

    @pl.when(step >= tiles)
    def _():
        hidden = jnp.concatenate([kept[tile] for tile in range(tiles)], axis=1)
        put_pieces(fed_refs, rows_times_rows(hidden, down_w_ref[...]))


def unit_back_kernel(
    grad_ref, gate_ref, up_ref, down_w_ref, two_w_ref, gate_grad_ref, up_grad_ref, *refs
):
    *feed_refs, kept = refs
    step = pl.program_id(0)
    tiles = kept.shape[0] // 2
    own = grad_ref.shape[0]
    half = own // CORES

    @pl.when(step < tiles)
    def _():
        for part in range(CORES):
            rows = pl.ds(part * half, half)
            grad = jnp.dot(grad_ref[rows, :], down_w_ref[...], preferred_element_type=jnp.float32)
            gelu, slope = gelu_parts(gate_ref[rows, :].astype(jnp.float32))
            gate_grad = (grad * up_ref[rows, :].astype(jnp.float32) * slope).astype(gate_grad_ref.dtype)
            up_grad = (grad * gelu).astype(up_grad_ref.dtype)
            gate_grad_ref[rows, :] = gate_grad
            up_grad_ref[rows, :] = up_grad
            kept[step, rows, :] = gate_grad
            kept[tiles + step, rows, :] = up_grad

    @pl.when(step >= tiles)
    def _():
        both = jnp.concatenate([kept[tile] for tile in range(2 * tiles)], axis=1)
        put_pieces(feed_refs, rows_times_rows(both, two_w_ref[...]))


def unit_here(x, weights):
    own, width = x.shape
    hidden = weights.shape[1] // 3
    tiles, sums = hidden // HIDDEN_TILE, width // WIDTH_TILE

    def tile(first):
        return pl.BlockSpec((width, HIDDEN_TILE), lambda i: (0, first * tiles + jnp.minimum(i, tiles - 1)))

    saved = pl.BlockSpec((own, HIDDEN_TILE), lambda i: (0, jnp.minimum(i, tiles - 1)))
    return pl.pallas_call(
        unit_kernel,
        grid=(tiles + sums,),
        out_shape=tuple(
            jax.ShapeDtypeStruct(shape, jnp.bfloat16)
            for shape in [(own, hidden)] * 3 + [(own // 8, width)] * 8
        ),
        in_specs=[
            whole(x.shape),
            tile(0),
            tile(1),
            pl.BlockSpec((WIDTH_TILE, hidden), lambda i: (jnp.maximum(i - tiles, 0), 2)),
        ],
        out_specs=(
            *[saved] * 3,
            *[pl.BlockSpec((own // 8, WIDTH_TILE), lambda i: (0, jnp.maximum(i - tiles, 0)))] * 8,
        ),
        scratch_shapes=[pltpu.VMEM((tiles, own, HIDDEN_TILE), jnp.bfloat16)],
        compiler_params=pltpu.CompilerParams(vmem_limit_bytes=48 << 20),
        cost_estimate=takes(18),
    )(x, weights, weights, weights)


def unit_back_here(grad, gate, up, weights):
    own, width = grad.shape
    hidden = gate.shape[1]
    tiles, sums = hidden // HIDDEN_TILE, width // WIDTH_TILE
    saved = pl.BlockSpec((own, HIDDEN_TILE), lambda i: (0, jnp.minimum(i, tiles - 1)))
    return pl.pallas_call(
        unit_back_kernel,
        grid=(tiles + sums,),
        out_shape=tuple(
            jax.ShapeDtypeStruct(shape, jnp.bfloat16)
            for shape in [(own, hidden)] * 2 + [(own // 8, width)] * 8
        ),
        in_specs=[
            whole(grad.shape),
            saved,
            saved,
            pl.BlockSpec((width, HIDDEN_TILE), lambda i: (0, 2 * tiles + jnp.minimum(i, tiles - 1))),
            pl.BlockSpec((WIDTH_TILE, 2 * hidden), lambda i: (jnp.maximum(i - tiles, 0), 0)),
        ],
        out_specs=(
            *[saved] * 2,
            *[pl.BlockSpec((own // 8, WIDTH_TILE), lambda i: (0, jnp.maximum(i - tiles, 0)))] * 8,
        ),
        scratch_shapes=[pltpu.VMEM((2 * tiles, own, HIDDEN_TILE), jnp.bfloat16)],
        compiler_params=pltpu.CompilerParams(vmem_limit_bytes=56 << 20),
        cost_estimate=takes(18),
    )(grad, gate, up, weights, weights)


def assemble_kernel(meta, *refs):
    query, kv, out = refs[:5], refs[5:10], refs[10:15]
    query_ref, out_ref, key_ref, value_ref, laurel_ref, io_ref = refs[15:]
    rows = key_ref.shape[0]
    pair = query[0].shape[1]
    head = pair // CORES
    part = io_ref.shape[0] // LINE
    key_ref[...] = jnp.zeros_like(key_ref)
    value_ref[...] = jnp.zeros_like(value_ref)
    laurel_ref[...] = jnp.zeros_like(laurel_ref)

    def put(sender, query_part, kv_part, to):
        columns = pl.ds(pl.multiple_of(sender * pair, pair), pair)
        query_ref[to, columns] = query_part.astype(jnp.float32)
        group = pl.ds(pl.multiple_of(sender // (LINE // KEY_VALUE_HEADS) * head, head), head)
        key_ref[to, group] += kv_part[:, :head].astype(jnp.float32)
        value_ref[to, group] += kv_part[:, head:].astype(jnp.float32)

    def put_out(sender, value, at):
        columns = pl.ds(pl.multiple_of(sender * pair, pair), pair)
        count = min(rows - at, value.shape[0])
        to = pl.ds(at, count)
        out_ref[to, columns] = value[:count, :pair].astype(jnp.float32)
        laurel_ref[to, :] += value[:count, pair:].astype(jnp.float32)
        if value.shape[0] > count:
            start = pl.multiple_of(sender * part, part)
            io_ref[pl.ds(start, part), :] = value[count:, : io_ref.shape[1]].astype(jnp.float32)

    for step, place in ((0, 0), (-1, 1), (1, 2)):
        sender = lax.rem(meta[2] + step + LINE, LINE)
        put(sender, query[place][...], kv[place][...], pl.ds(0, rows))
        put_out(sender, out[place][...], 0)
    sender = lax.rem(meta[2] + 2, LINE)
    put(sender, query[3][...], kv[3][...], pl.ds(0, rows // 2))
    put(sender, query[4][...], kv[4][...], pl.ds(rows // 2, rows // 2))
    put_out(sender, out[3][...], 0)
    put_out(sender, out[4][...], out[3].shape[0])


def assemble_here(meta, query, kv, out):
    rows, pair = query[0].shape
    small = 2 * LAYER_INPUT_SIZE
    shapes = (
        (rows, LINE * pair),
        (rows, LINE * pair),
        (rows, KEY_VALUE_HEADS * HEAD_WIDTH),
        (rows, KEY_VALUE_HEADS * HEAD_WIDTH),
        (rows, 2 * LAUREL_RANK),
        (rows, small),
    )
    return pl.pallas_call(
        assemble_kernel,
        out_shape=tuple(jax.ShapeDtypeStruct(shape, jnp.float32) for shape in shapes),
        in_specs=[in_smem()] + in_vmem(15),
        out_specs=tuple(in_vmem(len(shapes))),
        compiler_params=pltpu.CompilerParams(vmem_limit_bytes=32 << 20),
        cost_estimate=takes(4),
    )(meta, *query, *kv, *out)


def in_smem():
    return pl.BlockSpec(memory_space=pltpu.SMEM)


def token_block(count, width):
    return pl.BlockSpec((count, TOKEN_ROWS, width), lambda i: (0, i, 0))


def token_rows(width):
    return pl.BlockSpec((TOKEN_ROWS, width), lambda i: (i, 0))


def whole(shape):
    return pl.BlockSpec(shape, lambda i: (0,) * len(shape))


def predict_here(versions, gains, router, coef):
    tokens, width = versions.shape[1:]
    return pl.pallas_call(
        predict_kernel,
        grid=(tokens // TOKEN_ROWS,),
        out_shape=(
            jax.ShapeDtypeStruct(versions.shape, jnp.float32),
            jax.ShapeDtypeStruct((tokens, width), jnp.bfloat16),
        ),
        in_specs=[in_smem(), token_block(4, width), whole(gains.shape), whole(router.shape)],
        out_specs=(token_block(4, width), token_rows(width)),
        compiler_params=pltpu.CompilerParams(vmem_limit_bytes=32 << 20),
        cost_estimate=takes(4.5),
    )(coef, versions, gains, router)


def predict_back_here(versions, first, cotangent, normed, extra, gains, router, coef, early):
    tokens, width = first.shape
    return pl.pallas_call(
        predict_back_kernel,
        grid=(tokens // TOKEN_ROWS,),
        out_shape=(
            jax.ShapeDtypeStruct(versions.shape, jnp.bfloat16),
            jax.ShapeDtypeStruct(early.shape, jnp.float32),
        ),
        in_specs=[
            in_smem(),
            token_block(4, width),
            token_rows(width),
            token_block(4, width),
            token_rows(width),
            token_rows(width),
            whole(gains.shape),
            whole(router.shape),
            whole(early.shape),
        ],
        out_specs=(token_block(4, width), whole(early.shape)),
        scratch_shapes=[
            pltpu.VMEM((tokens, 128), jnp.float32),
            pltpu.VMEM((tokens, 128), jnp.float32),
        ],
        compiler_params=pltpu.CompilerParams(vmem_limit_bytes=32 << 20),
        cost_estimate=takes(10),
    )(coef, versions, first, cotangent, normed, extra, gains, router, early)


def middle_here(merged, fed, predicted, cotangent, layer_input, gains, router, coef, weights):
    tokens, width = merged.shape
    small = layer_input.shape[1]
    narrow, wide = jnp.bfloat16, jnp.float32
    shapes = (
        (predicted.shape, narrow),
        ((tokens, small), narrow),
        ((tokens, width), narrow),
        ((tokens, width), wide),
        ((tokens, width), wide),
        ((16, width), wide),
        ((tokens, width), narrow),
        ((tokens, small), narrow),
        ((tokens, width), narrow),
        ((tokens, small), narrow),
    )
    return pl.pallas_call(
        middle_kernel,
        out_shape=tuple(jax.ShapeDtypeStruct(*shape) for shape in shapes),
        in_specs=[in_smem()] + in_vmem(8),
        out_specs=tuple(in_vmem(len(shapes))),
        scratch_shapes=[
            pltpu.VMEM((tokens, width), wide),
            pltpu.VMEM((tokens, width), wide),
            pltpu.VMEM((tokens, 128), wide),
            pltpu.VMEM((tokens, 128), wide),
        ],
        compiler_params=pltpu.CompilerParams(vmem_limit_bytes=48 << 20),
        cost_estimate=takes(17),
    )(coef, merged, fed, predicted, cotangent, layer_input, gains, router, weights)


def chip_device(
    versions,
    layer_input,
    positions,
    documents,
    cotangent,
    norm_gains,
    router_weight,
    coefficients,
    query_key_gains,
    query_weight,
    key_matrix,
    value_matrix,
    out_weight,
    laurel_weight,
    input_gate,
    input_projection,
    gate_weight,
    up_weight,
    down_weight,
):
    narrow = jnp.bfloat16
    wide = jnp.float32
    line = lax.axis_index("heads")
    piece = lax.axis_index("blk")
    core = piece % CORES
    chip = piece // CORES
    first_core = core == 0
    tokens = versions.shape[1]
    own = 8 * tokens
    width = versions.shape[2]
    rows_here = query_weight.shape[0]
    hidden = gate_weight.shape[1] // CORES
    head = CORES * line + core
    group = head // (QUERY_HEAD_COUNT // KEY_VALUE_HEADS)

    def head_columns(index, kv):
        return jnp.concatenate(
            [
                pick(query_weight, index * HEAD_WIDTH, HEAD_WIDTH),
                pick(kv, group * HEAD_WIDTH, HEAD_WIDTH),
                pick(out_weight, index * HEAD_WIDTH, HEAD_WIDTH),
            ],
            axis=1,
        )

    kv_mine = jnp.where(first_core, key_matrix, value_matrix)
    kv_theirs = jnp.where(first_core, value_matrix, key_matrix)
    head_full = all_rows(
        weight_rows(head_columns(head, kv_mine), head_columns(head ^ 1, kv_theirs), core)
    )
    small_full = lax.all_gather(
        jnp.concatenate([laurel_weight, input_gate, input_projection], axis=1),
        "blk",
        axis=0,
        tiled=True,
    )

    query_kv_full = head_full[:, : 2 * HEAD_WIDTH]
    out_full = head_full[:, 2 * HEAD_WIDTH :]
    laurel_full = small_full[:, : 2 * LAUREL_RANK]
    gain_rows = norm_gains.astype(wide)
    router_wide = router_weight.astype(wide)
    coef_wide = coefficients.astype(wide)
    head_wide = query_key_gains.astype(wide)
    predicted, normed_low = predict_here(versions, gain_rows, router_wide, coef_wide)
    *unit_weights, normed_low = together(gate_weight, up_weight, down_weight, normed_low)

    def hidden_columns(index):
        return jnp.concatenate([pick(w, index * hidden, hidden) for w in unit_weights], axis=1)

    unit_full = all_rows(weight_rows(hidden_columns(core), hidden_columns(1 - core), core))

    digits = jnp.stack([positions // 128, positions % 128], axis=1).astype(narrow)
    sent = jnp.concatenate([normed_low, jnp.pad(digits, ((0, 0), (0, 126)))], axis=1)
    gathered = gather_chip(sent)
    normed_rows = gathered[:, :width]
    digits_all = natural(gathered[:, width : width + 2].astype(wide), core, line)
    phase_position = digits_all[:, :1] * 128.0 + digits_all[:, 1:2]
    frequency = rotary_base ** (-2.0 * jnp.arange(HEAD_WIDTH // 2, dtype=wide) / HEAD_WIDTH)
    phase = phase_position * frequency[None, :]
    cosine, sine = jnp.cos(phase), jnp.sin(phase)
    first_row = chip * own
    row_docs = lax.dynamic_slice_in_dim(documents, first_row, own)
    begin_one = jnp.sum(documents < 1)
    begin_two = jnp.sum(documents < 2)
    lo = jnp.where(row_docs == 0, 0, jnp.where(row_docs == 1, begin_one, begin_two)).astype(jnp.int32)

    def bounds(rows):
        found = []
        for start in range(0, own, rows):
            found.append(lo[start] // KEY_ROWS)
            found.append((lo[start + rows - 1] + KEY_ROWS - 1) // KEY_ROWS)
        return jnp.stack([chip, core, line, *found]).astype(jnp.int32)

    meta = bounds(QUERY_ROWS)
    rotated, kv_own, heads_pre = heads_here(meta, gathered, head_full, cosine, sine, head_wide)
    tables = (heads_pre, cosine, sine, head_wide)
    mine = (kv_own, *gather_chips(kv_own))
    theirs = tuple(other_core(part) for part in mine)

    attended, lse = attend_here(bounds(FORWARD_ROWS), rotated, lo, mine, theirs)
    mixed_rows = arrival(attended.astype(narrow), core, line)
    attention_out = scatter_chip(transposed_product(mixed_rows, out_full).astype(narrow))

    down_low = forward_product(normed_low, laurel_full[:, :LAUREL_RANK]).astype(narrow)
    lifted = transposed_product(down_low, laurel_full[:, LAUREL_RANK:])
    merged, feed_in = combine(
        predicted[0], attention_out, normed_low.astype(wide), lifted, gain_rows
    )
    unit_rows = gather_chip(feed_in.astype(narrow))
    gate_low, up_low, hidden_low, *fed_parts = unit_here(unit_rows, unit_full)
    fed = scatter_chip(fed_parts)
    def core_columns(x):
        top, bottom = x[:rows_here], x[rows_here:]
        keep = jnp.where(first_core, top, bottom)
        got = other_core(jnp.where(first_core, bottom, top))
        return jnp.where(first_core, keep, got), jnp.where(first_core, got, keep)

    def pairs(x, count):
        first, second = core_columns(x)
        parts = []
        for index in range(count):
            columns = slice(index * HEAD_WIDTH, (index + 1) * HEAD_WIDTH)
            parts += [first[:, columns], second[:, columns]]
        return jnp.concatenate(parts, axis=1)

    (
        result,
        layer_grad,
        fed_grad,
        merged_grad,
        first_grad,
        packed_middle,
        first_low,
        gate_pre_low,
        projected_low,
        gated_low,
    ) = middle_here(
        merged, fed, predicted, cotangent, layer_input, gain_rows, router_wide, coef_wide, small_full
    )

    io_sum = lax.psum_scatter(
        jnp.concatenate(
            [weight_product(first_low, gate_pre_low), weight_product(projected_low, gated_low)],
            axis=1,
        ).astype(narrow),
        "blk",
        scatter_dimension=0,
        tiled=True,
    )
    fed_rows = gather_chip(fed_grad)
    fed_rows, io_sum = together(fed_rows, io_sum)
    io_share = share_line(io_sum).astype(narrow)
    gate_grad, up_grad, *feed_parts = unit_back_here(fed_rows, gate_low, up_low, unit_full)
    feed_grad = scatter_chip(feed_parts)
    down_sum = own_rows(weight_product(fed_rows, hidden_low).astype(narrow))
    two_sum = own_rows(
        weight_product(unit_rows, jnp.concatenate([gate_grad, up_grad], axis=1)).astype(narrow)
    )
    feed_grad, down_sum = together(feed_grad, down_sum)
    first_total, active_grad, attention_low, lifted_low, packed_combine = combine_back_here(
        merged, attention_out, lifted, merged_grad, feed_grad, first_grad, gain_rows, packed_middle
    )
    down_grad_low = forward_product(lifted_low, laurel_full[:, LAUREL_RANK:]).astype(narrow)
    laurel_part = jnp.concatenate(
        [weight_product(normed_low, down_grad_low), weight_product(lifted_low, down_low)], axis=1
    ).astype(narrow)
    laurel_part = laurel_part + other_core(laurel_part)
    attention_rows = gather_chip(attention_low)
    out_part = jnp.concatenate(
        [weight_product(attention_rows, mixed_rows).astype(narrow), laurel_part], axis=1
    )
    mixed_grad_rows = forward_product(attention_rows, out_full).astype(narrow)
    mixed_grad_rows, two_sum, io_share, out_part = together(
        mixed_grad_rows, two_sum, io_share, out_part
    )
    out_sum = own_rows(out_part)
    mixed_grad = natural(mixed_grad_rows, core, line)
    delta = jnp.sum(mixed_grad.astype(wide) * attended, axis=-1)
    query_rows_grad, query_gain_grad, kv_keep, kv_send = attend_back_here(
        meta, rotated, mixed_grad, lse, delta, lo, tables, mine, theirs
    )
    query_part = weight_product(normed_rows, query_rows_grad).astype(narrow)
    kv_got = other_core(kv_send)
    *kv_parts, out_sum, query_part = together(
        *[(kv_keep[m].astype(wide) + kv_got[m].astype(wide)).astype(narrow) for m in range(CHIPS)],
        out_sum,
        query_part,
    )
    laurel_here = jnp.where(
        first_core, out_sum[:rows_here, HEAD_WIDTH:], out_sum[rows_here:, HEAD_WIDTH:]
    )
    out_here = jnp.concatenate(
        [
            jnp.concatenate([pairs(out_sum, 1), laurel_here], axis=1),
            jnp.pad(io_share, ((0, 0), (0, 2 * LAUREL_RANK))),
        ],
        axis=0,
    )
    out_near = line_neighbours(out_here)
    out_far = line_far(out_here, *out_near)
    query_sum = own_rows(query_part)
    (kv_grad,) = scatter_chips(kv_parts)
    kv_grad, out_here, *out_others = together(kv_grad, out_here, *out_near, *out_far)

    kv_rows_grad, kv_gain_grad = kv_back_here(meta, kv_grad, tables)
    head_grads = jnp.concatenate([query_rows_grad, kv_rows_grad], axis=1)
    kv_part = weight_product(normed_rows, kv_rows_grad).astype(narrow)
    normed_part = transposed_product(head_grads, query_kv_full).astype(narrow)
    kv_weight_sum = own_rows(kv_part)
    normed_sum = scatter_chip(normed_part)
    normed_sum, query_sum, kv_weight_sum, down_sum, two_sum, out_here = together(
        normed_sum, query_sum, kv_weight_sum, down_sum, two_sum, out_here
    )
    query_here, kv_here = pairs(query_sum, 1), pairs(kv_weight_sum, 1)
    query_near, kv_near = line_neighbours(query_here), line_neighbours(kv_here)
    head_gain_grad = jnp.concatenate([query_gain_grad, kv_gain_grad], axis=0)
    packed_early = packed_combine + jnp.pad(
        head_gain_grad, ((12, 2), (128, width - 128 - HEAD_WIDTH))
    )
    version_grad, packed = predict_back_here(
        versions,
        first_total,
        cotangent,
        normed_sum,
        active_grad + transposed_product(down_grad_low, laurel_full[:, :LAUREL_RANK]),
        gain_rows,
        router_wide,
        coef_wide,
        packed_early,
    )
    packed, *query_near = together(packed, *query_near)
    packed = butterfly(packed)
    query_far, kv_far = line_far(query_here, *query_near), line_far(kv_here, *kv_near)
    down_first, down_second = core_columns(down_sum)
    two_first, two_second = core_columns(two_sum)

    def unit(index):
        columns = slice(index * hidden, (index + 1) * hidden)
        return jnp.concatenate([two_first[:, columns], two_second[:, columns]], axis=1).astype(wide)

    units = (unit(0), unit(1), jnp.concatenate([down_first, down_second], axis=1).astype(wide))
    packed, *far = together(packed, *query_far, *kv_far, *units)
    query_far, kv_far, units = far[:2], far[2:4], far[4:]
    query_all, out_all, key_all, value_all, laurel_all, io_all = assemble_here(
        meta,
        (query_here, *query_near, *query_far),
        (kv_here, *kv_near, *kv_far),
        (out_here, *out_others),
    )
    heads_from, heads_to = 128, 128 + HEAD_WIDTH

    return (
        result,
        version_grad,
        layer_grad,
        packed[:8],
        packed[8:12],
        packed[12:16, :20],
        packed[12:14, heads_from:heads_to],
        query_all,
        key_all,
        value_all,
        out_all,
        laurel_all,
        io_all[:, :LAYER_INPUT_SIZE],
        io_all[:, LAYER_INPUT_SIZE:],
        *units,
    )


def solution(mesh):
    by_chip = mesh.shape["heads"] == LINE and mesh.shape["blk"] == CORES * CHIPS
    on_device = chip_device if by_chip else general_device

    in_specs = (
        P(None, ("blk", "heads"), None),
        P(("blk", "heads"), None),
        P(("blk", "heads")),
        P(),
        P(None, ("blk", "heads"), None),
        P(),
        P(),
        P(),
        P(),
        P("blk", None),
        P("blk", None),
        P("blk", None),
        P("blk", None),
        P("blk", None),
        P("blk", None),
        P("blk", None),
        P("blk", "heads"),
        P("blk", "heads"),
        P("blk", "heads"),
    )
    out_specs = (
        P(None, ("blk", "heads"), None),
        P(None, ("blk", "heads"), None),
        P(("blk", "heads"), None),
        P(),
        P(),
        P(),
        P(),
        P("blk", None),
        P("blk", None),
        P("blk", None),
        P("blk", None),
        P("blk", None),
        P("blk", None),
        P("blk", None),
        P("blk", "heads"),
        P("blk", "heads"),
        P("blk", "heads"),
    )
    return jax.shard_map(
        on_device, mesh=mesh, in_specs=in_specs, out_specs=out_specs, check_vma=False
    )
```

```python
import jax
import jax.numpy as jnp
from jax import lax
from jax.experimental import pallas as pl
from jax.experimental.pallas import tpu as pltpu
from jax.sharding import PartitionSpec as P

QUERY_HEAD_COUNT = 8
KEY_VALUE_HEADS = 2
HEAD_WIDTH = 256
LAUREL_RANK = 64
LAYER_INPUT_SIZE = 256
KEYB = 2048


epsilon = 1e-06
rotary_base = 1000000.0
highest = lax.Precision.HIGHEST
root_half = 0.5**0.5


def rms_norm_apply(value_states, gain):
    return (
        value_states
        * lax.rsqrt(jnp.mean(value_states * value_states, axis=-1, keepdims=True) + epsilon)
        * gain
    )


def rotary_apply(value_states, cosine_table, sine_table):
    half = value_states.shape[-1] // 2
    turned = jnp.concatenate([-value_states[..., half:], value_states[..., :half]], axis=-1)
    return value_states * cosine_table + turned * sine_table


def angles(positions):
    frequency = rotary_base ** (-2.0 * jnp.arange(HEAD_WIDTH // 2, dtype=jnp.float32) / HEAD_WIDTH)
    phase = positions.astype(jnp.float32)[:, None] * frequency[None, :]
    phase = jnp.concatenate([phase, phase], axis=-1)[:, None, :]
    return (jnp.cos(phase), jnp.sin(phase))


def modes(value_states, gain, router):
    return jnp.tanh(jnp.dot(rms_norm_apply(value_states, gain), router.T, precision=highest))


def predict(versions, gain_rows, router, coefficients):
    token_count = versions.shape[1]
    table = jnp.dot(
        modes(versions[0], gain_rows[0], router), coefficients[:, :16], precision=highest
    ).reshape(token_count, 4, 4)
    predicted = versions + jnp.einsum("tij,jtd->itd", table, versions, precision=highest)
    return (predicted, rms_norm_apply(predicted[0], gain_rows[1]))


def prepare(query_states, key, value_states, query_key_gains, cosine_table, sine_table):
    token_count = query_states.shape[0]
    query_states = rotary_apply(
        rms_norm_apply(
            query_states.reshape(token_count, QUERY_HEAD_COUNT, HEAD_WIDTH), query_key_gains[0]
        ),
        cosine_table,
        sine_table,
    )
    key = rotary_apply(
        rms_norm_apply(key.reshape(token_count, KEY_VALUE_HEADS, HEAD_WIDTH), query_key_gains[1]),
        cosine_table,
        sine_table,
    )
    value_states = value_states.reshape(token_count, KEY_VALUE_HEADS, HEAD_WIDTH)
    value_states = value_states * lax.rsqrt(
        jnp.mean(value_states * value_states, axis=-1, keepdims=True) + epsilon
    )
    return (
        query_states,
        jnp.repeat(key, QUERY_HEAD_COUNT // KEY_VALUE_HEADS, axis=1),
        jnp.repeat(value_states, QUERY_HEAD_COUNT // KEY_VALUE_HEADS, axis=1),
    )


def combine(active, attention_out, normed, lifted, gain_rows):
    merged = (
        active
        + rms_norm_apply(attention_out, gain_rows[2])
        + normed
        + rms_norm_apply(lifted, gain_rows[3])
    ) * root_half
    return (merged, rms_norm_apply(merged, gain_rows[4]))


def activate(gate, up):
    return jax.nn.gelu(gate, approximate=True) * up


def correct(merged, fed, predicted, gain_rows, router, coefficients):
    activated = merged + rms_norm_apply(fed, gain_rows[5])
    scale = (
        jnp.dot(modes(activated, gain_rows[0], router), coefficients[:, 16:], precision=highest)
        + 1.0
    )
    corrected = predicted + scale.T[:, :, None] * (activated - predicted[0])[None]
    return (corrected, corrected[0] * gain_rows[6])


def finish(corrected, projected, gain_rows):
    extra = rms_norm_apply(projected, gain_rows[7])
    return corrected + jnp.stack([jnp.zeros_like(extra), extra, extra, extra])


def forward_product(left, right):
    return jnp.dot(left, right, preferred_element_type=jnp.float32)


def transposed_product(left, right):
    return lax.dot_general(
        left, right, (((1,), (1,)), ((), ())), preferred_element_type=jnp.float32
    )


def weight_product(left, right):
    return lax.dot_general(
        left, right, (((0,), (0,)), ((), ())), preferred_element_type=jnp.float32
    )


def general_device(
    versions,
    layer_input,
    positions,
    documents,
    cotangent,
    norm_gains,
    router_weight,
    coefficients,
    query_key_gains,
    query_weight,
    key_matrix,
    value_matrix,
    out_weight,
    laurel_weight,
    input_gate,
    input_projection,
    gate_weight,
    up_weight,
    down_weight,
):
    narrow = jnp.bfloat16
    wide = jnp.float32
    (
        query_full,
        key_full,
        value_full,
        out_full,
        laurel_full,
        gate_full,
        projection_full,
        unit_gate,
        unit_up,
        unit_down,
    ) = (
        lax.all_gather(query_weight, "blk", axis=0, tiled=True),
        lax.all_gather(key_matrix, "blk", axis=0, tiled=True),
        lax.all_gather(value_matrix, "blk", axis=0, tiled=True),
        lax.all_gather(out_weight, "blk", axis=0, tiled=True),
        lax.all_gather(laurel_weight, "blk", axis=0, tiled=True),
        lax.all_gather(input_gate, "blk", axis=0, tiled=True),
        lax.all_gather(input_projection, "blk", axis=0, tiled=True),
        lax.all_gather(gate_weight, "blk", axis=0, tiled=True),
        lax.all_gather(up_weight, "blk", axis=0, tiled=True),
        lax.all_gather(down_weight, "blk", axis=0, tiled=True),
    )
    gain_rows = norm_gains.astype(wide)
    router_wide = router_weight.astype(wide)
    coef_wide = coefficients.astype(wide)
    head_wide = query_key_gains.astype(wide)
    (predicted, normed), pull_predict = jax.vjp(
        predict, versions.astype(wide), gain_rows, router_wide, coef_wide
    )
    normed_low = normed.astype(narrow)
    cosine_table, sine_table = angles(positions)

    def prepare_here(query_states, key, value_states, gains_here):
        return prepare(query_states, key, value_states, gains_here, cosine_table, sine_table)

    (rotated, keys_rep, values_rep), pull_prepare = jax.vjp(
        prepare_here,
        forward_product(normed_low, query_full),
        forward_product(normed_low, key_full),
        forward_product(normed_low, value_full),
        head_wide,
    )
    query_heads, key_heads, value_heads = (
        lax.all_to_all(rotated.astype(narrow), "heads", split_axis=1, concat_axis=0, tiled=True),
        lax.all_to_all(keys_rep.astype(narrow), "heads", split_axis=1, concat_axis=0, tiled=True),
        lax.all_to_all(values_rep.astype(narrow), "heads", split_axis=1, concat_axis=0, tiled=True),
    )
    keys_all, values_all = (
        lax.all_gather(key_heads, "blk", axis=0, tiled=True),
        lax.all_gather(value_heads, "blk", axis=0, tiled=True),
    )
    piece, local_heads, head_size = query_heads.shape
    first_row = lax.axis_index("blk") * piece
    last_row = first_row + piece - 1
    query_rows = first_row + jnp.arange(piece, dtype=jnp.int32)
    query_docs = lax.dynamic_slice_in_dim(documents, first_row, piece)
    block_starts = jnp.arange(keys_all.shape[0] // KEYB, dtype=jnp.int32) * KEYB

    def block_scores(offset):
        key_block = lax.dynamic_slice_in_dim(keys_all, offset, KEYB)
        value_block = lax.dynamic_slice_in_dim(values_all, offset, KEYB)
        key_rows = offset + jnp.arange(KEYB, dtype=jnp.int32)
        key_docs = lax.dynamic_slice_in_dim(documents, offset, KEYB)
        allowed = (key_rows[None, :] <= query_rows[:, None]) & (
            key_docs[None, :] == query_docs[:, None]
        )
        scores = jnp.einsum("qhd,khd->hqk", query_heads, key_block, preferred_element_type=wide)
        return (key_block, value_block, allowed[None], jnp.where(allowed[None], scores, -1e30))

    def attend(state, offset):

        def visit(carry):
            top, total, summed = carry
            key_block, value_block, allowed, scores = block_scores(offset)
            new_top = jnp.maximum(top, jnp.max(scores, axis=-1))
            weights = jnp.where(allowed, jnp.exp(scores - new_top[:, :, None]), 0.0)
            decay = jnp.exp(top - new_top)
            summed = summed * decay.T[:, :, None] + jnp.einsum(
                "hqk,khd->qhd", weights.astype(narrow), value_block, preferred_element_type=wide
            )
            return (new_top, total * decay + jnp.sum(weights, axis=-1), summed)

        def keep(carry):
            return carry

        return (lax.cond(offset <= last_row, visit, keep, state), None)

    start_state = (
        jnp.full((local_heads, piece), -1e30, wide),
        jnp.zeros((local_heads, piece), wide),
        jnp.zeros((piece, local_heads, head_size), wide),
    )
    (top, total, summed), unused = lax.scan(attend, start_state, block_starts)
    log_total = top + jnp.log(total)
    attended = summed / total.T[:, :, None]
    mixed = lax.all_to_all(
        attended.astype(narrow), "heads", split_axis=0, concat_axis=1, tiled=True
    )
    mixed_low = mixed.reshape(mixed.shape[0], -1)
    attention_out = transposed_product(mixed_low, out_full)
    down_low = forward_product(normed_low, laurel_full[:, :LAUREL_RANK]).astype(narrow)
    lifted = transposed_product(down_low, laurel_full[:, LAUREL_RANK:])
    (merged, feed_in), pull_combine = jax.vjp(
        combine, predicted[0], attention_out, normed_low.astype(wide), lifted, gain_rows
    )
    feed_low = feed_in.astype(narrow)
    unit_rows = lax.all_gather(feed_low, "heads", axis=0, tiled=True)
    hidden, pull_activate = jax.vjp(
        activate, forward_product(unit_rows, unit_gate), forward_product(unit_rows, unit_up)
    )
    hidden_low = hidden.astype(narrow)
    fed = transposed_product(hidden_low, unit_down)
    fed = lax.psum_scatter(
        fed.astype(jnp.bfloat16), "heads", scatter_dimension=0, tiled=True
    ).astype(jnp.float32)
    (corrected, first), pull_correct = jax.vjp(
        correct, merged, fed, predicted, gain_rows, router_wide, coef_wide
    )
    first_low = first.astype(narrow)
    gated, pull_gate = jax.vjp(
        activate, forward_product(first_low, gate_full), layer_input.astype(wide)
    )
    gated_low = gated.astype(narrow)
    projected = transposed_product(gated_low, projection_full)
    result, pull_finish = jax.vjp(finish, corrected, projected, gain_rows)
    corrected_grad, projected_grad, gains_finish = pull_finish(cotangent.astype(wide))
    projected_low = projected_grad.astype(narrow)
    gate_pre_grad, layer_grad = pull_gate(forward_product(projected_low, projection_full))
    gate_pre_low = gate_pre_grad.astype(narrow)
    merged_grad, fed_grad, predicted_grad, gains_correct, router_correct, coef_correct = (
        pull_correct((corrected_grad, transposed_product(gate_pre_low, gate_full)))
    )
    fed_low = fed_grad.astype(narrow)
    fed_rows = lax.all_gather(fed_low, "heads", axis=0, tiled=True)
    gate_grad, up_grad = pull_activate(forward_product(fed_rows, unit_down))
    gate_low = gate_grad.astype(narrow)
    up_low = up_grad.astype(narrow)
    feed_grad = transposed_product(gate_low, unit_gate) + transposed_product(up_low, unit_up)
    feed_grad = lax.psum_scatter(
        feed_grad.astype(jnp.bfloat16), "heads", scatter_dimension=0, tiled=True
    ).astype(jnp.float32)
    active_grad, attention_grad, normed_combine, lifted_grad, gains_combine = pull_combine(
        (merged_grad, feed_grad)
    )
    lifted_low = lifted_grad.astype(narrow)
    down_grad_low = forward_product(lifted_low, laurel_full[:, LAUREL_RANK:]).astype(narrow)
    attention_low = attention_grad.astype(narrow)
    mixed_grad = forward_product(attention_low, out_full).astype(narrow).reshape(mixed.shape)
    attended_grad = lax.all_to_all(mixed_grad, "heads", split_axis=1, concat_axis=0, tiled=True)
    delta = jnp.sum(attended_grad.astype(wide) * attended, axis=-1).T

    def attend_back(query_grad, offset):

        def visit(query_grad):
            key_block, value_block, allowed, scores = block_scores(offset)
            shares = jnp.where(allowed, jnp.exp(scores - log_total[:, :, None]), 0.0)
            share_grad = jnp.einsum(
                "qhd,khd->hqk", attended_grad, value_block, preferred_element_type=wide
            )
            score_low = (shares * (share_grad - delta[:, :, None])).astype(narrow)
            query_grad = query_grad + jnp.einsum(
                "hqk,khd->qhd", score_low, key_block, preferred_element_type=wide
            )
            key_grad = jnp.einsum(
                "hqk,qhd->khd", score_low, query_heads, preferred_element_type=wide
            )
            value_grad = jnp.einsum(
                "hqk,qhd->khd", shares.astype(narrow), attended_grad, preferred_element_type=wide
            )
            return (query_grad, (key_grad, value_grad))

        def skip(query_grad):
            empty = jnp.zeros((KEYB, local_heads, head_size), wide)
            return (query_grad, (empty, empty))

        return lax.cond(offset <= last_row, visit, skip, query_grad)

    query_grad, (key_grads, value_grads) = lax.scan(
        attend_back, jnp.zeros((piece, local_heads, head_size), wide), block_starts
    )
    key_own, value_own = (
        lax.psum_scatter(
            key_grads.reshape(keys_all.shape).astype(jnp.bfloat16),
            "blk",
            scatter_dimension=0,
            tiled=True,
        ).astype(jnp.float32),
        lax.psum_scatter(
            value_grads.reshape(keys_all.shape).astype(jnp.bfloat16),
            "blk",
            scatter_dimension=0,
            tiled=True,
        ).astype(jnp.float32),
    )
    query_back, key_back, value_back = (
        lax.all_to_all(query_grad.astype(narrow), "heads", split_axis=0, concat_axis=1, tiled=True),
        lax.all_to_all(key_own.astype(narrow), "heads", split_axis=0, concat_axis=1, tiled=True),
        lax.all_to_all(value_own.astype(narrow), "heads", split_axis=0, concat_axis=1, tiled=True),
    )
    query_pre, key_pre, value_pre, head_grad = pull_prepare(
        (query_back.astype(wide), key_back.astype(wide), value_back.astype(wide))
    )
    query_low = query_pre.astype(narrow)
    key_low = key_pre.astype(narrow)
    value_low = value_pre.astype(narrow)
    normed_grad = (
        normed_combine
        + transposed_product(query_low, query_full)
        + transposed_product(key_low, key_full)
        + transposed_product(value_low, value_full)
        + transposed_product(down_grad_low, laurel_full[:, :LAUREL_RANK])
    )
    predicted_grad = predicted_grad.at[0].add(active_grad)
    version_grad, gains_predict, router_predict, coef_predict = pull_predict(
        (predicted_grad, normed_grad)
    )
    small = lax.psum(
        (
            gains_finish + gains_correct + gains_combine + gains_predict,
            router_correct + router_predict,
            coef_correct + coef_predict,
            head_grad,
        ),
        ("heads", "blk"),
    )
    normed_targets = jnp.concatenate([query_low, key_low, value_low, down_grad_low], axis=1)
    summed_grads = lax.psum_scatter(
        jnp.concatenate(
            [
                weight_product(normed_low, normed_targets),
                weight_product(attention_low, mixed_low),
                weight_product(lifted_low, down_low),
                weight_product(first_low, gate_pre_low),
                weight_product(projected_low, gated_low),
                weight_product(unit_rows, gate_low),
                weight_product(unit_rows, up_low),
                weight_product(fed_rows, hidden_low),
            ],
            axis=1,
        ).astype(jnp.bfloat16),
        "blk",
        scatter_dimension=0,
        tiled=True,
    ).astype(jnp.float32)
    bounds = [0]
    for feature_width in (
        QUERY_HEAD_COUNT * HEAD_WIDTH,
        KEY_VALUE_HEADS * HEAD_WIDTH,
        KEY_VALUE_HEADS * HEAD_WIDTH,
        LAUREL_RANK,
        QUERY_HEAD_COUNT * HEAD_WIDTH,
        LAUREL_RANK,
        LAYER_INPUT_SIZE,
        LAYER_INPUT_SIZE,
    ):
        bounds.append(bounds[-1] + feature_width)
    attention_sum = lax.psum(summed_grads[:, : bounds[8]].astype(jnp.bfloat16), "heads").astype(
        jnp.float32
    )
    parts = [attention_sum[:, bounds[place] : bounds[place + 1]] for place in range(8)]
    unit_width = (summed_grads.shape[1] - bounds[8]) // 3
    gate_part = summed_grads[:, bounds[8] : bounds[8] + unit_width]
    up_part = summed_grads[:, bounds[8] + unit_width : bounds[8] + 2 * unit_width]
    down_part = summed_grads[:, bounds[8] + 2 * unit_width :]
    return (
        result.astype(narrow),
        version_grad.astype(narrow),
        layer_grad.astype(narrow),
        small[0],
        small[1],
        small[2],
        small[3],
        parts[0],
        parts[1],
        parts[2],
        parts[4],
        jnp.concatenate([parts[3], parts[5]], axis=1),
        parts[6],
        parts[7],
        gate_part,
        up_part,
        down_part,
    )


CORES = 2
LINE = 4
CHIPS = 4


def along_heads(x, step):
    return lax.ppermute(x, "heads", [(i, (i + step) % LINE) for i in range(LINE)])


def across_blk(x, mask):
    return lax.ppermute(x, "blk", [(i, i ^ mask) for i in range(CORES * CHIPS)])


def other_core(x):
    return across_blk(x, 1)


def gather_chip(x, *others):
    half = x.shape[0] // 2
    before = along_heads(x, 1)
    after = along_heads(x, -1)
    if others:
        before, after, *others = together(before, after, *others)
    far = jnp.concatenate([along_heads(before[:half], 1), along_heads(after[half:], -1)], axis=0)
    own = [before, x, after, far]
    rows = jnp.concatenate(own + [other_core(part) for part in own], axis=0)
    return (rows, *others) if others else rows


def scatter_chip(y, *others):
    wide = jnp.float32
    if not isinstance(y, (list, tuple)):
        n = y.shape[0] // 8
        y = [y[k * n : (k + 1) * n] for k in range(8)]
    half = y[0].shape[0] // 2
    before, own, after, far = (
        y[k].astype(wide) + other_core(y[k + 4]).astype(wide) for k in range(4)
    )
    far = far.astype(jnp.bfloat16)
    first = along_heads(far[:half], 1).astype(wide)
    second = along_heads(far[half:], -1).astype(wide)
    after = jnp.concatenate([after[:half] + first, after[half:]], axis=0).astype(jnp.bfloat16)
    before = jnp.concatenate([before[:half], before[half:] + second], axis=0).astype(jnp.bfloat16)
    if others:
        after, before, *others = together(after, before, *others)
    total = own + along_heads(after, 1).astype(wide) + along_heads(before, -1).astype(wide)
    return (total, *others) if others else total


def line_neighbours(x):
    return along_heads(x, 1), along_heads(x, -1)


def line_far(x, before, after):
    half = x.shape[0] // 2
    return along_heads(before[:half], 1), along_heads(after[half:], -1)


def share_line(x):
    line = lax.axis_index("heads")
    rows = x.shape[0] // LINE
    total = lax.dynamic_slice_in_dim(x, line * rows, rows).astype(jnp.float32)
    for step in range(1, LINE):
        piece = lax.dynamic_slice_in_dim(x, ((line + step) % LINE) * rows, rows)
        total = total + along_heads(piece, step).astype(jnp.float32)
    return total


def turn(x, blocks):
    rows = x.shape[0] // LINE
    twice = jnp.concatenate([x, x], axis=0)
    return lax.dynamic_slice_in_dim(twice, blocks * rows, x.shape[0])


def natural(x, core, line):
    half = x.shape[0] // 2
    own, other = (turn(part, (1 - line) % LINE) for part in (x[:half], x[half:]))
    first = core == 0
    return jnp.concatenate([jnp.where(first, own, other), jnp.where(first, other, own)], axis=0)


def arrival(x, core, line):
    half = x.shape[0] // 2
    first = core == 0
    own, other = jnp.where(first, x[:half], x[half:]), jnp.where(first, x[half:], x[:half])
    return jnp.concatenate([turn(part, (line - 1) % LINE) for part in (own, other)], axis=0)


def gather_chips(x):
    half = x.shape[0] // 2
    side = across_blk(x, 2)
    front = across_blk(x, 4)
    return side, front, across_blk(side[:half], 4), across_blk(front[half:], 2)


def scatter_chips(parts, *others):
    wide = jnp.float32
    half = parts[0].shape[0] // 2
    own, side, front, far = parts
    low = across_blk(jnp.concatenate([side[:half], far[:half]], axis=0), 2)
    high = across_blk(jnp.concatenate([front[half:], far[half:]], axis=0), 4)
    front_sum = (front[:half].astype(wide) + low[half:].astype(wide)).astype(jnp.bfloat16)
    side_sum = (side[half:].astype(wide) + high[half:].astype(wide)).astype(jnp.bfloat16)
    front_sum, side_sum, *others = together(front_sum, side_sum, *others)
    upper = own[:half].astype(wide) + low[:half].astype(wide) + across_blk(front_sum, 4).astype(wide)
    lower = own[half:].astype(wide) + high[:half].astype(wide) + across_blk(side_sum, 2).astype(wide)
    return jnp.concatenate([upper, lower], axis=0), *others


def butterfly(x):
    for mask in (1, 2, 4):
        x = x + across_blk(x, mask)
    for mask in (1, 2):
        x = x + lax.ppermute(x, "heads", [(i, i ^ mask) for i in range(LINE)])
    return x


def chip_groups():
    return [[core + CORES * chip for chip in range(CHIPS)] for core in range(CORES)]


def weight_rows(keep, send, core):
    got = other_core(send)
    first = core == 0
    return jnp.concatenate([jnp.where(first, keep, got), jnp.where(first, got, keep)], axis=0)


def all_rows(x):
    return lax.all_gather(x, "blk", axis=0, tiled=True, axis_index_groups=chip_groups())


def own_rows(x):
    return lax.psum_scatter(
        x, "blk", scatter_dimension=0, tiled=True, axis_index_groups=chip_groups()
    )


def together(*values):
    return lax.optimization_barrier(values)


def pick(x, start, size):
    return lax.dynamic_slice_in_dim(x, start, size, axis=1)


QUERY_ROWS = 512
FORWARD_ROWS = 1024
KEY_ROWS = 512


def place_rows(target, parts, chip):
    own, side, front, near, far = parts
    size = own.shape[0]
    half = size // 2
    target[pl.ds(pl.multiple_of(chip * size, size), size), :] = own[...]
    target[pl.ds(pl.multiple_of((chip ^ 1) * size, size), size), :] = side[...]
    target[pl.ds(pl.multiple_of((chip ^ 2) * size, size), size), :] = front[...]
    base = (chip ^ 3) * size
    target[pl.ds(pl.multiple_of(base, size), half), :] = near[...]
    target[pl.ds(pl.multiple_of(base + half, half), half), :] = far[...]


def place_both(meta, mine, theirs, k_all, v_all):
    chip = meta[0]

    @pl.when(meta[1] == 0)
    def _():
        place_rows(k_all, mine, chip)
        place_rows(v_all, theirs, chip)

    @pl.when(meta[1] != 0)
    def _():
        place_rows(v_all, mine, chip)
        place_rows(k_all, theirs, chip)


def rows_times_rows(left, right):
    return lax.dot_general(
        left, right, (((1,), (1,)), ((), ())), preferred_element_type=jnp.float32
    )


def columns_times_columns(left, right):
    return lax.dot_general(
        left, right, (((0,), (0,)), ((), ())), preferred_element_type=jnp.float32
    )


def arrival_rows(meta, block, rows):
    place = lax.rem(block % LINE - meta[2] + 1 + LINE, LINE)
    place = place + jnp.where(meta[1] == block // LINE, 0, LINE)
    return pl.ds(pl.multiple_of(place * rows, rows), rows)


def head_forward(x, gain, cosine, sine):
    normed = x * lax.rsqrt(jnp.mean(x * x, axis=-1, keepdims=True) + epsilon) * gain
    half = x.shape[-1] // 2
    low, high = normed[:, :half], normed[:, half:]
    return jnp.concatenate([low * cosine - high * sine, high * cosine + low * sine], axis=-1)


def head_backward(x, grad, gain, cosine, sine):
    half = x.shape[-1] // 2
    low, high = grad[:, :half], grad[:, half:]
    turned = jnp.concatenate([low * cosine + high * sine, high * cosine - low * sine], axis=-1)
    scale = lax.rsqrt(jnp.mean(x * x, axis=-1, keepdims=True) + epsilon)
    normed = x * scale
    inner = turned * gain
    x_grad = scale * (inner - normed * jnp.mean(inner * normed, axis=-1, keepdims=True))
    return x_grad, jnp.sum(turned * normed, axis=0, keepdims=True)


def kv_tables(meta, gain, cosine, sine):
    is_key = meta[1] == 0
    return jnp.where(is_key, gain, 1.0), jnp.where(is_key, cosine, 1.0), jnp.where(is_key, sine, 0.0)


def heads_kernel(meta, x_ref, w_ref, cosine_ref, sine_ref, gain_ref, q_ref, kv_ref, pre_ref, total):
    own, width = q_ref.shape
    depth = w_ref.shape[0]
    for half in range(CORES):
        rows = pl.ds(half * (own // CORES), own // CORES)
        total[rows, :] = jnp.dot(
            x_ref[rows, :depth], w_ref[:, : 2 * width], preferred_element_type=jnp.float32
        )
    size = own // (CORES * LINE)
    for block in range(CORES * LINE):
        rows = pl.ds(block * size, size)
        pre = total[arrival_rows(meta, block, size), :]
        pre_ref[rows, :] = pre
        cosine, sine = cosine_ref[rows, :], sine_ref[rows, :]
        q_ref[rows, :] = head_forward(pre[:, :width], gain_ref[0:1, :], cosine, sine).astype(q_ref.dtype)
        kv_ref[rows, :] = head_forward(
            pre[:, width:], *kv_tables(meta, gain_ref[1:2, :], cosine, sine)
        ).astype(kv_ref.dtype)


def kv_back_kernel(meta, pre_ref, grad_ref, cosine_ref, sine_ref, gain_ref, out_ref, gain_grad_ref):
    own, width = grad_ref.shape
    size = own // (CORES * LINE)
    total = jnp.zeros((1, width), jnp.float32)
    for block in range(CORES * LINE):
        rows = pl.ds(block * size, size)
        x_grad, gain_grad = head_backward(
            pre_ref[rows, width:],
            grad_ref[rows, :],
            *kv_tables(meta, gain_ref[1:2, :], cosine_ref[rows, :], sine_ref[rows, :]),
        )
        out_ref[arrival_rows(meta, block, size), :] = x_grad.astype(out_ref.dtype)
        total = total + gain_grad
    gain_grad_ref[...] = jnp.where(meta[1] == 0, total, 0.0)


def attend_kernel(meta, q_ref, lo_ref, *refs):
    mine, theirs = refs[:5], refs[5:10]
    out_ref, lse_ref, k_all, v_all, total, summed = refs[10:]
    place_both(meta, mine, theirs, k_all, v_all)
    own = q_ref.shape[0]
    for part in range(own // FORWARD_ROWS):
        rows = pl.ds(part * FORWARD_ROWS, FORWARD_ROWS)
        first = meta[0] * own + part * FORWARD_ROWS
        total[...] = jnp.zeros_like(total)
        summed[...] = jnp.zeros_like(summed)

        def visit(block, masked, rows=rows, first=first):
            at = pl.multiple_of(block * KEY_ROWS, KEY_ROWS)
            scores = rows_times_rows(q_ref[rows, :], k_all[pl.ds(at, KEY_ROWS), :])
            weights = jnp.exp(scores)
            if masked:
                key = at + lax.broadcasted_iota(jnp.int32, weights.shape, 1)
                query = first + lax.broadcasted_iota(jnp.int32, weights.shape, 0)
                weights = jnp.where((key >= lo_ref[rows, :]) & (key <= query), weights, 0.0)
            for lane in range(0, KEY_ROWS, 128):
                total[...] += weights[:, lane : lane + 128]
            summed[...] += jnp.dot(
                weights.astype(jnp.bfloat16),
                v_all[pl.ds(at, KEY_ROWS), :],
                preferred_element_type=jnp.float32,
            )

        start, full_from = meta[3 + 2 * part], meta[4 + 2 * part]
        end = (first + FORWARD_ROWS - 1) // KEY_ROWS + 1
        full_from = jnp.minimum(full_from, end)
        full_to = jnp.maximum(jnp.minimum((first + 1) // KEY_ROWS, end), full_from)

        @pl.loop(start, full_from)
        def _(block, visit=visit):
            visit(block, True)

        @pl.loop(full_from, full_to)
        def _(block, visit=visit):
            visit(block, False)

        @pl.loop(full_to, end)
        def _(block, visit=visit):
            visit(block, True)

        denominator = jnp.sum(total[...], axis=1, keepdims=True)
        out_ref[rows, :] = summed[...] / denominator
        lse_ref[rows, :] = jnp.log(denominator)


def attend_back_kernel(
    meta, q_ref, grad_ref, lse_ref, delta_ref, lo_ref, pre_ref, cosine_ref, sine_ref, gain_ref, *refs
):
    mine, theirs = refs[:5], refs[5:10]
    out_ref, gain_grad_ref, keep_ref, send_ref, k_all, v_all, dk_sum, dv_sum, dq_ref = refs[10:]
    place_both(meta, mine, theirs, k_all, v_all)
    chip = meta[0]
    own = q_ref.shape[0]
    parts = own // QUERY_ROWS
    keep_ref[...] = jnp.zeros_like(keep_ref)
    send_ref[...] = jnp.zeros_like(send_ref)
    dq_ref[...] = jnp.zeros_like(dq_ref)
    per_chip = own // KEY_ROWS

    @pl.loop(meta[3], (chip + 1) * per_chip)
    def _(block):
        at = pl.multiple_of(block * KEY_ROWS, KEY_ROWS)
        dk_sum[...] = jnp.zeros_like(dk_sum)
        dv_sum[...] = jnp.zeros_like(dv_sum)
        for part in range(parts):
            rows = pl.ds(part * QUERY_ROWS, QUERY_ROWS)
            first = chip * own + part * QUERY_ROWS

            def visit(masked, rows=rows, first=first):
                keys = k_all[pl.ds(at, KEY_ROWS), :]
                queries = q_ref[rows, :]
                grads = grad_ref[rows, :]
                shares = jnp.exp(rows_times_rows(keys, queries) - lse_ref[:, rows])
                if masked:
                    key = at + lax.broadcasted_iota(jnp.int32, shares.shape, 0)
                    query = first + lax.broadcasted_iota(jnp.int32, shares.shape, 1)
                    shares = jnp.where((key >= lo_ref[:, rows]) & (key <= query), shares, 0.0)
                share_grad = rows_times_rows(v_all[pl.ds(at, KEY_ROWS), :], grads)
                score_grad = (shares * (share_grad - delta_ref[:, rows])).astype(jnp.bfloat16)
                dv_sum[...] += jnp.dot(
                    shares.astype(jnp.bfloat16), grads, preferred_element_type=jnp.float32
                )
                dk_sum[...] += jnp.dot(score_grad, queries, preferred_element_type=jnp.float32)
                dq_ref[rows, :] += columns_times_columns(score_grad, keys)

            start, full_from = meta[3 + 2 * part], meta[4 + 2 * part]
            full = (block >= full_from) & ((block + 1) * KEY_ROWS <= first + 1)
            needed = (block >= start) & (block * KEY_ROWS < first + QUERY_ROWS)

            @pl.when(full)
            def _(visit=visit):
                visit(False)

            @pl.when(needed & jnp.logical_not(full))
            def _(visit=visit):
                visit(True)

        place = (block // per_chip) ^ chip
        inner = pl.multiple_of((block % per_chip) * KEY_ROWS, KEY_ROWS)
        dk_low = dk_sum[...].astype(jnp.bfloat16)
        dv_low = dv_sum[...].astype(jnp.bfloat16)

        @pl.when(meta[1] == 0)
        def _():
            keep_ref[place, pl.ds(inner, KEY_ROWS), :] = dk_low
            send_ref[place, pl.ds(inner, KEY_ROWS), :] = dv_low

        @pl.when(meta[1] != 0)
        def _():
            keep_ref[place, pl.ds(inner, KEY_ROWS), :] = dv_low
            send_ref[place, pl.ds(inner, KEY_ROWS), :] = dk_low

    width = q_ref.shape[1]
    size = own // (CORES * LINE)
    total = jnp.zeros((1, width), jnp.float32)
    for block in range(CORES * LINE):
        rows = pl.ds(block * size, size)
        x_grad, gain_grad = head_backward(
            pre_ref[rows, :width],
            dq_ref[rows, :].astype(jnp.bfloat16).astype(jnp.float32),
            gain_ref[0:1, :],
            cosine_ref[rows, :],
            sine_ref[rows, :],
        )
        out_ref[arrival_rows(meta, block, size), :] = x_grad.astype(out_ref.dtype)
        total = total + gain_grad
    gain_grad_ref[...] = total


def takes(microseconds):
    return pl.CostEstimate(
        flops=int(microseconds * 1e9), bytes_accessed=int(microseconds * 3.3e6), transcendentals=0
    )


def in_vmem(count):
    return [pl.BlockSpec(memory_space=pltpu.VMEM)] * count


def attend_here(meta, q, lo, mine, theirs):
    own, width = q.shape
    row = own * CHIPS
    return pl.pallas_call(
        attend_kernel,
        out_shape=(
            jax.ShapeDtypeStruct((own, width), jnp.float32),
            jax.ShapeDtypeStruct((own, 1), jnp.float32),
        ),
        in_specs=[pl.BlockSpec(memory_space=pltpu.SMEM)] + in_vmem(12),
        out_specs=tuple(in_vmem(2)),
        scratch_shapes=[
            pltpu.VMEM((row, width), jnp.bfloat16),
            pltpu.VMEM((row, width), jnp.bfloat16),
            pltpu.VMEM((FORWARD_ROWS, 128), jnp.float32),
            pltpu.VMEM((FORWARD_ROWS, width), jnp.float32),
        ],
        compiler_params=pltpu.CompilerParams(vmem_limit_bytes=40 << 20),
        cost_estimate=takes(9),
    )(meta, q, lo.reshape(own, 1), *mine, *theirs)


def attend_back_here(meta, q, grad, lse, delta, lo, tables, mine, theirs):
    own, width = q.shape
    row = own * CHIPS
    return pl.pallas_call(
        attend_back_kernel,
        out_shape=(
            jax.ShapeDtypeStruct((own, width), jnp.bfloat16),
            jax.ShapeDtypeStruct((1, width), jnp.float32),
            jax.ShapeDtypeStruct((CHIPS, own, width), jnp.bfloat16),
            jax.ShapeDtypeStruct((CHIPS, own, width), jnp.bfloat16),
        ),
        in_specs=[pl.BlockSpec(memory_space=pltpu.SMEM)] + in_vmem(19),
        out_specs=tuple(in_vmem(4)),
        scratch_shapes=[
            pltpu.VMEM((row, width), jnp.bfloat16),
            pltpu.VMEM((row, width), jnp.bfloat16),
            pltpu.VMEM((KEY_ROWS, width), jnp.float32),
            pltpu.VMEM((KEY_ROWS, width), jnp.float32),
            pltpu.VMEM((own, width), jnp.float32),
        ],
        compiler_params=pltpu.CompilerParams(vmem_limit_bytes=48 << 20),
        cost_estimate=takes(20.5),
    )(
        meta,
        q,
        grad,
        lse.reshape(1, own),
        delta.reshape(1, own),
        lo.reshape(1, own),
        *tables,
        *mine,
        *theirs,
    )


def heads_here(meta, x, weights, cosine, sine, gains):
    own, width = x.shape[0], gains.shape[1]
    return pl.pallas_call(
        heads_kernel,
        out_shape=(
            jax.ShapeDtypeStruct((own, width), jnp.bfloat16),
            jax.ShapeDtypeStruct((own, width), jnp.bfloat16),
            jax.ShapeDtypeStruct((own, 2 * width), jnp.float32),
        ),
        in_specs=[pl.BlockSpec(memory_space=pltpu.SMEM)] + in_vmem(5),
        out_specs=tuple(in_vmem(3)),
        scratch_shapes=[pltpu.VMEM((own, 2 * width), jnp.float32)],
        compiler_params=pltpu.CompilerParams(vmem_limit_bytes=48 << 20),
        cost_estimate=takes(7),
    )(meta, x, weights, cosine, sine, gains)


def kv_back_here(meta, grad, tables):
    own, width = grad.shape
    pre, *others = tables
    return pl.pallas_call(
        kv_back_kernel,
        out_shape=(
            jax.ShapeDtypeStruct((own, width), jnp.bfloat16),
            jax.ShapeDtypeStruct((1, width), jnp.float32),
        ),
        in_specs=[pl.BlockSpec(memory_space=pltpu.SMEM)] + in_vmem(5),
        out_specs=tuple(in_vmem(2)),
        compiler_params=pltpu.CompilerParams(vmem_limit_bytes=32 << 20),
        cost_estimate=takes(1.5),
    )(meta, pre, grad, *others)


TOKEN_ROWS = 32
COMBINE_TIME = 45


def scaled(x):
    return x * lax.rsqrt(jnp.mean(x * x, axis=-1, keepdims=True) + epsilon)


def scaled_back(x, grad):
    scale = lax.rsqrt(jnp.mean(x * x, axis=-1, keepdims=True) + epsilon)
    normed = x * scale
    return scale * (grad - normed * jnp.mean(grad * normed, axis=-1, keepdims=True))


def inner(left, right):
    return jnp.sum(left * right, axis=-1, keepdims=True)


def over_rows(x):
    return jnp.sum(x, axis=0, keepdims=True)


def mode_columns(aligned, router_ref):
    return [jnp.tanh(inner(aligned, router_ref[k : k + 1, :])) for k in range(4)]


def mixed_columns(mode, coef, column):
    return sum(mode[k] * coef[k, column] for k in range(4))


def predict_kernel(coef, x_ref, gain_ref, router_ref, predicted_ref, normed_ref):
    x = [x_ref[i].astype(jnp.float32) for i in range(4)]
    mode = mode_columns(scaled(x[0]) * gain_ref[0:1, :], router_ref)
    for i in range(4):
        value = x[i]
        for j in range(4):
            value = value + mixed_columns(mode, coef, 4 * i + j) * x[j]
        predicted_ref[i] = value
        if i == 0:
            normed_ref[...] = (scaled(value) * gain_ref[1:2, :]).astype(normed_ref.dtype)


def predict_back_kernel(
    coef, x_ref, first_ref, cotangent_ref, normed_ref, extra_ref, gain_ref, router_ref, early_ref,
    out_ref, packed_ref, mode_all, table_all,
):
    step = pl.program_id(0)

    @pl.when(step == 0)
    def _():
        packed_ref[...] = early_ref[...]
        mode_all[...] = jnp.zeros_like(mode_all)
        table_all[...] = jnp.zeros_like(table_all)

    rows = pl.ds(pl.multiple_of(step * TOKEN_ROWS, TOKEN_ROWS), TOKEN_ROWS)
    x = [x_ref[i].astype(jnp.float32) for i in range(4)]
    normed_zero = scaled(x[0])
    aligned = normed_zero * gain_ref[0:1, :]
    mode = mode_columns(aligned, router_ref)
    table = [[mixed_columns(mode, coef, 4 * i + j) for j in range(4)] for i in range(4)]
    predicted = x[0] + sum(table[0][j] * x[j] for j in range(4))
    normed_grad = normed_ref[...] + extra_ref[...]
    packed_ref[1:2, :] += over_rows(normed_grad * scaled(predicted))
    grads = [first_ref[...] + scaled_back(predicted, normed_grad * gain_ref[1:2, :])]
    grads += [cotangent_ref[i].astype(jnp.float32) for i in (1, 2, 3)]
    mode_grad = [0.0] * 4
    for i in range(4):
        for j in range(4):
            table_grad = inner(grads[i], x[j])
            table_all[rows, 4 * i + j : 4 * i + j + 1] = table_grad
            for k in range(4):
                mode_grad[k] = mode_grad[k] + table_grad * coef[k, 4 * i + j]
    aligned_grad = 0.0
    for k in range(4):
        mode_all[rows, k : k + 1] = mode[k]
        logit_grad = mode_grad[k] * (1.0 - mode[k] * mode[k])
        aligned_grad = aligned_grad + logit_grad * router_ref[k : k + 1, :]
        packed_ref[8 + k : 9 + k, :] += over_rows(logit_grad * aligned)
    packed_ref[0:1, :] += over_rows(aligned_grad * normed_zero)
    for j in range(4):
        value = grads[j] + sum(table[i][j] * grads[i] for i in range(4))
        if j == 0:
            value = value + scaled_back(x[0], aligned_grad * gain_ref[0:1, :])
        out_ref[j] = value.astype(out_ref.dtype)

    @pl.when(step == pl.num_programs(0) - 1)
    def _():
        products = lax.dot_general(
            mode_all[...],
            table_all[...],
            (((0,), (0,)), ((), ())),
            precision=highest,
            preferred_element_type=jnp.float32,
        )
        packed_ref[12:16, 0:128] += products[0:4, :]


def gelu_parts(x):
    slope = (2.0 / jnp.pi) ** 0.5
    bend = jnp.tanh(slope * (x + 0.044715 * x * x * x))
    value = 0.5 * x * (1.0 + bend)
    derivative = 0.5 * (1.0 + bend) + 0.5 * x * (1.0 - bend * bend) * slope * (
        1.0 + 3.0 * 0.044715 * x * x
    )
    return value, derivative


def middle_kernel(
    coef, merged_ref, fed_ref, predicted_ref, cotangent_ref, input_ref, gain_ref, router_ref, weight_ref,
    result_ref, layer_grad_ref, fed_grad_ref, merged_grad_ref, first_grad_ref, packed_ref,
    first_ref, gate_pre_ref, projected_ref, gated_ref,
    active, wide_rows, mode_all, scale_grads,
):
    tokens, width = merged_ref.shape
    small = input_ref.shape[1]
    ranks = weight_ref.shape[1] - 2 * small
    gate_columns = pl.ds(ranks, small)
    projection_columns = pl.ds(ranks + small, small)
    packed_ref[...] = jnp.zeros_like(packed_ref)
    mode_all[...] = jnp.zeros_like(mode_all)
    scale_grads[...] = jnp.zeros_like(scale_grads)

    def scales(value):
        normed = scaled(value)
        aligned = normed * gain_ref[0:1, :]
        mode = mode_columns(aligned, router_ref)
        return normed, aligned, mode, [mixed_columns(mode, coef, 16 + i) + 1.0 for i in range(4)]

    @pl.loop(0, tokens // TOKEN_ROWS)
    def _(step):
        rows = pl.ds(pl.multiple_of(step * TOKEN_ROWS, TOKEN_ROWS), TOKEN_ROWS)
        value = merged_ref[rows, :] + scaled(fed_ref[rows, :]) * gain_ref[5:6, :]
        active[rows, :] = value
        _, _, _, scale = scales(value)
        start = predicted_ref[0, rows, :]
        corrected = start + scale[0] * (value - start)
        first_ref[rows, :] = (corrected * gain_ref[6:7, :]).astype(first_ref.dtype)

    gate_pre = jnp.dot(first_ref[...], weight_ref[:, gate_columns], preferred_element_type=jnp.float32)
    gelu, slope = gelu_parts(gate_pre)
    layer_input = input_ref[...].astype(jnp.float32)
    gated_ref[...] = (gelu * layer_input).astype(gated_ref.dtype)
    wide_rows[...] = rows_times_rows(gated_ref[...], weight_ref[:, projection_columns])

    @pl.loop(0, tokens // TOKEN_ROWS)
    def _(step):
        rows = pl.ds(pl.multiple_of(step * TOKEN_ROWS, TOKEN_ROWS), TOKEN_ROWS)
        projected = wide_rows[rows, :]
        normed = scaled(projected)
        extra = normed * gain_ref[7:8, :]
        value = active[rows, :]
        _, _, _, scale = scales(value)
        change = value - predicted_ref[0, rows, :]
        extra_grad = 0.0
        for i in range(4):
            corrected = predicted_ref[i, rows, :] + scale[i] * change
            if i:
                corrected = corrected + extra
                extra_grad = extra_grad + cotangent_ref[i, rows, :].astype(jnp.float32)
            result_ref[i, rows, :] = corrected.astype(result_ref.dtype)
        packed_ref[7:8, :] += over_rows(extra_grad * normed)
        projected_ref[rows, :] = scaled_back(projected, extra_grad * gain_ref[7:8, :]).astype(
            projected_ref.dtype
        )

    gated_grad = jnp.dot(
        projected_ref[...], weight_ref[:, projection_columns], preferred_element_type=jnp.float32
    )
    layer_grad_ref[...] = (gated_grad * gelu).astype(layer_grad_ref.dtype)
    gate_pre_ref[...] = (gated_grad * layer_input * slope).astype(gate_pre_ref.dtype)
    wide_rows[...] = rows_times_rows(gate_pre_ref[...], weight_ref[:, gate_columns])

    @pl.loop(0, tokens // TOKEN_ROWS)
    def _(step):
        rows = pl.ds(pl.multiple_of(step * TOKEN_ROWS, TOKEN_ROWS), TOKEN_ROWS)
        value = active[rows, :]
        normed, aligned, mode, scale = scales(value)
        start = predicted_ref[0, rows, :]
        change = value - start
        first_grad = wide_rows[rows, :]
        packed_ref[6:7, :] += over_rows(first_grad * (start + scale[0] * change))
        grads = [cotangent_ref[i, rows, :].astype(jnp.float32) for i in range(4)]
        grads[0] = grads[0] + first_grad * gain_ref[6:7, :]
        change_grad = sum(scale[i] * grads[i] for i in range(4))
        mode_grad = [0.0] * 4
        for i in range(4):
            scale_grad = inner(grads[i], change)
            scale_grads[rows, 16 + i : 17 + i] = scale_grad
            for k in range(4):
                mode_grad[k] = mode_grad[k] + scale_grad * coef[k, 16 + i]
        aligned_grad = 0.0
        for k in range(4):
            mode_all[rows, k : k + 1] = mode[k]
            logit_grad = mode_grad[k] * (1.0 - mode[k] * mode[k])
            aligned_grad = aligned_grad + logit_grad * router_ref[k : k + 1, :]
            packed_ref[8 + k : 9 + k, :] += over_rows(logit_grad * aligned)
        packed_ref[0:1, :] += over_rows(aligned_grad * normed)
        active_grad = change_grad + scaled_back(value, aligned_grad * gain_ref[0:1, :])
        first_grad_ref[rows, :] = grads[0] - change_grad
        merged_grad_ref[rows, :] = active_grad
        fed = fed_ref[rows, :]
        packed_ref[5:6, :] += over_rows(active_grad * scaled(fed))
        fed_grad_ref[rows, :] = scaled_back(fed, active_grad * gain_ref[5:6, :]).astype(
            fed_grad_ref.dtype
        )

    products = lax.dot_general(
        mode_all[...],
        scale_grads[...],
        (((0,), (0,)), ((), ())),
        precision=highest,
        preferred_element_type=jnp.float32,
    )
    packed_ref[12:16, 0:128] += products[0:4, :]


def combine_back_kernel(
    merged_ref, attention_ref, lifted_ref, merged_grad_ref, feed_ref, first_ref, gain_ref, early_ref,
    total_ref, active_ref, attention_grad_ref, lifted_grad_ref, packed_ref,
):
    @pl.when(pl.program_id(0) == 0)
    def _():
        packed_ref[...] = early_ref[...]

    merged, feed_grad = merged_ref[...], feed_ref[...]
    packed_ref[4:5, :] += over_rows(feed_grad * scaled(merged))
    grad = (merged_grad_ref[...] + scaled_back(merged, feed_grad * gain_ref[4:5, :])) * root_half
    active_ref[...] = grad
    total_ref[...] = first_ref[...] + grad
    for value_ref, row, out_ref in ((attention_ref, 2, attention_grad_ref), (lifted_ref, 3, lifted_grad_ref)):
        value = value_ref[...]
        packed_ref[row : row + 1, :] += over_rows(grad * scaled(value))
        out_ref[...] = scaled_back(value, grad * gain_ref[row : row + 1, :]).astype(out_ref.dtype)


def combine_back_here(merged, attention, lifted, merged_grad, feed_grad, first, gains, early):
    tokens, width = merged.shape
    rows = token_rows(width)
    full = jax.ShapeDtypeStruct((tokens, width), jnp.float32)
    low = jax.ShapeDtypeStruct((tokens, width), jnp.bfloat16)
    return pl.pallas_call(
        combine_back_kernel,
        grid=(tokens // TOKEN_ROWS,),
        out_shape=(full, full, low, low, jax.ShapeDtypeStruct(early.shape, jnp.float32)),
        in_specs=[rows] * 6 + [whole(gains.shape), whole(early.shape)],
        out_specs=(rows, rows, rows, rows, whole(early.shape)),
        compiler_params=pltpu.CompilerParams(vmem_limit_bytes=60 << 20),
        cost_estimate=takes(COMBINE_TIME),
    )(merged, attention, lifted, merged_grad, feed_grad, first, gains, early)


HIDDEN_TILE = 256
WIDTH_TILE = 512


def gelu_of(x):
    return gelu_parts(x)[0]


def put_pieces(refs, value):
    rows = refs[0].shape[0]
    for place, ref in enumerate(refs):
        ref[...] = value[place * rows : (place + 1) * rows].astype(ref.dtype)


def unit_kernel(x_ref, gate_w_ref, up_w_ref, down_w_ref, gate_ref, up_ref, hidden_ref, *refs):
    *fed_refs, kept = refs
    step = pl.program_id(0)
    tiles = kept.shape[0]
    own = x_ref.shape[0]
    half = own // CORES

    @pl.when(step < tiles)
    def _():
        for part in range(CORES):
            rows = pl.ds(part * half, half)
            x = x_ref[rows, :]
            gate = jnp.dot(x, gate_w_ref[...], preferred_element_type=jnp.float32)
            up = jnp.dot(x, up_w_ref[...], preferred_element_type=jnp.float32)
            hidden = (gelu_of(gate) * up).astype(hidden_ref.dtype)
            gate_ref[rows, :] = gate.astype(gate_ref.dtype)
            up_ref[rows, :] = up.astype(up_ref.dtype)
            hidden_ref[rows, :] = hidden
            kept[step, rows, :] = hidden

    @pl.when(step >= tiles)
    def _():
        hidden = jnp.concatenate([kept[tile] for tile in range(tiles)], axis=1)
        put_pieces(fed_refs, rows_times_rows(hidden, down_w_ref[...]))


def unit_back_kernel(
    grad_ref, gate_ref, up_ref, down_w_ref, two_w_ref, gate_grad_ref, up_grad_ref, *refs
):
    *feed_refs, kept = refs
    step = pl.program_id(0)
    tiles = kept.shape[0] // 2
    own = grad_ref.shape[0]
    half = own // CORES

    @pl.when(step < tiles)
    def _():
        for part in range(CORES):
            rows = pl.ds(part * half, half)
            grad = jnp.dot(grad_ref[rows, :], down_w_ref[...], preferred_element_type=jnp.float32)
            gelu, slope = gelu_parts(gate_ref[rows, :].astype(jnp.float32))
            gate_grad = (grad * up_ref[rows, :].astype(jnp.float32) * slope).astype(gate_grad_ref.dtype)
            up_grad = (grad * gelu).astype(up_grad_ref.dtype)
            gate_grad_ref[rows, :] = gate_grad
            up_grad_ref[rows, :] = up_grad
            kept[step, rows, :] = gate_grad
            kept[tiles + step, rows, :] = up_grad

    @pl.when(step >= tiles)
    def _():
        both = jnp.concatenate([kept[tile] for tile in range(2 * tiles)], axis=1)
        put_pieces(feed_refs, rows_times_rows(both, two_w_ref[...]))


def unit_here(x, weights):
    own, width = x.shape
    hidden = weights.shape[1] // 3
    tiles, sums = hidden // HIDDEN_TILE, width // WIDTH_TILE

    def tile(first):
        return pl.BlockSpec((width, HIDDEN_TILE), lambda i: (0, first * tiles + jnp.minimum(i, tiles - 1)))

    saved = pl.BlockSpec((own, HIDDEN_TILE), lambda i: (0, jnp.minimum(i, tiles - 1)))
    return pl.pallas_call(
        unit_kernel,
        grid=(tiles + sums,),
        out_shape=tuple(
            jax.ShapeDtypeStruct(shape, jnp.bfloat16)
            for shape in [(own, hidden)] * 3 + [(own // 8, width)] * 8
        ),
        in_specs=[
            whole(x.shape),
            tile(0),
            tile(1),
            pl.BlockSpec((WIDTH_TILE, hidden), lambda i: (jnp.maximum(i - tiles, 0), 2)),
        ],
        out_specs=(
            *[saved] * 3,
            *[pl.BlockSpec((own // 8, WIDTH_TILE), lambda i: (0, jnp.maximum(i - tiles, 0)))] * 8,
        ),
        scratch_shapes=[pltpu.VMEM((tiles, own, HIDDEN_TILE), jnp.bfloat16)],
        compiler_params=pltpu.CompilerParams(vmem_limit_bytes=48 << 20),
        cost_estimate=takes(18),
    )(x, weights, weights, weights)


def unit_back_here(grad, gate, up, weights):
    own, width = grad.shape
    hidden = gate.shape[1]
    tiles, sums = hidden // HIDDEN_TILE, width // WIDTH_TILE
    saved = pl.BlockSpec((own, HIDDEN_TILE), lambda i: (0, jnp.minimum(i, tiles - 1)))
    return pl.pallas_call(
        unit_back_kernel,
        grid=(tiles + sums,),
        out_shape=tuple(
            jax.ShapeDtypeStruct(shape, jnp.bfloat16)
            for shape in [(own, hidden)] * 2 + [(own // 8, width)] * 8
        ),
        in_specs=[
            whole(grad.shape),
            saved,
            saved,
            pl.BlockSpec((width, HIDDEN_TILE), lambda i: (0, 2 * tiles + jnp.minimum(i, tiles - 1))),
            pl.BlockSpec((WIDTH_TILE, 2 * hidden), lambda i: (jnp.maximum(i - tiles, 0), 0)),
        ],
        out_specs=(
            *[saved] * 2,
            *[pl.BlockSpec((own // 8, WIDTH_TILE), lambda i: (0, jnp.maximum(i - tiles, 0)))] * 8,
        ),
        scratch_shapes=[pltpu.VMEM((2 * tiles, own, HIDDEN_TILE), jnp.bfloat16)],
        compiler_params=pltpu.CompilerParams(vmem_limit_bytes=56 << 20),
        cost_estimate=takes(18),
    )(grad, gate, up, weights, weights)


def assemble_kernel(meta, *refs):
    query, kv, out = refs[:5], refs[5:10], refs[10:15]
    query_ref, out_ref, key_ref, value_ref, laurel_ref, io_ref = refs[15:]
    rows = key_ref.shape[0]
    pair = query[0].shape[1]
    head = pair // CORES
    part = io_ref.shape[0] // LINE
    key_ref[...] = jnp.zeros_like(key_ref)
    value_ref[...] = jnp.zeros_like(value_ref)
    laurel_ref[...] = jnp.zeros_like(laurel_ref)

    def put(sender, query_part, kv_part, to):
        columns = pl.ds(pl.multiple_of(sender * pair, pair), pair)
        query_ref[to, columns] = query_part.astype(jnp.float32)
        group = pl.ds(pl.multiple_of(sender // (LINE // KEY_VALUE_HEADS) * head, head), head)
        key_ref[to, group] += kv_part[:, :head].astype(jnp.float32)
        value_ref[to, group] += kv_part[:, head:].astype(jnp.float32)

    def put_out(sender, value, at):
        columns = pl.ds(pl.multiple_of(sender * pair, pair), pair)
        count = min(rows - at, value.shape[0])
        to = pl.ds(at, count)
        out_ref[to, columns] = value[:count, :pair].astype(jnp.float32)
        laurel_ref[to, :] += value[:count, pair:].astype(jnp.float32)
        if value.shape[0] > count:
            start = pl.multiple_of(sender * part, part)
            io_ref[pl.ds(start, part), :] = value[count:, : io_ref.shape[1]].astype(jnp.float32)

    for step, place in ((0, 0), (-1, 1), (1, 2)):
        sender = lax.rem(meta[2] + step + LINE, LINE)
        put(sender, query[place][...], kv[place][...], pl.ds(0, rows))
        put_out(sender, out[place][...], 0)
    sender = lax.rem(meta[2] + 2, LINE)
    put(sender, query[3][...], kv[3][...], pl.ds(0, rows // 2))
    put(sender, query[4][...], kv[4][...], pl.ds(rows // 2, rows // 2))
    put_out(sender, out[3][...], 0)
    put_out(sender, out[4][...], out[3].shape[0])


def assemble_here(meta, query, kv, out):
    rows, pair = query[0].shape
    small = 2 * LAYER_INPUT_SIZE
    shapes = (
        (rows, LINE * pair),
        (rows, LINE * pair),
        (rows, KEY_VALUE_HEADS * HEAD_WIDTH),
        (rows, KEY_VALUE_HEADS * HEAD_WIDTH),
        (rows, 2 * LAUREL_RANK),
        (rows, small),
    )
    return pl.pallas_call(
        assemble_kernel,
        out_shape=tuple(jax.ShapeDtypeStruct(shape, jnp.float32) for shape in shapes),
        in_specs=[in_smem()] + in_vmem(15),
        out_specs=tuple(in_vmem(len(shapes))),
        compiler_params=pltpu.CompilerParams(vmem_limit_bytes=32 << 20),
        cost_estimate=takes(4),
    )(meta, *query, *kv, *out)


def in_smem():
    return pl.BlockSpec(memory_space=pltpu.SMEM)


def token_block(count, width):
    return pl.BlockSpec((count, TOKEN_ROWS, width), lambda i: (0, i, 0))


def token_rows(width):
    return pl.BlockSpec((TOKEN_ROWS, width), lambda i: (i, 0))


def whole(shape):
    return pl.BlockSpec(shape, lambda i: (0,) * len(shape))


def predict_here(versions, gains, router, coef):
    tokens, width = versions.shape[1:]
    return pl.pallas_call(
        predict_kernel,
        grid=(tokens // TOKEN_ROWS,),
        out_shape=(
            jax.ShapeDtypeStruct(versions.shape, jnp.float32),
            jax.ShapeDtypeStruct((tokens, width), jnp.bfloat16),
        ),
        in_specs=[in_smem(), token_block(4, width), whole(gains.shape), whole(router.shape)],
        out_specs=(token_block(4, width), token_rows(width)),
        compiler_params=pltpu.CompilerParams(vmem_limit_bytes=32 << 20),
        cost_estimate=takes(4.5),
    )(coef, versions, gains, router)


def predict_back_here(versions, first, cotangent, normed, extra, gains, router, coef, early):
    tokens, width = first.shape
    return pl.pallas_call(
        predict_back_kernel,
        grid=(tokens // TOKEN_ROWS,),
        out_shape=(
            jax.ShapeDtypeStruct(versions.shape, jnp.bfloat16),
            jax.ShapeDtypeStruct(early.shape, jnp.float32),
        ),
        in_specs=[
            in_smem(),
            token_block(4, width),
            token_rows(width),
            token_block(4, width),
            token_rows(width),
            token_rows(width),
            whole(gains.shape),
            whole(router.shape),
            whole(early.shape),
        ],
        out_specs=(token_block(4, width), whole(early.shape)),
        scratch_shapes=[
            pltpu.VMEM((tokens, 128), jnp.float32),
            pltpu.VMEM((tokens, 128), jnp.float32),
        ],
        compiler_params=pltpu.CompilerParams(vmem_limit_bytes=32 << 20),
        cost_estimate=takes(10),
    )(coef, versions, first, cotangent, normed, extra, gains, router, early)


def middle_here(merged, fed, predicted, cotangent, layer_input, gains, router, coef, weights):
    tokens, width = merged.shape
    small = layer_input.shape[1]
    narrow, wide = jnp.bfloat16, jnp.float32
    shapes = (
        (predicted.shape, narrow),
        ((tokens, small), narrow),
        ((tokens, width), narrow),
        ((tokens, width), wide),
        ((tokens, width), wide),
        ((16, width), wide),
        ((tokens, width), narrow),
        ((tokens, small), narrow),
        ((tokens, width), narrow),
        ((tokens, small), narrow),
    )
    return pl.pallas_call(
        middle_kernel,
        out_shape=tuple(jax.ShapeDtypeStruct(*shape) for shape in shapes),
        in_specs=[in_smem()] + in_vmem(8),
        out_specs=tuple(in_vmem(len(shapes))),
        scratch_shapes=[
            pltpu.VMEM((tokens, width), wide),
            pltpu.VMEM((tokens, width), wide),
            pltpu.VMEM((tokens, 128), wide),
            pltpu.VMEM((tokens, 128), wide),
        ],
        compiler_params=pltpu.CompilerParams(vmem_limit_bytes=48 << 20),
        cost_estimate=takes(17),
    )(coef, merged, fed, predicted, cotangent, layer_input, gains, router, weights)


def chip_device(
    versions,
    layer_input,
    positions,
    documents,
    cotangent,
    norm_gains,
    router_weight,
    coefficients,
    query_key_gains,
    query_weight,
    key_matrix,
    value_matrix,
    out_weight,
    laurel_weight,
    input_gate,
    input_projection,
    gate_weight,
    up_weight,
    down_weight,
):
    narrow = jnp.bfloat16
    wide = jnp.float32
    line = lax.axis_index("heads")
    piece = lax.axis_index("blk")
    core = piece % CORES
    chip = piece // CORES
    first_core = core == 0
    tokens = versions.shape[1]
    own = 8 * tokens
    width = versions.shape[2]
    rows_here = query_weight.shape[0]
    hidden = gate_weight.shape[1] // CORES
    head = CORES * line + core
    group = head // (QUERY_HEAD_COUNT // KEY_VALUE_HEADS)

    def head_columns(index, kv):
        return jnp.concatenate(
            [
                pick(query_weight, index * HEAD_WIDTH, HEAD_WIDTH),
                pick(kv, group * HEAD_WIDTH, HEAD_WIDTH),
                pick(out_weight, index * HEAD_WIDTH, HEAD_WIDTH),
            ],
            axis=1,
        )

    kv_mine = jnp.where(first_core, key_matrix, value_matrix)
    kv_theirs = jnp.where(first_core, value_matrix, key_matrix)
    head_full = all_rows(
        weight_rows(head_columns(head, kv_mine), head_columns(head ^ 1, kv_theirs), core)
    )
    small_full = lax.all_gather(
        jnp.concatenate([laurel_weight, input_gate, input_projection], axis=1),
        "blk",
        axis=0,
        tiled=True,
    )

    query_kv_full = head_full[:, : 2 * HEAD_WIDTH]
    out_full = head_full[:, 2 * HEAD_WIDTH :]
    laurel_full = small_full[:, : 2 * LAUREL_RANK]
    gain_rows = norm_gains.astype(wide)
    router_wide = router_weight.astype(wide)
    coef_wide = coefficients.astype(wide)
    head_wide = query_key_gains.astype(wide)
    predicted, normed_low = predict_here(versions, gain_rows, router_wide, coef_wide)
    *unit_weights, normed_low = together(gate_weight, up_weight, down_weight, normed_low)

    def hidden_columns(index):
        return jnp.concatenate([pick(w, index * hidden, hidden) for w in unit_weights], axis=1)

    unit_full = all_rows(weight_rows(hidden_columns(core), hidden_columns(1 - core), core))

    digits = jnp.stack([positions // 128, positions % 128], axis=1).astype(narrow)
    sent = jnp.concatenate([normed_low, jnp.pad(digits, ((0, 0), (0, 126)))], axis=1)
    gathered = gather_chip(sent)
    normed_rows = gathered[:, :width]
    digits_all = natural(gathered[:, width : width + 2].astype(wide), core, line)
    phase_position = digits_all[:, :1] * 128.0 + digits_all[:, 1:2]
    frequency = rotary_base ** (-2.0 * jnp.arange(HEAD_WIDTH // 2, dtype=wide) / HEAD_WIDTH)
    phase = phase_position * frequency[None, :]
    cosine, sine = jnp.cos(phase), jnp.sin(phase)
    first_row = chip * own
    row_docs = lax.dynamic_slice_in_dim(documents, first_row, own)
    begin_one = jnp.sum(documents < 1)
    begin_two = jnp.sum(documents < 2)
    lo = jnp.where(row_docs == 0, 0, jnp.where(row_docs == 1, begin_one, begin_two)).astype(jnp.int32)

    def bounds(rows):
        found = []
        for start in range(0, own, rows):
            found.append(lo[start] // KEY_ROWS)
            found.append((lo[start + rows - 1] + KEY_ROWS - 1) // KEY_ROWS)
        return jnp.stack([chip, core, line, *found]).astype(jnp.int32)

    meta = bounds(QUERY_ROWS)
    rotated, kv_own, heads_pre = heads_here(meta, gathered, head_full, cosine, sine, head_wide)
    tables = (heads_pre, cosine, sine, head_wide)
    mine = (kv_own, *gather_chips(kv_own))
    theirs = tuple(other_core(part) for part in mine)

    attended, lse = attend_here(bounds(FORWARD_ROWS), rotated, lo, mine, theirs)
    mixed_rows = arrival(attended.astype(narrow), core, line)
    attention_out = scatter_chip(transposed_product(mixed_rows, out_full).astype(narrow))

    down_low = forward_product(normed_low, laurel_full[:, :LAUREL_RANK]).astype(narrow)
    lifted = transposed_product(down_low, laurel_full[:, LAUREL_RANK:])
    merged, feed_in = combine(
        predicted[0], attention_out, normed_low.astype(wide), lifted, gain_rows
    )
    unit_rows = gather_chip(feed_in.astype(narrow))
    gate_low, up_low, hidden_low, *fed_parts = unit_here(unit_rows, unit_full)
    fed = scatter_chip(fed_parts)
    def core_columns(x):
        top, bottom = x[:rows_here], x[rows_here:]
        keep = jnp.where(first_core, top, bottom)
        got = other_core(jnp.where(first_core, bottom, top))
        return jnp.where(first_core, keep, got), jnp.where(first_core, got, keep)

    def pairs(x, count):
        first, second = core_columns(x)
        parts = []
        for index in range(count):
            columns = slice(index * HEAD_WIDTH, (index + 1) * HEAD_WIDTH)
            parts += [first[:, columns], second[:, columns]]
        return jnp.concatenate(parts, axis=1)

    (
        result,
        layer_grad,
        fed_grad,
        merged_grad,
        first_grad,
        packed_middle,
        first_low,
        gate_pre_low,
        projected_low,
        gated_low,
    ) = middle_here(
        merged, fed, predicted, cotangent, layer_input, gain_rows, router_wide, coef_wide, small_full
    )

    io_sum = lax.psum_scatter(
        jnp.concatenate(
            [weight_product(first_low, gate_pre_low), weight_product(projected_low, gated_low)],
            axis=1,
        ).astype(narrow),
        "blk",
        scatter_dimension=0,
        tiled=True,
    )
    fed_rows = gather_chip(fed_grad)
    fed_rows, io_sum = together(fed_rows, io_sum)
    io_share = share_line(io_sum).astype(narrow)
    gate_grad, up_grad, *feed_parts = unit_back_here(fed_rows, gate_low, up_low, unit_full)
    feed_grad = scatter_chip(feed_parts)
    down_sum = own_rows(weight_product(fed_rows, hidden_low).astype(narrow))
    two_sum = own_rows(
        weight_product(unit_rows, jnp.concatenate([gate_grad, up_grad], axis=1)).astype(narrow)
    )
    feed_grad, down_sum = together(feed_grad, down_sum)
    first_total, active_grad, attention_low, lifted_low, packed_combine = combine_back_here(
        merged, attention_out, lifted, merged_grad, feed_grad, first_grad, gain_rows, packed_middle
    )
    down_grad_low = forward_product(lifted_low, laurel_full[:, LAUREL_RANK:]).astype(narrow)
    laurel_part = jnp.concatenate(
        [weight_product(normed_low, down_grad_low), weight_product(lifted_low, down_low)], axis=1
    ).astype(narrow)
    laurel_part = laurel_part + other_core(laurel_part)
    attention_rows = gather_chip(attention_low)
    out_part = jnp.concatenate(
        [weight_product(attention_rows, mixed_rows).astype(narrow), laurel_part], axis=1
    )
    mixed_grad_rows = forward_product(attention_rows, out_full).astype(narrow)
    mixed_grad_rows, two_sum, io_share, out_part = together(
        mixed_grad_rows, two_sum, io_share, out_part
    )
    out_sum = own_rows(out_part)
    mixed_grad = natural(mixed_grad_rows, core, line)
    delta = jnp.sum(mixed_grad.astype(wide) * attended, axis=-1)
    query_rows_grad, query_gain_grad, kv_keep, kv_send = attend_back_here(
        meta, rotated, mixed_grad, lse, delta, lo, tables, mine, theirs
    )
    query_part = weight_product(normed_rows, query_rows_grad).astype(narrow)
    kv_got = other_core(kv_send)
    *kv_parts, out_sum, query_part = together(
        *[(kv_keep[m].astype(wide) + kv_got[m].astype(wide)).astype(narrow) for m in range(CHIPS)],
        out_sum,
        query_part,
    )
    laurel_here = jnp.where(
        first_core, out_sum[:rows_here, HEAD_WIDTH:], out_sum[rows_here:, HEAD_WIDTH:]
    )
    out_here = jnp.concatenate(
        [
            jnp.concatenate([pairs(out_sum, 1), laurel_here], axis=1),
            jnp.pad(io_share, ((0, 0), (0, 2 * LAUREL_RANK))),
        ],
        axis=0,
    )
    out_near = line_neighbours(out_here)
    out_far = line_far(out_here, *out_near)
    query_sum = own_rows(query_part)
    (kv_grad,) = scatter_chips(kv_parts)
    kv_grad, out_here, *out_others = together(kv_grad, out_here, *out_near, *out_far)

    kv_rows_grad, kv_gain_grad = kv_back_here(meta, kv_grad, tables)
    head_grads = jnp.concatenate([query_rows_grad, kv_rows_grad], axis=1)
    kv_part = weight_product(normed_rows, kv_rows_grad).astype(narrow)
    normed_part = transposed_product(head_grads, query_kv_full).astype(narrow)
    kv_weight_sum = own_rows(kv_part)
    normed_sum = scatter_chip(normed_part)
    normed_sum, query_sum, kv_weight_sum, down_sum, two_sum, out_here = together(
        normed_sum, query_sum, kv_weight_sum, down_sum, two_sum, out_here
    )
    query_here, kv_here = pairs(query_sum, 1), pairs(kv_weight_sum, 1)
    query_near, kv_near = line_neighbours(query_here), line_neighbours(kv_here)
    head_gain_grad = jnp.concatenate([query_gain_grad, kv_gain_grad], axis=0)
    packed_early = packed_combine + jnp.pad(
        head_gain_grad, ((12, 2), (128, width - 128 - HEAD_WIDTH))
    )
    version_grad, packed = predict_back_here(
        versions,
        first_total,
        cotangent,
        normed_sum,
        active_grad + transposed_product(down_grad_low, laurel_full[:, :LAUREL_RANK]),
        gain_rows,
        router_wide,
        coef_wide,
        packed_early,
    )
    packed, *query_near = together(packed, *query_near)
    packed = butterfly(packed)
    query_far, kv_far = line_far(query_here, *query_near), line_far(kv_here, *kv_near)
    down_first, down_second = core_columns(down_sum)
    two_first, two_second = core_columns(two_sum)

    def unit(index):
        columns = slice(index * hidden, (index + 1) * hidden)
        return jnp.concatenate([two_first[:, columns], two_second[:, columns]], axis=1).astype(wide)

    units = (unit(0), unit(1), jnp.concatenate([down_first, down_second], axis=1).astype(wide))
    packed, *far = together(packed, *query_far, *kv_far, *units)
    query_far, kv_far, units = far[:2], far[2:4], far[4:]
    query_all, out_all, key_all, value_all, laurel_all, io_all = assemble_here(
        meta,
        (query_here, *query_near, *query_far),
        (kv_here, *kv_near, *kv_far),
        (out_here, *out_others),
    )
    heads_from, heads_to = 128, 128 + HEAD_WIDTH

    return (
        result,
        version_grad,
        layer_grad,
        packed[:8],
        packed[8:12],
        packed[12:16, :20],
        packed[12:14, heads_from:heads_to],
        query_all,
        key_all,
        value_all,
        out_all,
        laurel_all,
        io_all[:, :LAYER_INPUT_SIZE],
        io_all[:, LAYER_INPUT_SIZE:],
        *units,
    )


def solution(mesh):
    by_chip = mesh.shape["heads"] == LINE and mesh.shape["blk"] == CORES * CHIPS
    on_device = chip_device if by_chip else general_device

    in_specs = (
        P(None, ("blk", "heads"), None),
        P(("blk", "heads"), None),
        P(("blk", "heads")),
        P(),
        P(None, ("blk", "heads"), None),
        P(),
        P(),
        P(),
        P(),
        P("blk", None),
        P("blk", None),
        P("blk", None),
        P("blk", None),
        P("blk", None),
        P("blk", None),
        P("blk", None),
        P("blk", "heads"),
        P("blk", "heads"),
        P("blk", "heads"),
    )
    out_specs = (
        P(None, ("blk", "heads"), None),
        P(None, ("blk", "heads"), None),
        P(("blk", "heads"), None),
        P(),
        P(),
        P(),
        P(),
        P("blk", None),
        P("blk", None),
        P("blk", None),
        P("blk", None),
        P("blk", None),
        P("blk", None),
        P("blk", None),
        P("blk", "heads"),
        P("blk", "heads"),
        P("blk", "heads"),
    )
    return jax.shard_map(
        on_device, mesh=mesh, in_specs=in_specs, out_specs=out_specs, check_vma=False
    )
```
